32 devices in a mesh: dp: 16 (over z, x, core), seq: 2 (over y).
Axes of the slice: x: 2, y: 2, z: 4, core: 2. Of those that a mesh axis runs over, the one named last changes fastest.
Arguments:
- layer_input: float32 [16384, 768], P(('dp', 'seq')), may hold values from -6 to 6
- cotangent: float32 [16384, 768], P(('dp', 'seq')), may hold values from -6 to 6
- seq_lengths: int32 [16], P('dp'), may hold values from 1024 to 1024, as said below
- qkv_weight: float32 [768, 2304], P(('dp', 'seq')), may hold values from -0.21875 to 0.21875
- qv_bias: float32 [1536], P(('dp', 'seq')), may hold values from -1.5 to 1.5
- out_weight: float32 [768, 768], P(('dp', 'seq')), may hold values from -1.25 to 1.25
- out_bias: float32 [768], P(('dp', 'seq')), may hold values from -1.5 to 1.5
- first_gain: float32 [768], P(('dp', 'seq')), may hold values from 0.25 to 1.75
- first_shift: float32 [768], P(('dp', 'seq')), may hold values from -1.5 to 1.5
- up_weight: float32 [768, 3072], P(('dp', 'seq')), may hold values from -0.21875 to 0.21875
- up_bias: float32 [3072], P(('dp', 'seq')), may hold values from -1.5 to 1.5
- down_weight: float32 [3072, 768], P(('dp', 'seq')), may hold values from -0.109375 to 0.109375
- down_bias: float32 [768], P(('dp', 'seq')), may hold values from -1.5 to 1.5
- second_gain: float32 [768], P(('dp', 'seq')), may hold values from 0.25 to 1.75
- second_shift: float32 [768], P(('dp', 'seq')), may hold values from -1.5 to 1.5
Outputs:
- layer_output: float32 [16384, 768], P(('dp', 'seq'))
- input_grad: float32 [16384, 768], P(('dp', 'seq'))
- qkvweight_grad: float32 [768, 2304], P(('dp', 'seq'))
- qvbias_grad: float32 [1536], P(('dp', 'seq'))
- outweight_grad: float32 [768, 768], P(('dp', 'seq'))
- outbias_grad: float32 [768], P(('dp', 'seq'))
- firstgain_grad: float32 [768], P(('dp', 'seq'))
- firstshift_grad: float32 [768], P(('dp', 'seq'))
- upweight_grad: float32 [768, 3072], P(('dp', 'seq'))
- upbias_grad: float32 [3072], P(('dp', 'seq'))
- downweight_grad: float32 [3072, 768], P(('dp', 'seq'))
- downbias_grad: float32 [768], P(('dp', 'seq'))
- secondgain_grad: float32 [768], P(('dp', 'seq'))
- secondshift_grad: float32 [768], P(('dp', 'seq'))
The draws below stay inside these ranges and needn't reach their ends.
Inputs may be any that keep to these rules, and one draw needn't show every extreme that they name: Each group holds one sequence at its positions 0 to seq_lengths - 1, reaching into every device of the group; the rest of its 1024 positions is padding. Some group is full.
All inputs are finite; a program needn't handle non-finite values.
Results may differ from the reference program's by a relative error of at most 0.0003.
Values sent between devices are 32-bit elements; how exact they have to be, the bound alone decides.
No kernel may reach another device: no remote copies, remote signals or barrier semaphores. Data moves between devices by JAX's collectives and lax.ppermute only.
A program may use at most 256 MiB of HBM per device.

```python
import jax
import jax.numpy as jnp
from jax import lax

D = 768
FF = 3072
HEADS = 12
HEAD_DIM = 64
TOK_DEV = 512
GROUP_TOK = 1024
LEAST = 1024
TOKENS = 16384
N_DP = 16
N_SEQ = 2


def draw_seq_lengths(key, part):
    key = jax.random.fold_in(key, 11)
    key_list = jax.random.split(key, 3)
    sequence_len = jax.random.randint(key_list[0], (N_DP,), LEAST, GROUP_TOK + 1, dtype=jnp.int32)
    longest_row = jax.random.randint(key_list[1], (), 0, N_DP, dtype=jnp.int32)
    offset_row = jax.random.randint(key_list[2], (), 1, N_DP, dtype=jnp.int32)
    shortest_row = (longest_row + offset_row) % N_DP
    row_index = jnp.arange(N_DP, dtype=jnp.int32)
    sequence_len = jnp.where(row_index == longest_row, GROUP_TOK, sequence_len)
    sequence_len = jnp.where(row_index == shortest_row, LEAST, sequence_len)
    return sequence_len


def with_spikes(values, own_key, source, target, blocks, factor):
    def block_of(dim):
        return (jnp.arange(values.shape[dim]) // (values.shape[dim] // blocks)).reshape((-1,) + (1,) * (values.ndim - 1 - dim))

    first = jax.random.permutation(own_key, blocks)[block_of(target)]
    other_side = (block_of(target) + blocks // 2) % blocks
    return jnp.where((block_of(source) == first) | (block_of(source) == other_side), factor * values, values)


def steps_of(rng, dims, cuts, low, top_value):
    level, own = 1.0, jax.random.fold_in(rng, 6)
    for axis_at, parts in cuts:
        steps = jnp.exp(jax.random.uniform(jax.random.fold_in(own, axis_at), (parts,), jnp.float32, low / len(cuts), top_value / len(cuts)))
        level = level * jnp.repeat(steps, dims[axis_at] // parts).reshape([-1 if axis == axis_at else 1 for axis in range(len(dims))])
    return level


def noise(rng, extent, spread, most, cuts=(), held_as=jnp.bfloat16):
    entries = jax.random.normal(rng, extent, jnp.float32) * spread
    if len(cuts) > 0:
        entries = steps_of(rng, extent, cuts, -0.22, 0.18) * entries
    return jnp.clip(entries, min=-most, max=most).astype(held_as)


def gaussian_with(rng, shape, scale, bound, cuts, heavy, kind=jnp.bfloat16):
    array = scale * jax.random.normal(rng, shape, jnp.float32)
    if cuts:
        array = array * steps_of(rng, shape, cuts, -0.22, 0.18)
    return jnp.clip(with_spikes(array, jax.random.fold_in(rng, 3), *heavy), -bound, bound).astype(kind)


def setup_inputs(seed: int = 0) -> dict:
    keys = jax.random.split(jax.random.key(seed), 16)
    layer_input = noise(keys[0], (TOKENS, D), 1.0, 6.0, ((0, 32),), jnp.float32)
    cotangent = gaussian_with(keys[1], (TOKENS, D), 1.0, 6.0, ((0, 32),), (0, 1, 32, 2.75), jnp.float32)
    seq_lengths = draw_seq_lengths(jax.random.fold_in(keys[15], 71), 0)
    qkv_weight = noise(keys[3], (D, 3 * D), D ** -0.5, 0.21875, ((0, 32),), jnp.float32)
    qv_bias = noise(keys[4], (2 * D,), 0.3, 1.5, ((0, 32),), jnp.float32)
    out_weight = noise(keys[5], (D, D), (D // 32) ** -0.5, 1.25, ((0, 32),), jnp.float32)
    out_bias = noise(keys[6], (D,), 0.3, 1.5, ((0, 32),), jnp.float32)
    first_gain = jnp.clip(1.0 + 0.15 * jax.random.normal(keys[7], (D,), jnp.float32), 0.25, 1.75)
    first_shift = noise(keys[8], (D,), 0.3, 1.5, ((0, 32),), jnp.float32)
    up_weight = noise(keys[9], (D, FF), D ** -0.5, 0.21875, ((0, 32),), jnp.float32)
    up_bias = noise(keys[10], (FF,), 0.3, 1.5, ((0, 32),), jnp.float32)
    down_weight = noise(keys[11], (FF, D), FF ** -0.5, 0.109375, ((0, 32),), jnp.float32)
    down_bias = noise(keys[12], (D,), 0.3, 1.5, ((0, 32),), jnp.float32)
    second_gain = jnp.clip(1.0 + 0.15 * jax.random.normal(keys[13], (D,), jnp.float32), 0.25, 1.75)
    second_shift = noise(keys[14], (D,), 0.3, 1.5, ((0, 32),), jnp.float32)
    return {"layer_input": layer_input, "cotangent": cotangent, "seq_lengths": seq_lengths, "qkv_weight": qkv_weight, "qv_bias": qv_bias, "out_weight": out_weight, "out_bias": out_bias, "first_gain": first_gain, "first_shift": first_shift, "up_weight": up_weight, "up_bias": up_bias, "down_weight": down_weight, "down_bias": down_bias, "second_gain": second_gain, "second_shift": second_shift}


eps_norm = 1e-05
neg_big = -1e+30
top_prec = lax.Precision.HIGHEST

@jax.custom_vjp
def low(v):
    return lax.optimization_barrier(v.astype(jnp.bfloat16)).astype(jnp.float32)

@jax.custom_vjp
def low_back(v):
    return v

def low_keep(v):
    return (low(v), None)

def low_pass(kept, grad):
    return (grad,)

def back_keep(v):
    return (v, None)

def back_low(kept, grad):
    return (low(grad),)
low.defvjp(low_keep, low_pass)
low_back.defvjp(back_keep, back_low)

def layer_norm(values, gain, shift):
    centred = values - lax.optimization_barrier(jnp.mean(values, axis=1, keepdims=True))
    inv_std = lax.rsqrt(lax.optimization_barrier(jnp.mean(centred * centred, axis=1, keepdims=True)) + eps_norm)
    return centred * inv_std * gain + shift

def attend_group(projected, seq_len):
    positions = jnp.arange(GROUP_TOK, dtype=jnp.int32)
    segment = jnp.where(positions < seq_len, 0, positions + 1)
    queries = projected[:, :D].reshape(GROUP_TOK, HEADS, HEAD_DIM)
    key_heads = projected[:, D:2 * D].reshape(GROUP_TOK, HEADS, HEAD_DIM)
    value_heads = projected[:, 2 * D:].reshape(GROUP_TOK, HEADS, HEAD_DIM)

    def block(first_row):
        q_block = lax.dynamic_slice_in_dim(queries, first_row.astype(jnp.int32), TOK_DEV, 0)
        q_pos = first_row.astype(jnp.int32) + jnp.arange(TOK_DEV, dtype=jnp.int32)
        q_seg = jnp.where(q_pos < seq_len, 0, q_pos + 1)
        allowed = (segment[None, :] == q_seg[:, None]) & (positions[None, :] <= q_pos[:, None])
        scores = jnp.einsum('qhd,khd->hqk', q_block, key_heads, precision=top_prec) * HEAD_DIM ** (-0.5)
        weights_soft = jax.nn.softmax(jnp.where(allowed[None], scores, neg_big), axis=-1)
        return jnp.einsum('hqk,khd->qhd', weights_soft, value_heads, precision=top_prec).reshape(TOK_DEV, D)
    starts = jnp.arange(N_SEQ, dtype=jnp.int32) * TOK_DEV
    return lax.map(jax.checkpoint(block), starts).reshape(GROUP_TOK, D)

def layer_forward(seq_lengths, layer_input, weight_tuple):
    qkv_weight, qv_bias, out_weight, out_bias, first_gain, first_shift, up_weight, up_bias, down_weight, down_bias, second_gain, second_shift = weight_tuple
    normed_one = layer_norm(layer_input, first_gain, first_shift)
    qkv_bias = jnp.concatenate([qv_bias[:D], jnp.zeros((D,), jnp.float32), qv_bias[D:]])
    projected = jnp.dot(normed_one, qkv_weight, precision=top_prec) + qkv_bias
    groups = projected.reshape(N_DP, GROUP_TOK, 3 * D)

    def one_group(group_item):
        return jax.checkpoint(attend_group)(group_item[0], group_item[1])
    attended = lax.map(one_group, (groups, seq_lengths)).reshape(TOKENS, D)
    middle = layer_input + jnp.dot(attended, out_weight, precision=top_prec) + out_bias
    normed_two = layer_norm(middle, second_gain, second_shift)
    activ = jax.nn.gelu(jnp.dot(normed_two, up_weight, precision=top_prec) + up_bias, approximate=False)
    return middle + jnp.dot(activ, down_weight, precision=top_prec) + down_bias

def reference(layer_input, cotangent, seq_lengths, qkv_weight, qv_bias, out_weight, out_bias, first_gain, first_shift, up_weight, up_bias, down_weight, down_bias, second_gain, second_shift):
    weight_tuple = (qkv_weight, qv_bias, out_weight, out_bias, first_gain, first_shift, up_weight, up_bias, down_weight, down_bias, second_gain, second_shift)

    def forward(inputs, weights_in):
        return layer_forward(seq_lengths, inputs, weights_in)
    layer_output, pullback = jax.vjp(forward, layer_input, weight_tuple)
    input_grad, grads = pullback(cotangent)
    return (layer_output, input_grad, grads[0], grads[1], grads[2], grads[3], grads[4], grads[5], grads[6], grads[7], grads[8], grads[9], grads[10], grads[11])
```

```python
import functools

import jax
import jax.numpy as jnp
from jax import lax
from jax.experimental import pallas as pl
from jax.experimental.pallas import tpu as pltpu
from jax.sharding import PartitionSpec as P

D = 768
HEADS = 12
HEAD_DIM = 64
PAIR = 2 * HEAD_DIM
TILE = 256
AXES = ("dp", "seq")

eps_norm = 1e-05
neg_big = -1e30
top_prec = lax.Precision.HIGH
f32 = jnp.float32
bf16 = jnp.bfloat16


def matmul(left, right):
    return jnp.dot(left, right, precision=top_prec, preferred_element_type=jnp.float32)


def matmul_tn(left, right):
    return lax.dot_general(
        left,
        right,
        (((0,), (0,)), ((), ())),
        precision=top_prec,
        preferred_element_type=jnp.float32,
    )


def matmul_nt(left, right):
    return lax.dot_general(
        left,
        right,
        (((1,), (1,)), ((), ())),
        precision=top_prec,
        preferred_element_type=jnp.float32,
    )


def norm_forward(values, gain, shift):
    centred = values - jnp.mean(values, axis=1, keepdims=True)
    inv_std = lax.rsqrt(jnp.mean(centred * centred, axis=1, keepdims=True) + eps_norm)
    normed = centred * inv_std
    return (normed * gain + shift, normed, inv_std)


def norm_backward(upstream, normed, inv_std, gain):
    scaled = upstream * gain
    inner = (
        scaled
        - jnp.mean(scaled, axis=1, keepdims=True)
        - normed * jnp.mean(scaled * normed, axis=1, keepdims=True)
    )
    return (inner * inv_std, jnp.sum(upstream * normed, axis=0), jnp.sum(upstream, axis=0))


def split_heads(values):
    return values.reshape(values.shape[0], HEADS, HEAD_DIM).transpose(1, 0, 2)


def join_heads(values):
    return values.transpose(1, 0, 2).reshape(values.shape[1], HEADS * HEAD_DIM)


def gelu_forward(values):
    return 0.5 * values * (1.0 + lax.erf(values * 0.7071067811865476))


def gelu_slope(values):
    cdf_part = 0.5 * (1.0 + lax.erf(values * 0.7071067811865476))
    return cdf_part + values * jnp.exp(-0.5 * values * values) * 0.3989422804014327


def body_general(
    layer_input,
    cotangent,
    seq_lengths,
    qkv_weight,
    qv_bias,
    out_weight,
    out_bias,
    first_gain,
    first_shift,
    up_weight,
    up_bias,
    down_weight,
    down_bias,
    second_gain,
    second_shift,
):
    gathered = (
        lax.all_gather(qkv_weight, ("dp", "seq"), axis=0, tiled=True),
        lax.all_gather(qv_bias, ("dp", "seq"), axis=0, tiled=True),
        lax.all_gather(out_weight, ("dp", "seq"), axis=0, tiled=True),
        lax.all_gather(out_bias, ("dp", "seq"), axis=0, tiled=True),
        lax.all_gather(first_gain, ("dp", "seq"), axis=0, tiled=True),
        lax.all_gather(first_shift, ("dp", "seq"), axis=0, tiled=True),
        lax.all_gather(up_weight, ("dp", "seq"), axis=0, tiled=True),
        lax.all_gather(up_bias, ("dp", "seq"), axis=0, tiled=True),
        lax.all_gather(down_weight, ("dp", "seq"), axis=0, tiled=True),
        lax.all_gather(down_bias, ("dp", "seq"), axis=0, tiled=True),
        lax.all_gather(second_gain, ("dp", "seq"), axis=0, tiled=True),
        lax.all_gather(second_shift, ("dp", "seq"), axis=0, tiled=True),
    )
    (
        w_qkv,
        b_qv,
        w_out,
        b_out,
        gain_one,
        shift_one,
        w_up,
        b_up,
        w_down,
        b_down,
        gain_two,
        shift_two,
    ) = gathered
    tok_rows = layer_input.shape[0]
    group_rows = tok_rows * lax.axis_size("seq")
    score_scale = HEAD_DIM ** (-0.5)
    seq_len = seq_lengths[0]
    first_own = lax.axis_index("seq") * tok_rows
    query_pos = first_own + jnp.arange(tok_rows, dtype=jnp.int32)
    last_query = first_own + tok_rows - 1

    def segment_of(positions):
        return jnp.where(positions < seq_len, 0, positions + 1)

    query_seg = segment_of(query_pos)

    def key_mask(key_pos):
        return (segment_of(key_pos)[None, :] == query_seg[:, None]) & (
            key_pos[None, :] <= query_pos[:, None]
        )

    normed_out_one, normed_one, inv_one = norm_forward(layer_input, gain_one, shift_one)
    qkv_bias = jnp.concatenate([b_qv[:D], jnp.zeros((D,), jnp.float32), b_qv[D:]])
    projected = matmul(normed_out_one, w_qkv) + qkv_bias
    queries = projected[:, :D]
    keys_local = projected[:, D : 2 * D]
    values_local = projected[:, 2 * D :]
    query_heads = split_heads(queries)
    start_state = (
        jnp.full((HEADS, tok_rows), neg_big, jnp.float32),
        jnp.zeros((HEADS, tok_rows), jnp.float32),
        jnp.zeros((HEADS, tok_rows, HEAD_DIM), jnp.float32),
    )
    key_piece = lax.all_gather(keys_local, "seq", axis=0, tiled=True)
    value_piece = lax.all_gather(values_local, "seq", axis=0, tiled=True)

    def compute_block(state_in):
        key_pos = jnp.arange(key_piece.shape[0], dtype=jnp.int32)
        allowed = key_mask(key_pos)
        key_heads = split_heads(key_piece)
        value_heads = split_heads(value_piece)

        def one_head(ignored, head_item):
            q_head, k_head, v_head, old_max, old_sum, old_acc = head_item
            scores = jnp.where(allowed, matmul_nt(q_head, k_head) * score_scale, neg_big)
            new_max = jnp.maximum(old_max, jnp.max(scores, axis=1))
            weights_soft = jnp.where(allowed, jnp.exp(scores - new_max[:, None]), 0.0)
            decay_old = jnp.exp(old_max - new_max)
            new_sum = old_sum * decay_old + jnp.sum(weights_soft, axis=1)
            new_acc = old_acc * decay_old[:, None] + matmul(weights_soft, v_head)
            return (ignored, (new_max, new_sum, new_acc))

        unused, updated = lax.scan(
            one_head,
            jnp.zeros((), jnp.float32),
            (query_heads, key_heads, value_heads, state_in[0], state_in[1], state_in[2]),
        )
        return updated

    def keep_block(state_in):
        return (state_in[0], state_in[1], state_in[2])

    run_max, run_sum, run_acc = lax.cond(
        jnp.int32(0) > last_query, keep_block, compute_block, start_state
    )
    head_out = run_acc / run_sum[:, :, None]
    log_sum = run_max + jnp.log(run_sum)
    attended = join_heads(head_out)
    middle = layer_input + matmul(attended, w_out) + b_out
    normed_out_two, normed_two, inv_two = norm_forward(middle, gain_two, shift_two)
    pre_act = matmul(normed_out_two, w_up) + b_up
    activ = gelu_forward(pre_act)
    layer_output = middle + matmul(activ, w_down) + b_down
    d_down_b = jnp.sum(cotangent, axis=0)
    d_down_w = matmul_tn(activ, cotangent)
    d_pre = matmul_nt(cotangent, w_down) * gelu_slope(pre_act)
    d_up_b = jnp.sum(d_pre, axis=0)
    d_up_w = matmul_tn(normed_out_two, d_pre)
    d_norm_two, d_gain_two, d_shift_two = norm_backward(
        matmul_nt(d_pre, w_up), normed_two, inv_two, gain_two
    )
    d_middle = cotangent + d_norm_two
    d_out_b = jnp.sum(d_middle, axis=0)
    d_out_w = matmul_tn(attended, d_middle)
    d_att = matmul_nt(d_middle, w_out)
    dout_heads = split_heads(d_att)
    delta_heads = jnp.sum(dout_heads * head_out, axis=2)
    key_all, value_all = (
        lax.all_gather(keys_local, "seq", axis=0, tiled=True),
        lax.all_gather(values_local, "seq", axis=0, tiled=True),
    )
    allowed_all = key_mask(jnp.arange(group_rows, dtype=jnp.int32))

    def back_head(ignored, head_item):
        q_head, k_head, v_head, do_head, lse_head, delta_head = head_item
        scores = jnp.where(allowed_all, matmul_nt(q_head, k_head) * score_scale, neg_big)
        weights_soft = jnp.where(allowed_all, jnp.exp(scores - lse_head[:, None]), 0.0)
        dv_head = matmul_tn(weights_soft, do_head)
        d_soft = matmul_nt(do_head, v_head)
        d_scores = weights_soft * (d_soft - delta_head[:, None]) * score_scale
        return (ignored, (matmul(d_scores, k_head), matmul_tn(d_scores, q_head), dv_head))

    unused, head_grads = lax.scan(
        back_head,
        jnp.zeros((), jnp.float32),
        (
            query_heads,
            split_heads(key_all),
            split_heads(value_all),
            dout_heads,
            log_sum,
            delta_heads,
        ),
    )
    d_query = join_heads(head_grads[0])
    key_terms = join_heads(head_grads[1])
    value_terms = join_heads(head_grads[2])
    d_key, d_value = (
        lax.psum_scatter(key_terms, "seq", scatter_dimension=0, tiled=True),
        lax.psum_scatter(value_terms, "seq", scatter_dimension=0, tiled=True),
    )
    d_proj = jnp.concatenate([d_query, d_key, d_value], axis=1)
    d_qv_b = jnp.concatenate([jnp.sum(d_query, axis=0), jnp.sum(d_value, axis=0)])
    d_qkv_w = matmul_tn(normed_out_one, d_proj)
    d_norm_one, d_gain_one, d_shift_one = norm_backward(
        matmul_nt(d_proj, w_qkv), normed_one, inv_one, gain_one
    )
    input_grad = d_middle + d_norm_one
    summed = (
        lax.psum_scatter(d_qkv_w, ("dp", "seq"), scatter_dimension=0, tiled=True),
        lax.psum_scatter(d_qv_b, ("dp", "seq"), scatter_dimension=0, tiled=True),
        lax.psum_scatter(d_out_w, ("dp", "seq"), scatter_dimension=0, tiled=True),
        lax.psum_scatter(d_out_b, ("dp", "seq"), scatter_dimension=0, tiled=True),
        lax.psum_scatter(d_gain_one, ("dp", "seq"), scatter_dimension=0, tiled=True),
        lax.psum_scatter(d_shift_one, ("dp", "seq"), scatter_dimension=0, tiled=True),
        lax.psum_scatter(d_up_w, ("dp", "seq"), scatter_dimension=0, tiled=True),
        lax.psum_scatter(d_up_b, ("dp", "seq"), scatter_dimension=0, tiled=True),
        lax.psum_scatter(d_down_w, ("dp", "seq"), scatter_dimension=0, tiled=True),
        lax.psum_scatter(d_down_b, ("dp", "seq"), scatter_dimension=0, tiled=True),
        lax.psum_scatter(d_gain_two, ("dp", "seq"), scatter_dimension=0, tiled=True),
        lax.psum_scatter(d_shift_two, ("dp", "seq"), scatter_dimension=0, tiled=True),
    )
    return (
        layer_output,
        input_grad,
        summed[0],
        summed[1],
        summed[2],
        summed[3],
        summed[4],
        summed[5],
        summed[6],
        summed[7],
        summed[8],
        summed[9],
        summed[10],
        summed[11],
    )


def split(v):
    high=v.astype(bf16)
    return high,(v-high.astype(f32)).astype(bf16)

def dot_nn(a,b):
    return lax.dot_general(a,b,(((1,),(0,)),((),())),preferred_element_type=f32)
def dot_nt(a,b):
    return lax.dot_general(a,b,(((1,),(1,)),((),())),preferred_element_type=f32)
def dot_tn(a,b):
    return lax.dot_general(a,b,(((0,),(0,)),((),())),preferred_element_type=f32)

def fold(v):
    return v[:,:PAIR]+v[:,PAIR:]

def attend_kernel(len_ref,qkv_ref,out_ref,lse_ref):
    rows=qkv_ref.shape[0]
    seq_len=len_ref[0]
    lane=lax.broadcasted_iota(jnp.int32,(1,PAIR),1)
    q_high,q_low=split(qkv_ref[:,:PAIR]*(HEAD_DIM**-0.5))
    q_both=jnp.concatenate([q_high,q_low],axis=1)
    v_high,v_low=split(qkv_ref[:,2*PAIR:])
    v_both=jnp.concatenate([v_high,v_low],axis=1)
    k_all=qkv_ref[:,PAIR:2*PAIR]
    k_parts=[]
    for head in range(2):
        kh,kl=split(jnp.where(lane//HEAD_DIM==head,k_all,0.0))
        k_parts.append((jnp.concatenate([kh,kh],axis=1),kl))
    for start in range(0,rows,TILE):
        stop=start+TILE
        q_pos=start+lax.broadcasted_iota(jnp.int32,(TILE,1),0)
        first=jnp.where(q_pos<seq_len,0,q_pos)
        k_pos=lax.broadcasted_iota(jnp.int32,(1,stop),1)
        allowed=(k_pos>=first)&(k_pos<=q_pos)
        outs,lses=[],[]
        for head in range(2):
            kd,kl=k_parts[head]
            scores=dot_nt(q_both[start:stop],kd[:stop])+dot_nt(q_high[start:stop],kl[:stop])
            scores=jnp.where(allowed,scores,neg_big)
            top=jnp.max(scores,axis=1,keepdims=True)
            probs=jnp.exp(scores-top)
            total=jnp.sum(probs,axis=1,keepdims=True)
            ph,pw=split(probs)
            acc=fold(dot_nn(ph,v_both[:stop]))+dot_nn(pw,v_high[:stop])
            outs.append(acc*(1.0/total))
            lses.append(jnp.broadcast_to(top+jnp.log(total),(TILE,PAIR)))
        out_ref[start:stop]=jnp.where(lane<HEAD_DIM,outs[0],outs[1])
        lse_ref[start:stop]=jnp.where(lane<HEAD_DIM,lses[0],lses[1])

def attend_back_kernel(len_ref,qkv_ref,do_ref,out_ref,lse_ref,grad_ref):
    rows=qkv_ref.shape[0]
    seq_len=len_ref[0]
    lane=lax.broadcasted_iota(jnp.int32,(1,PAIR),1)
    scale=HEAD_DIM**-0.5
    q_high,q_low=split(qkv_ref[:,:PAIR]*scale)
    q_both=jnp.concatenate([q_high,q_low],axis=1)
    q_twice=jnp.concatenate([q_high,q_high],axis=1)
    do_all=do_ref[...]
    do_high,do_low=split(do_all)
    do_both=jnp.concatenate([do_high,do_low],axis=1)
    do_twice=jnp.concatenate([do_high,do_high],axis=1)
    delta_t=jnp.transpose(do_all*out_ref[...])
    lse_t=jnp.transpose(lse_ref[...])
    q_sum=[None,None]
    dq=[[jnp.zeros((TILE,PAIR),f32) for _ in range(rows//TILE)] for _ in range(2)]
    for start in range(0,rows,TILE):
        stop=start+TILE
        n=rows-start
        k_pos=start+lax.broadcasted_iota(jnp.int32,(TILE,1),0)
        q_pos=start+lax.broadcasted_iota(jnp.int32,(1,n),1)
        first=jnp.where(q_pos<seq_len,0,q_pos)
        allowed=(k_pos>=first)&(k_pos<=q_pos)
        k_all=qkv_ref[start:stop,PAIR:2*PAIR]
        v_all=qkv_ref[start:stop,2*PAIR:]
        k_grads,v_grads=[],[]
        for head in range(2):
            mine=lane//HEAD_DIM==head
            kh,kl=split(jnp.where(mine,k_all,0.0))
            vh,vl=split(jnp.where(mine,v_all,0.0))
            k_both=jnp.concatenate([kh,kl],axis=1)
            v_both=jnp.concatenate([vh,vl],axis=1)
            scores=dot_nt(k_both,q_twice[start:])+dot_nt(kh,q_low[start:])
            lse_row=lse_t[head*HEAD_DIM:head*HEAD_DIM+1,start:]
            probs=jnp.where(allowed,jnp.exp(scores-lse_row),0.0)
            ph,pw=split(probs)
            v_grads.append(fold(dot_nn(ph,do_both[start:]))+dot_nn(pw,do_high[start:]))
            d_probs=dot_nt(v_both,do_twice[start:])+dot_nt(vh,do_low[start:])
            delta_row=jnp.sum(delta_t[head*HEAD_DIM:(head+1)*HEAD_DIM,start:],axis=0,keepdims=True)
            d_scores=probs*(d_probs-delta_row)
            sh,sl=split(d_scores)
            k_grads.append(fold(dot_nn(sh,q_both[start:]))+dot_nn(sl,q_high[start:]))
            part=fold(dot_tn(sh,k_both))+dot_tn(sl,kh)
            for t in range(n//TILE):
                dq[head][start//TILE+t]+=part[t*TILE:(t+1)*TILE]
        grad_ref[start:stop,PAIR:2*PAIR]=jnp.where(lane<HEAD_DIM,k_grads[0],k_grads[1])
        grad_ref[start:stop,2*PAIR:]=jnp.where(lane<HEAD_DIM,v_grads[0],v_grads[1])
        grad_ref[start:stop,:PAIR]=(dq[0][start//TILE]+dq[1][start//TILE])*scale

def attend(seq_len,qkv):
    rows,cols=qkv.shape
    pairs=cols//(3*PAIR)
    block=lambda w: pl.BlockSpec((rows,w),lambda j:(0,j))
    return pl.pallas_call(
        attend_kernel,
        grid=(pairs,),
        in_specs=[pl.BlockSpec(memory_space=pltpu.SMEM),block(3*PAIR)],
        out_specs=[block(PAIR),block(PAIR)],
        out_shape=[jax.ShapeDtypeStruct((rows,pairs*PAIR),f32)]*2,
        compiler_params=pltpu.CompilerParams(vmem_limit_bytes=48*2**20),
        cost_estimate=pl.CostEstimate(flops=40*10**9//3,bytes_accessed=4*rows*pairs*PAIR*5,transcendentals=rows*rows*pairs),
        name="attend",
    )(seq_len,qkv)

def attend_back(seq_len,qkv,d_out,out,lse):
    rows,cols=qkv.shape
    pairs=cols//(3*PAIR)
    block=lambda w: pl.BlockSpec((rows,w),lambda j:(0,j))
    return pl.pallas_call(
        attend_back_kernel,
        grid=(pairs,),
        in_specs=[pl.BlockSpec(memory_space=pltpu.SMEM),block(3*PAIR),block(PAIR),block(PAIR),block(PAIR)],
        out_specs=block(3*PAIR),
        out_shape=jax.ShapeDtypeStruct((rows,cols),f32),
        compiler_params=pltpu.CompilerParams(vmem_limit_bytes=48*2**20),
        cost_estimate=pl.CostEstimate(flops=40*10**9,bytes_accessed=4*rows*pairs*PAIR*9,transcendentals=rows*rows*pairs),
        name="attend_back",
    )(seq_len,qkv,d_out,out,lse)


COLUMNS = 4


def table(move):
    pairs = []
    for z in range(COLUMNS):
        for x in range(2):
            for core in range(2):
                for y in range(2):
                    there = move(z, x, core, y)
                    number = lambda p: ((p[0] * 2 + p[1]) * 2 + p[2]) * 2 + p[3]
                    pairs.append((number((z, x, core, y)), number(there)))
    return pairs


over_core = table(lambda z, x, core, y: (z, x, 1 - core, y))
over_x = table(lambda z, x, core, y: (z, 1 - x, core, y))
over_y = table(lambda z, x, core, y: (z, x, core, 1 - y))
over_z = [None] + [
    table(lambda z, x, core, y, k=k: (z ^ k, x, core, y)) for k in range(1, COLUMNS)
]


def swap(values, pairs):
    return lax.ppermute(values, AXES, pairs)


def place():
    dp = lax.axis_index("dp")
    return dp // 4, (dp // 2) % 2, dp % 2, lax.axis_index("seq")


def pick(values, index, axis):
    return lax.dynamic_index_in_dim(values, index, axis, keepdims=False)


def assemble_kernel(count, place_ref, *refs):
    pieces, out_ref, sems = refs[:count], refs[count], refs[count + 1]
    z, x, core, y = (place_ref[i] for i in range(4))
    copies = []
    for c in range(2):
        own, beside_x, beside_y, corner_a, corner_b = pieces[c * 5 : c * 5 + 5]
        sources = [(own, 0, 0, 0, 4), (beside_x, 1, 0, 0, 4), (beside_y, 0, 1, 0, 4)]
        sources += [(corner_a, 1, 1, 0, 2), (corner_b, 1, 1, 2, 4)]
        for piece, dx, dy, first, last in sources:
            for k in range(first, last):
                slot = out_ref.at[z ^ k, x ^ dx, core ^ c, y ^ dy]
                copies.append(
                    pltpu.make_async_copy(piece.at[k - first], slot, sems.at[len(copies)])
                )
    for copy in copies:
        copy.start()
    for copy in copies:
        copy.wait()


def assemble(where, pieces, rows, cols):
    anywhere = pl.BlockSpec(memory_space=pl.ANY)
    return pl.pallas_call(
        functools.partial(assemble_kernel, len(pieces)),
        in_specs=[pl.BlockSpec(memory_space=pltpu.SMEM)] + [anywhere] * len(pieces),
        out_specs=anywhere,
        out_shape=jax.ShapeDtypeStruct((COLUMNS, 2, 2, 2, rows, cols), f32),
        scratch_shapes=[pltpu.SemaphoreType.DMA((32,))],
        cost_estimate=pl.CostEstimate(
            flops=0, bytes_accessed=2 * 32 * rows * cols * 4, transcendentals=0
        ),
        name="assemble",
    )(where, *pieces)


def gather_weight(where, shard):
    rows, cols = shard.shape
    own = jnp.stack([shard] + [swap(shard, over_z[k]) for k in range(1, COLUMNS)])
    beside_x = swap(own, over_x)
    beside_y = swap(own, over_y)
    corner_a = swap(beside_y[:2], over_x)
    corner_b = swap(beside_x[2:], over_y)
    mine = [own, beside_x, beside_y, corner_a, corner_b]
    other = [swap(piece, over_core) for piece in mine]
    return assemble(where, mine + other, rows, cols).reshape(32 * rows, cols)


def scatter_grad(grad, z, x, core, y):
    rows, cols = grad.shape[0] // 32, grad.shape[1]
    grid = grad.reshape(COLUMNS, 2, 2, 2, rows, cols)
    arrived = swap(pick(grid, 1 - core, 2), over_core)
    chip = pick(grid, core, 2) + arrived
    low, high = chip[:2], chip[2:]
    from_x = swap(pick(low, 1 - x, 1), over_x)
    from_y = swap(pick(high, 1 - y, 2), over_y)
    low = pick(low, x, 1) + from_x
    high = pick(high, y, 2) + from_y
    from_y = swap(pick(low, 1 - y, 1), over_y)
    from_x = swap(pick(high, 1 - x, 1), over_x)
    low = pick(low, y, 1) + from_y
    high = pick(high, x, 1) + from_x
    return sum_column(jnp.concatenate([low, high]), z)


def sum_column(column, z):
    total = pick(column, z, 0)
    for k in range(1, COLUMNS):
        total = total + swap(pick(column, z ^ k, 0), over_z[k])
    return total


def body_grid(
    layer_input,
    cotangent,
    seq_lengths,
    qkv_weight,
    qv_bias,
    out_weight,
    out_bias,
    first_gain,
    first_shift,
    up_weight,
    up_bias,
    down_weight,
    down_bias,
    second_gain,
    second_shift,
):
    z, x, core, y = place()
    where = jnp.stack([z, x, core, y]).astype(jnp.int32)
    rows = layer_input.shape[0]
    shard = qkv_weight.shape[0]
    half = D // 2
    pairs = half // PAIR
    wide = 3 * half

    def both_rows(own, other):
        return jnp.where(
            y == 0, jnp.concatenate([own, other]), jnp.concatenate([other, own])
        )

    def rows_of(values, part):
        return lax.dynamic_slice_in_dim(values, part * rows, rows, 0)

    other_input = swap(layer_input, over_y)

    by_head = qkv_weight.reshape(shard, 3, 2, pairs, PAIR).transpose(2, 0, 3, 1, 4)
    by_head = by_head.reshape(2, shard, wide)
    line_one = jnp.concatenate([qv_bias, out_bias, first_gain, first_shift])
    line_two = jnp.concatenate([up_bias, down_bias])
    line_three = jnp.concatenate([second_gain, second_shift])
    lines = jnp.stack(
        [jnp.pad(line, (0, PAIR - line.shape[0])) for line in (line_one, line_two, line_three)]
    )
    small = jnp.pad(lines, ((0, shard - 3), (0, 0)))
    sent = swap(jnp.concatenate([pick(by_head, 1 - y, 0), small], axis=1), over_y)
    kept = jnp.concatenate([pick(by_head, y, 0), small], axis=1)
    block = jnp.where(y == 0, jnp.stack([kept, sent]), jnp.stack([sent, kept]))
    column = [block] + [swap(block, over_z[k]) for k in range(1, COLUMNS)]
    column = jnp.stack(column)
    column = jnp.stack([pick(column, z ^ k, 0) for k in range(COLUMNS)])
    beside = swap(column, over_x)
    plane = jnp.where(x == 0, jnp.stack([column, beside], 1), jnp.stack([beside, column], 1))
    beside = swap(plane, over_core)
    whole = jnp.where(core == 0, jnp.stack([plane, beside], 2), jnp.stack([beside, plane], 2))
    whole = whole.reshape(32, shard, wide + PAIR)
    w_qkv = whole[:, :, :wide].reshape(D, wide)
    lines = whole[:, :3, wide:]
    b_qv = lines[:, 0, : 2 * shard].reshape(2 * D)
    b_out = lines[:, 0, 2 * shard : 3 * shard].reshape(D)
    gain_one = lines[:, 0, 3 * shard : 4 * shard].reshape(D)
    shift_one = lines[:, 0, 4 * shard : 5 * shard].reshape(D)
    b_up = lines[:, 1, : 4 * shard].reshape(4 * D)
    b_down = lines[:, 1, 4 * shard : 5 * shard].reshape(D)
    gain_two = lines[:, 2, :shard].reshape(D)
    shift_two = lines[:, 2, shard : 2 * shard].reshape(D)

    w_out = gather_weight(where, out_weight)
    w_up = gather_weight(where, up_weight)
    w_down = gather_weight(where, down_weight)

    inputs = both_rows(layer_input, other_input)
    normed_out_one, normed_one, inv_one = norm_forward(inputs, gain_one, shift_one)
    bias = pick(b_qv.reshape(2, 2, pairs, PAIR), y, 1)
    qkv_bias = jnp.stack([bias[0], jnp.zeros_like(bias[0]), bias[1]], axis=1).reshape(wide)
    projected = matmul(normed_out_one, w_qkv) + qkv_bias
    head_out, log_sum = attend(seq_lengths, projected)
    there = swap(rows_of(head_out, 1 - y), over_y)
    here = rows_of(head_out, y)
    attended = jnp.where(
        y == 0, jnp.concatenate([here, there], 1), jnp.concatenate([there, here], 1)
    )
    middle = layer_input + matmul(attended, w_out) + b_out
    normed_out_two, normed_two, inv_two = norm_forward(middle, gain_two, shift_two)
    pre_act = matmul(normed_out_two, w_up) + b_up
    activ = gelu_forward(pre_act)
    layer_output = middle + matmul(activ, w_down) + b_down

    d_down_b = jnp.sum(cotangent, axis=0)
    d_pre = matmul_nt(cotangent, w_down) * gelu_slope(pre_act)
    d_norm_two, d_gain_two, d_shift_two = norm_backward(
        matmul_nt(d_pre, w_up), normed_two, inv_two, gain_two
    )
    d_middle = cotangent + d_norm_two
    d_att = matmul_nt(d_middle, w_out)
    d_heads = d_att.reshape(rows, 2, half)
    there = swap(pick(d_heads, 1 - y, 1), over_y)
    d_out = both_rows(pick(d_heads, y, 1), there)
    d_down_w = matmul_tn(activ, cotangent)
    down_grad = scatter_grad(d_down_w, z, x, core, y)
    d_up_b = jnp.sum(d_pre, axis=0)
    d_up_w = matmul_tn(normed_out_two, d_pre)
    up_grad = scatter_grad(d_up_w, z, x, core, y)
    d_out_b = jnp.sum(d_middle, axis=0)
    d_out_w = matmul_tn(attended, d_middle)
    out_grad = scatter_grad(d_out_w, z, x, core, y)

    d_proj = attend_back(seq_lengths, projected, d_out, head_out, log_sum)
    d_qkv_w = matmul_tn(normed_out_one, d_proj)
    d_norm = matmul_nt(d_proj, w_qkv)
    d_gain_one = jnp.sum(d_norm * normed_one, axis=0)
    d_shift_one = jnp.sum(d_norm, axis=0)
    d_norm_own = rows_of(d_norm, y) + swap(rows_of(d_norm, 1 - y), over_y)
    d_norm_one, unused, unused = norm_backward(
        d_norm_own, rows_of(normed_one, y), rows_of(inv_one, y), gain_one
    )
    input_grad = d_middle + d_norm_one

    d_bias = jnp.sum(d_proj, axis=0).reshape(pairs, 3, PAIR)
    d_bias = jnp.stack([d_bias[:, 0], d_bias[:, 2]]).reshape(2, 1, half)
    blank = jnp.zeros_like(d_bias)
    d_qv_b = jnp.where(
        y == 0, jnp.concatenate([d_bias, blank], 1), jnp.concatenate([blank, d_bias], 1)
    )

    def lanes(*vectors):
        line = jnp.concatenate([v.reshape(32, -1) for v in vectors], axis=1)
        return jnp.pad(line, ((0, 0), (0, PAIR - line.shape[1])))

    lines = jnp.stack(
        [
            lanes(d_qv_b, d_out_b, d_gain_one, d_shift_one),
            lanes(d_up_b, d_down_b),
            lanes(d_gain_two, d_shift_two),
        ],
        axis=1,
    )
    small = jnp.pad(lines, ((0, 0), (0, shard - 3), (0, 0)))
    grid = jnp.concatenate([d_qkv_w.reshape(32, shard, wide), small], axis=2)
    grid = grid.reshape(COLUMNS, 2, 2, 2, shard, wide + PAIR)
    grid = pick(grid, core, 2) + swap(pick(grid, 1 - core, 2), over_core)
    grid = pick(grid, x, 1) + swap(pick(grid, 1 - x, 1), over_x)
    grid = sum_column(grid, z)
    here = pick(grid, y, 0)
    there = swap(pick(grid, 1 - y, 0), over_y)
    lines = here[:, wide:] + there[:, wide:]
    here, there = here[:, :wide], there[:, :wide]
    qkv_grad = jnp.where(y == 0, jnp.stack([here, there]), jnp.stack([there, here]))
    qkv_grad = qkv_grad.reshape(2, shard, pairs, 3, PAIR).transpose(1, 3, 0, 2, 4)
    return (
        layer_output,
        input_grad,
        qkv_grad.reshape(shard, 3 * D),
        lines[0, : 2 * shard],
        out_grad,
        lines[0, 2 * shard : 3 * shard],
        lines[0, 3 * shard : 4 * shard],
        lines[0, 4 * shard : 5 * shard],
        up_grad,
        lines[1, : 4 * shard],
        down_grad,
        lines[1, 4 * shard : 5 * shard],
        lines[2, :shard],
        lines[2, shard : 2 * shard],
    )


def solution(mesh):
    shape = (mesh.shape["dp"], mesh.shape["seq"])
    body = body_grid if shape == (COLUMNS * 4, 2) else body_general
    row = P(AXES, None)
    vec = P(AXES)
    return jax.shard_map(
        body,
        mesh=mesh,
        in_specs=(row, row, P("dp"), row, vec, row, vec, vec, vec, row, vec, row, vec, vec, vec),
        out_specs=(row, row, row, vec, row, vec, vec, vec, row, vec, row, vec, vec, vec),
        check_vma=False,
    )
```

```python
import functools

import jax
import jax.numpy as jnp
from jax import lax
from jax.experimental import pallas as pl
from jax.experimental.pallas import tpu as pltpu
from jax.sharding import PartitionSpec as P

D = 768
HEADS = 12
HEAD_DIM = 64
PAIR = 2 * HEAD_DIM
TILE = 256
AXES = ("dp", "seq")

eps_norm = 1e-05
neg_big = -1e30
top_prec = lax.Precision.HIGH
f32 = jnp.float32
bf16 = jnp.bfloat16


def matmul(left, right):
    return jnp.dot(left, right, precision=top_prec, preferred_element_type=jnp.float32)


def matmul_tn(left, right):
    return lax.dot_general(
        left,
        right,
        (((0,), (0,)), ((), ())),
        precision=top_prec,
        preferred_element_type=jnp.float32,
    )


def matmul_nt(left, right):
    return lax.dot_general(
        left,
        right,
        (((1,), (1,)), ((), ())),
        precision=top_prec,
        preferred_element_type=jnp.float32,
    )


def norm_forward(values, gain, shift):
    centred = values - jnp.mean(values, axis=1, keepdims=True)
    inv_std = lax.rsqrt(jnp.mean(centred * centred, axis=1, keepdims=True) + eps_norm)
    normed = centred * inv_std
    return (normed * gain + shift, normed, inv_std)


def norm_backward(upstream, normed, inv_std, gain):
    scaled = upstream * gain
    inner = (
        scaled
        - jnp.mean(scaled, axis=1, keepdims=True)
        - normed * jnp.mean(scaled * normed, axis=1, keepdims=True)
    )
    return (inner * inv_std, jnp.sum(upstream * normed, axis=0), jnp.sum(upstream, axis=0))


def split_heads(values):
    return values.reshape(values.shape[0], HEADS, HEAD_DIM).transpose(1, 0, 2)


def join_heads(values):
    return values.transpose(1, 0, 2).reshape(values.shape[1], HEADS * HEAD_DIM)


def gelu_forward(values):
    return 0.5 * values * (1.0 + lax.erf(values * 0.7071067811865476))


def gelu_slope(values):
    cdf_part = 0.5 * (1.0 + lax.erf(values * 0.7071067811865476))
    return cdf_part + values * jnp.exp(-0.5 * values * values) * 0.3989422804014327


def body_general(
    layer_input,
    cotangent,
    seq_lengths,
    qkv_weight,
    qv_bias,
    out_weight,
    out_bias,
    first_gain,
    first_shift,
    up_weight,
    up_bias,
    down_weight,
    down_bias,
    second_gain,
    second_shift,
):
    gathered = (
        lax.all_gather(qkv_weight, ("dp", "seq"), axis=0, tiled=True),
        lax.all_gather(qv_bias, ("dp", "seq"), axis=0, tiled=True),
        lax.all_gather(out_weight, ("dp", "seq"), axis=0, tiled=True),
        lax.all_gather(out_bias, ("dp", "seq"), axis=0, tiled=True),
        lax.all_gather(first_gain, ("dp", "seq"), axis=0, tiled=True),
        lax.all_gather(first_shift, ("dp", "seq"), axis=0, tiled=True),
        lax.all_gather(up_weight, ("dp", "seq"), axis=0, tiled=True),
        lax.all_gather(up_bias, ("dp", "seq"), axis=0, tiled=True),
        lax.all_gather(down_weight, ("dp", "seq"), axis=0, tiled=True),
        lax.all_gather(down_bias, ("dp", "seq"), axis=0, tiled=True),
        lax.all_gather(second_gain, ("dp", "seq"), axis=0, tiled=True),
        lax.all_gather(second_shift, ("dp", "seq"), axis=0, tiled=True),
    )
    (
        w_qkv,
        b_qv,
        w_out,
        b_out,
        gain_one,
        shift_one,
        w_up,
        b_up,
        w_down,
        b_down,
        gain_two,
        shift_two,
    ) = gathered
    tok_rows = layer_input.shape[0]
    group_rows = tok_rows * lax.axis_size("seq")
    score_scale = HEAD_DIM ** (-0.5)
    seq_len = seq_lengths[0]
    first_own = lax.axis_index("seq") * tok_rows
    query_pos = first_own + jnp.arange(tok_rows, dtype=jnp.int32)
    last_query = first_own + tok_rows - 1

    def segment_of(positions):
        return jnp.where(positions < seq_len, 0, positions + 1)

    query_seg = segment_of(query_pos)

    def key_mask(key_pos):
        return (segment_of(key_pos)[None, :] == query_seg[:, None]) & (
            key_pos[None, :] <= query_pos[:, None]
        )

    normed_out_one, normed_one, inv_one = norm_forward(layer_input, gain_one, shift_one)
    qkv_bias = jnp.concatenate([b_qv[:D], jnp.zeros((D,), jnp.float32), b_qv[D:]])
    projected = matmul(normed_out_one, w_qkv) + qkv_bias
    queries = projected[:, :D]
    keys_local = projected[:, D : 2 * D]
    values_local = projected[:, 2 * D :]
    query_heads = split_heads(queries)
    start_state = (
        jnp.full((HEADS, tok_rows), neg_big, jnp.float32),
        jnp.zeros((HEADS, tok_rows), jnp.float32),
        jnp.zeros((HEADS, tok_rows, HEAD_DIM), jnp.float32),
    )
    key_piece = lax.all_gather(keys_local, "seq", axis=0, tiled=True)
    value_piece = lax.all_gather(values_local, "seq", axis=0, tiled=True)

    def compute_block(state_in):
        key_pos = jnp.arange(key_piece.shape[0], dtype=jnp.int32)
        allowed = key_mask(key_pos)
        key_heads = split_heads(key_piece)
        value_heads = split_heads(value_piece)

        def one_head(ignored, head_item):
            q_head, k_head, v_head, old_max, old_sum, old_acc = head_item
            scores = jnp.where(allowed, matmul_nt(q_head, k_head) * score_scale, neg_big)
            new_max = jnp.maximum(old_max, jnp.max(scores, axis=1))
            weights_soft = jnp.where(allowed, jnp.exp(scores - new_max[:, None]), 0.0)
            decay_old = jnp.exp(old_max - new_max)
            new_sum = old_sum * decay_old + jnp.sum(weights_soft, axis=1)
            new_acc = old_acc * decay_old[:, None] + matmul(weights_soft, v_head)
            return (ignored, (new_max, new_sum, new_acc))

        unused, updated = lax.scan(
            one_head,
            jnp.zeros((), jnp.float32),
            (query_heads, key_heads, value_heads, state_in[0], state_in[1], state_in[2]),
        )
        return updated

    def keep_block(state_in):
        return (state_in[0], state_in[1], state_in[2])

    run_max, run_sum, run_acc = lax.cond(
        jnp.int32(0) > last_query, keep_block, compute_block, start_state
    )
    head_out = run_acc / run_sum[:, :, None]
    log_sum = run_max + jnp.log(run_sum)
    attended = join_heads(head_out)
    middle = layer_input + matmul(attended, w_out) + b_out
    normed_out_two, normed_two, inv_two = norm_forward(middle, gain_two, shift_two)
    pre_act = matmul(normed_out_two, w_up) + b_up
    activ = gelu_forward(pre_act)
    layer_output = middle + matmul(activ, w_down) + b_down
    d_down_b = jnp.sum(cotangent, axis=0)
    d_down_w = matmul_tn(activ, cotangent)
    d_pre = matmul_nt(cotangent, w_down) * gelu_slope(pre_act)
    d_up_b = jnp.sum(d_pre, axis=0)
    d_up_w = matmul_tn(normed_out_two, d_pre)
    d_norm_two, d_gain_two, d_shift_two = norm_backward(
        matmul_nt(d_pre, w_up), normed_two, inv_two, gain_two
    )
    d_middle = cotangent + d_norm_two
    d_out_b = jnp.sum(d_middle, axis=0)
    d_out_w = matmul_tn(attended, d_middle)
    d_att = matmul_nt(d_middle, w_out)
    dout_heads = split_heads(d_att)
    delta_heads = jnp.sum(dout_heads * head_out, axis=2)
    key_all, value_all = (
        lax.all_gather(keys_local, "seq", axis=0, tiled=True),
        lax.all_gather(values_local, "seq", axis=0, tiled=True),
    )
    allowed_all = key_mask(jnp.arange(group_rows, dtype=jnp.int32))

    def back_head(ignored, head_item):
        q_head, k_head, v_head, do_head, lse_head, delta_head = head_item
        scores = jnp.where(allowed_all, matmul_nt(q_head, k_head) * score_scale, neg_big)
        weights_soft = jnp.where(allowed_all, jnp.exp(scores - lse_head[:, None]), 0.0)
        dv_head = matmul_tn(weights_soft, do_head)
        d_soft = matmul_nt(do_head, v_head)
        d_scores = weights_soft * (d_soft - delta_head[:, None]) * score_scale
        return (ignored, (matmul(d_scores, k_head), matmul_tn(d_scores, q_head), dv_head))

    unused, head_grads = lax.scan(
        back_head,
        jnp.zeros((), jnp.float32),
        (
            query_heads,
            split_heads(key_all),
            split_heads(value_all),
            dout_heads,
            log_sum,
            delta_heads,
        ),
    )
    d_query = join_heads(head_grads[0])
    key_terms = join_heads(head_grads[1])
    value_terms = join_heads(head_grads[2])
    d_key, d_value = (
        lax.psum_scatter(key_terms, "seq", scatter_dimension=0, tiled=True),
        lax.psum_scatter(value_terms, "seq", scatter_dimension=0, tiled=True),
    )
    d_proj = jnp.concatenate([d_query, d_key, d_value], axis=1)
    d_qv_b = jnp.concatenate([jnp.sum(d_query, axis=0), jnp.sum(d_value, axis=0)])
    d_qkv_w = matmul_tn(normed_out_one, d_proj)
    d_norm_one, d_gain_one, d_shift_one = norm_backward(
        matmul_nt(d_proj, w_qkv), normed_one, inv_one, gain_one
    )
    input_grad = d_middle + d_norm_one
    summed = (
        lax.psum_scatter(d_qkv_w, ("dp", "seq"), scatter_dimension=0, tiled=True),
        lax.psum_scatter(d_qv_b, ("dp", "seq"), scatter_dimension=0, tiled=True),
        lax.psum_scatter(d_out_w, ("dp", "seq"), scatter_dimension=0, tiled=True),
        lax.psum_scatter(d_out_b, ("dp", "seq"), scatter_dimension=0, tiled=True),
        lax.psum_scatter(d_gain_one, ("dp", "seq"), scatter_dimension=0, tiled=True),
        lax.psum_scatter(d_shift_one, ("dp", "seq"), scatter_dimension=0, tiled=True),
        lax.psum_scatter(d_up_w, ("dp", "seq"), scatter_dimension=0, tiled=True),
        lax.psum_scatter(d_up_b, ("dp", "seq"), scatter_dimension=0, tiled=True),
        lax.psum_scatter(d_down_w, ("dp", "seq"), scatter_dimension=0, tiled=True),
        lax.psum_scatter(d_down_b, ("dp", "seq"), scatter_dimension=0, tiled=True),
        lax.psum_scatter(d_gain_two, ("dp", "seq"), scatter_dimension=0, tiled=True),
        lax.psum_scatter(d_shift_two, ("dp", "seq"), scatter_dimension=0, tiled=True),
    )
    return (
        layer_output,
        input_grad,
        summed[0],
        summed[1],
        summed[2],
        summed[3],
        summed[4],
        summed[5],
        summed[6],
        summed[7],
        summed[8],
        summed[9],
        summed[10],
        summed[11],
    )


def split(v):
    high=v.astype(bf16)
    return high,(v-high.astype(f32)).astype(bf16)

def dot_nn(a,b):
    return lax.dot_general(a,b,(((1,),(0,)),((),())),preferred_element_type=f32)
def dot_nt(a,b):
    return lax.dot_general(a,b,(((1,),(1,)),((),())),preferred_element_type=f32)
def dot_tn(a,b):
    return lax.dot_general(a,b,(((0,),(0,)),((),())),preferred_element_type=f32)

def fold(v):
    return v[:,:PAIR]+v[:,PAIR:]

def attend_kernel(len_ref,qkv_ref,*refs):
    out_ref,lse_ref=refs[-2:]
    rows=qkv_ref.shape[0]
    seq_len=len_ref[0]
    lane=lax.broadcasted_iota(jnp.int32,(1,PAIR),1)
    q_high,q_low=split(qkv_ref[:,:PAIR]*(HEAD_DIM**-0.5))
    q_both=jnp.concatenate([q_high,q_low],axis=1)
    v_high,v_low=split(qkv_ref[:,2*PAIR:])
    v_both=jnp.concatenate([v_high,v_low],axis=1)
    k_all=qkv_ref[:,PAIR:2*PAIR]
    k_parts=[]
    for head in range(2):
        kh,kl=split(jnp.where(lane//HEAD_DIM==head,k_all,0.0))
        k_parts.append((jnp.concatenate([kh,kh],axis=1),kl))
    for start in range(0,rows,TILE):
        stop=start+TILE
        q_pos=start+lax.broadcasted_iota(jnp.int32,(TILE,1),0)
        first=jnp.where(q_pos<seq_len,0,q_pos)
        k_pos=lax.broadcasted_iota(jnp.int32,(1,stop),1)
        allowed=(k_pos>=first)&(k_pos<=q_pos)
        outs,lses=[],[]
        for head in range(2):
            kd,kl=k_parts[head]
            scores=dot_nt(q_both[start:stop],kd[:stop])+dot_nt(q_high[start:stop],kl[:stop])
            scores=jnp.where(allowed,scores,neg_big)
            top=jnp.max(scores,axis=1,keepdims=True)
            probs=jnp.exp(scores-top)
            total=jnp.sum(probs,axis=1,keepdims=True)
            ph,pw=split(probs)
            acc=fold(dot_nn(ph,v_both[:stop]))+dot_nn(pw,v_high[:stop])
            outs.append(acc*(1.0/total))
            lses.append(jnp.broadcast_to(top+jnp.log(total),(TILE,PAIR)))
        out_ref[start:stop]=jnp.where(lane<HEAD_DIM,outs[0],outs[1])
        lse_ref[start:stop]=jnp.where(lane<HEAD_DIM,lses[0],lses[1])

def attend_back_kernel(len_ref,qkv_ref,do_ref,out_ref,lse_ref,*refs):
    grad_ref=refs[-1]
    rows=qkv_ref.shape[0]
    seq_len=len_ref[0]
    lane=lax.broadcasted_iota(jnp.int32,(1,PAIR),1)
    scale=HEAD_DIM**-0.5
    q_high,q_low=split(qkv_ref[:,:PAIR]*scale)
    q_both=jnp.concatenate([q_high,q_low],axis=1)
    q_twice=jnp.concatenate([q_high,q_high],axis=1)
    do_all=do_ref[...]
    do_high,do_low=split(do_all)
    do_both=jnp.concatenate([do_high,do_low],axis=1)
    do_twice=jnp.concatenate([do_high,do_high],axis=1)
    delta_t=jnp.transpose(do_all*out_ref[...])
    lse_t=jnp.transpose(lse_ref[...])
    dq=[[jnp.zeros((TILE,PAIR),f32) for _ in range(rows//TILE)] for _ in range(2)]
    for start in range(0,rows,TILE):
        stop=start+TILE
        n=rows-start
        k_pos=start+lax.broadcasted_iota(jnp.int32,(TILE,1),0)
        q_pos=start+lax.broadcasted_iota(jnp.int32,(1,n),1)
        first=jnp.where(q_pos<seq_len,0,q_pos)
        allowed=(k_pos>=first)&(k_pos<=q_pos)
        k_all=qkv_ref[start:stop,PAIR:2*PAIR]
        v_all=qkv_ref[start:stop,2*PAIR:]
        k_grads,v_grads=[],[]
        for head in range(2):
            mine=lane//HEAD_DIM==head
            kh,kl=split(jnp.where(mine,k_all,0.0))
            vh,vl=split(jnp.where(mine,v_all,0.0))
            k_both=jnp.concatenate([kh,kl],axis=1)
            v_both=jnp.concatenate([vh,vl],axis=1)
            scores=dot_nt(k_both,q_twice[start:])+dot_nt(kh,q_low[start:])
            lse_row=lse_t[head*HEAD_DIM:head*HEAD_DIM+1,start:]
            probs=jnp.where(allowed,jnp.exp(scores-lse_row),0.0)
            ph,pw=split(probs)
            v_grads.append(fold(dot_nn(ph,do_both[start:]))+dot_nn(pw,do_high[start:]))
            d_probs=dot_nt(v_both,do_twice[start:])+dot_nt(vh,do_low[start:])
            delta_row=jnp.sum(delta_t[head*HEAD_DIM:(head+1)*HEAD_DIM,start:],axis=0,keepdims=True)
            d_scores=probs*(d_probs-delta_row)
            sh,sl=split(d_scores)
            k_grads.append(fold(dot_nn(sh,q_both[start:]))+dot_nn(sl,q_high[start:]))
            part=fold(dot_tn(sh,k_both))+dot_tn(sl,kh)
            for t in range(n//TILE):
                dq[head][start//TILE+t]+=part[t*TILE:(t+1)*TILE]
        grad_ref[start:stop,PAIR:2*PAIR]=jnp.where(lane<HEAD_DIM,k_grads[0],k_grads[1])
        grad_ref[start:stop,2*PAIR:]=jnp.where(lane<HEAD_DIM,v_grads[0],v_grads[1])
        grad_ref[start:stop,:PAIR]=(dq[0][start//TILE]+dq[1][start//TILE])*scale

def attend(seq_len,qkv,*earlier):
    rows,cols=qkv.shape
    pairs=cols//(3*PAIR)
    block=lambda w: pl.BlockSpec((rows,w),lambda j:(0,j))
    return pl.pallas_call(
        attend_kernel,
        grid=(pairs,),
        in_specs=[pl.BlockSpec(memory_space=pltpu.SMEM),block(3*PAIR)]
        +[pl.BlockSpec(memory_space=pl.ANY)]*len(earlier),
        out_specs=[block(PAIR),block(PAIR)],
        out_shape=[jax.ShapeDtypeStruct((rows,pairs*PAIR),f32)]*2,
        compiler_params=pltpu.CompilerParams(vmem_limit_bytes=48*2**20),
        cost_estimate=pl.CostEstimate(flops=0,bytes_accessed=0,transcendentals=0),
        name="attend",
    )(seq_len,qkv,*earlier)

def attend_back(seq_len,qkv,d_out,out,lse,*earlier):
    rows,cols=qkv.shape
    pairs=cols//(3*PAIR)
    block=lambda w: pl.BlockSpec((rows,w),lambda j:(0,j))
    return pl.pallas_call(
        attend_back_kernel,
        grid=(pairs,),
        in_specs=[pl.BlockSpec(memory_space=pltpu.SMEM),block(3*PAIR),block(PAIR),block(PAIR),block(PAIR)]
        +[pl.BlockSpec(memory_space=pl.ANY)]*len(earlier),
        out_specs=block(3*PAIR),
        out_shape=jax.ShapeDtypeStruct((rows,cols),f32),
        compiler_params=pltpu.CompilerParams(vmem_limit_bytes=48*2**20),
        cost_estimate=pl.CostEstimate(flops=0,bytes_accessed=0,transcendentals=0),
        name="attend_back",
    )(seq_len,qkv,d_out,out,lse,*earlier)


COLUMNS = 4


def table(move):
    pairs = []
    for z in range(COLUMNS):
        for x in range(2):
            for core in range(2):
                for y in range(2):
                    there = move(z, x, core, y)
                    number = lambda p: ((p[0] * 2 + p[1]) * 2 + p[2]) * 2 + p[3]
                    pairs.append((number((z, x, core, y)), number(there)))
    return pairs


over_core = table(lambda z, x, core, y: (z, x, 1 - core, y))
over_x = table(lambda z, x, core, y: (z, 1 - x, core, y))
over_y = table(lambda z, x, core, y: (z, x, core, 1 - y))
over_z = [None] + [
    table(lambda z, x, core, y, k=k: (z ^ k, x, core, y)) for k in range(1, COLUMNS)
]


def swap(values, pairs):
    return lax.ppermute(values, AXES, pairs)


def place():
    dp = lax.axis_index("dp")
    return dp // 4, (dp // 2) % 2, dp % 2, lax.axis_index("seq")


def pick(values, index, axis):
    return lax.dynamic_index_in_dim(values, index, axis, keepdims=False)


def order_kernel(*refs):
    pass


def after(values, *earlier):
    anywhere = pl.BlockSpec(memory_space=pl.ANY)
    return pl.pallas_call(
        order_kernel,
        in_specs=[anywhere] * (1 + len(earlier)),
        out_specs=anywhere,
        out_shape=jax.ShapeDtypeStruct(values.shape, values.dtype),
        input_output_aliases={0: 0},
        cost_estimate=pl.CostEstimate(flops=0, bytes_accessed=0, transcendentals=0),
        name="after",
    )(values, *earlier)


def assemble_kernel(plan, place_ref, *refs):
    count, copies_of = plan
    pieces, outs, sems = refs[:count], refs[count:-1], refs[-1]
    mine = [place_ref[i] for i in range(4)]
    copies = []
    for piece, source, out, shift, axes in copies_of:
        slot = tuple(mine[axis] ^ move for axis, move in zip(axes, shift))
        copies.append(
            pltpu.make_async_copy(
                pieces[piece].at[source], outs[out].at[slot], sems.at[len(copies)]
            )
        )
    for copy in copies:
        copy.start()
    for copy in copies:
        copy.wait()


def assemble(where, pieces, shapes, copies):
    anywhere = pl.BlockSpec(memory_space=pl.ANY)
    whole = pl.BlockSpec(memory_space=pltpu.VMEM)
    size = 4 * sum(functools.reduce(lambda m, n: m * n, shape) for shape in shapes)
    return pl.pallas_call(
        functools.partial(assemble_kernel, (len(pieces), copies)),
        in_specs=[pl.BlockSpec(memory_space=pltpu.SMEM)] + [anywhere] * len(pieces),
        out_specs=[whole] * len(shapes),
        out_shape=[jax.ShapeDtypeStruct(shape, f32) for shape in shapes],
        scratch_shapes=[pltpu.SemaphoreType.DMA((len(copies),))],
        compiler_params=pltpu.CompilerParams(vmem_limit_bytes=size + 4 * 2**20),
        cost_estimate=pl.CostEstimate(flops=0, bytes_accessed=0, transcendentals=0),
        name="assemble",
    )(where, *pieces)


def plane_pieces():
    for k in range(COLUMNS):
        yield 0, k, k, 0, 0
        yield 1, k, k, 1, 0
        yield 2, k, k, 0, 1
        yield 3 + k // 2, k % 2, k, 1, 1


def gather_column(shard):
    return jnp.stack([shard] + [swap(shard, over_z[k]) for k in range(1, COLUMNS)])


def gather_sides(own):
    return swap(own, over_x), swap(own, over_y)


def gather_corners(beside_x, beside_y, before_x, before_y):
    return (
        swap(after(beside_y[:2], *before_x), over_x),
        swap(after(beside_x[2:], *before_y), over_y),
    )


def by_core(own, other, core, axis):
    return jnp.where(
        core == 0, jnp.stack([own, other], axis), jnp.stack([other, own], axis)
    )


def plane_sent(chip, x, y, y_axis):
    return pick(chip[:2], 1 - x, 1), pick(chip[2:], 1 - y, y_axis)


def over_plane(chip, sent, x, y, y_axis, earlier):
    low = pick(chip[:2], x, 1) + after(swap(sent[0], over_x), earlier)
    high = pick(chip[2:], y, y_axis) + after(swap(sent[1], over_y), earlier)
    return low, high


def corner_sent(low, high, x, y, y_axis):
    return pick(low, 1 - y, y_axis - 1), pick(high, 1 - x, 1)


def over_corner(low, high, sent, x, y, y_axis, earlier):
    from_y = after(swap(sent[0], over_y), earlier)
    from_x = after(swap(sent[1], over_x), earlier)
    return jnp.concatenate([pick(low, y, y_axis - 1) + from_y, pick(high, x, 1) + from_x])


def sum_column(column, z, *earlier):
    total = pick(column, z, 0)
    for k in range(1, COLUMNS):
        arrived = swap(pick(column, z ^ k, 0), over_z[k])
        total = total + (after(arrived, *earlier) if earlier else arrived)
    return total


def normalise(values):
    centred = values - jnp.mean(values, axis=1, keepdims=True)
    inv_std = lax.rsqrt(jnp.mean(centred * centred, axis=1, keepdims=True) + eps_norm)
    return centred * inv_std, inv_std


def body_grid(
    layer_input,
    cotangent,
    seq_lengths,
    qkv_weight,
    qv_bias,
    out_weight,
    out_bias,
    first_gain,
    first_shift,
    up_weight,
    up_bias,
    down_weight,
    down_bias,
    second_gain,
    second_shift,
):
    z, x, core, y = place()
    where = jnp.stack([z, x, core, y]).astype(jnp.int32)
    rows = layer_input.shape[0]
    shard = qkv_weight.shape[0]
    half = D // 2
    pairs = half // PAIR
    wide = 3 * half
    hidden = 2 * D

    def both_rows(own, other):
        return jnp.where(
            y == 0, jnp.concatenate([own, other]), jnp.concatenate([other, own])
        )

    def rows_of(values, part):
        return lax.dynamic_slice_in_dim(values, part * rows, rows, 0)

    normed_own, inv_one = normalise(layer_input)
    other_normed = swap(normed_own, over_y)
    other_cotangent = swap(cotangent, over_core)

    by_head = qkv_weight.reshape(shard, 3, 2, pairs, PAIR).transpose(2, 0, 3, 1, 4)
    by_head = by_head.reshape(2, shard, wide)
    line_one = jnp.concatenate([qv_bias, out_bias, first_gain, first_shift])
    line_two = jnp.concatenate([up_bias, down_bias])
    line_three = jnp.concatenate([second_gain, second_shift])
    lines = jnp.stack(
        [jnp.pad(line, (0, PAIR - line.shape[0])) for line in (line_one, line_two, line_three)]
    )
    small = jnp.pad(lines, ((0, shard - 3), (0, 0)))
    sent = swap(jnp.concatenate([pick(by_head, 1 - y, 0), small], axis=1), over_y)
    kept = jnp.concatenate([pick(by_head, y, 0), small], axis=1)
    block = jnp.where(y == 0, jnp.stack([kept, sent]), jnp.stack([sent, kept]))
    column = gather_column(block)
    beside = swap(column, over_x)

    by_unit = up_weight.reshape(shard, 2 * COLUMNS, 2, 8 * shard).transpose(2, 0, 1, 3)
    by_unit = by_unit.reshape(2, shard, hidden)
    kept_up = pick(by_unit, core, 0)
    arrived_up = swap(pick(by_unit, 1 - core, 0), over_core)
    both_up = by_core(kept_up, arrived_up, core, 1).reshape(shard, 2 * hidden)
    shard_a = after(jnp.concatenate([out_weight, both_up], axis=1), column)
    arrived_a = [swap(shard_a, over_z[k]) for k in range(1, COLUMNS)]
    own_a = jnp.stack([shard_a] + arrived_a)
    beside = after(beside, arrived_a[0])
    arrived_b = [swap(after(down_weight, own_a), over_z[k]) for k in range(1, COLUMNS)]
    own_a = after(own_a, beside)
    sides_a = gather_sides(own_a)

    pieces = [column, beside]
    pieces += [swap(column, over_core), swap(after(beside, other_normed), over_core)]
    copies = []
    for k in range(COLUMNS):
        for piece in range(4):
            shift = (k, piece % 2, piece // 2)
            copies.append((piece, (k, slice(None), slice(None), slice(0, wide)), 0, shift, (0, 1, 2)))
            copies.append(
                (piece, (k, slice(None), slice(0, 8), slice(wide, wide + PAIR)), 1, shift, (0, 1, 2))
            )
    grid = (COLUMNS, 2, 2, 2)
    w_qkv, lines = assemble(
        where, pieces, [grid + (shard, wide), grid + (8, PAIR)], copies
    )
    w_qkv = w_qkv.reshape(D, wide)
    lines = lines.reshape(32, 8, PAIR)
    b_qv = lines[:, 0, : 2 * shard].reshape(2 * D)
    b_out = lines[:, 0, 2 * shard : 3 * shard].reshape(D)
    gain_one = lines[:, 0, 3 * shard : 4 * shard].reshape(D)
    shift_one = lines[:, 0, 4 * shard : 5 * shard].reshape(D)
    b_up = lines[:, 1, : 4 * shard].reshape(2 * COLUMNS, 2, 2, 4 * shard)
    b_up = pick(b_up, core, 1).reshape(hidden)
    b_down = lines[:, 1, 4 * shard : 5 * shard].reshape(D)
    gain_two = lines[:, 2, :shard].reshape(D)
    shift_two = lines[:, 2, shard : 2 * shard].reshape(D)

    normed_one = both_rows(normed_own, other_normed)
    normed_out_one = normed_one * gain_one + shift_one
    bias = pick(b_qv.reshape(2, 2, pairs, PAIR), y, 1)
    qkv_bias = jnp.stack([bias[0], jnp.zeros_like(bias[0]), bias[1]], axis=1).reshape(wide)
    projected = matmul(normed_out_one, w_qkv) + qkv_bias
    own_b = jnp.stack([down_weight] + [after(piece, projected) for piece in arrived_b])
    head_out, log_sum = attend(seq_lengths, projected, own_b)
    there = swap(rows_of(head_out, 1 - y), over_y)
    here = rows_of(head_out, y)
    attended = jnp.where(
        y == 0, jnp.concatenate([here, there], 1), jnp.concatenate([there, here], 1)
    )

    corners_a = gather_corners(*sides_a, [head_out], [there])
    sides_b = swap(after(own_b, head_out), over_x), swap(after(own_b, there), over_y)
    corners_b = gather_corners(*sides_b, corners_a, corners_a)
    every = slice(None)
    copies = []
    for piece, at, dz, dx, dy in plane_pieces():
        copies.append((piece, (at, every, slice(0, D)), 0, (dz, dx, dy), (0, 1, 3)))
    w_out_half, = assemble(
        where, [own_a, *sides_a, *corners_a], [(COLUMNS, 2, 2, shard, D)], copies
    )
    copies = []
    for piece, at, dz, dx, dy in plane_pieces():
        for c in range(2):
            cols = slice(D + c * hidden, D + (c + 1) * hidden)
            copies.append((piece, (at, every, cols), c, (dz, dx, dy), (0, 1, 3)))
    w_up_parts = assemble(
        where, [own_a, *sides_a, *corners_a], [(COLUMNS, 2, 2, shard, hidden)] * 2, copies
    )
    copies = []
    for piece, at, dz, dx, dy in plane_pieces():
        copies.append((piece, (at,), 0, (dz, dx, dy), (0, 1, 3)))
    w_down, = assemble(
        where, [own_b, *sides_b, *corners_b], [(COLUMNS, 2, 2, 4 * shard, D)], copies
    )
    w_out = by_core(w_out_half, swap(w_out_half, over_core), core, 2).reshape(D, D)
    w_up = jnp.stack(w_up_parts, axis=2).reshape(D, hidden)
    w_down = w_down.reshape(hidden, D)

    middle = layer_input + matmul(attended, w_out) + b_out
    normed_out_two, normed_two, inv_two = norm_forward(middle, gain_two, shift_two)
    both_normed = jnp.concatenate([normed_out_two, swap(normed_out_two, over_core)])
    both_cotangent = jnp.concatenate([cotangent, other_cotangent])
    raw_act = matmul(both_normed, w_up)
    pre_act = raw_act + b_up
    activ = gelu_forward(pre_act)

    d_down_b = jnp.sum(cotangent, axis=0)
    d_down_w = matmul_tn(activ, both_cotangent)
    chip_b = d_down_w.reshape(COLUMNS, 2, 2, 4 * shard, D)
    d_pre = matmul_nt(both_cotangent, w_down) * gelu_slope(pre_act)
    d_up_b = jnp.sum(d_pre, axis=0)
    d_part = matmul_nt(d_pre, w_up)
    d_norm_two, d_gain_two, d_shift_two = norm_backward(
        d_part[:rows] + swap(d_part[rows:], over_core), normed_two, inv_two, gain_two
    )
    d_middle = cotangent + d_norm_two
    d_att = matmul_nt(d_middle, w_out)
    d_heads = d_att.reshape(rows, 2, half)
    sent = pick(d_heads, 1 - y, 1)
    d_out = both_rows(pick(d_heads, y, 1), swap(sent, over_y))
    down_part = matmul(gelu_forward(raw_act + after(b_up, sent)), w_down)
    layer_output = middle + down_part[:rows] + swap(down_part[rows:], over_core) + b_down
    chip_a = matmul_tn(both_normed, d_pre).reshape(COLUMNS, 2, 2, 2, shard, hidden)
    low_b, high_b = over_plane(chip_b, plane_sent(chip_b, x, y, 2), x, y, 2, chip_a)
    sent_b = corner_sent(low_b, high_b, x, y, 2)
    column_b = over_corner(low_b, high_b, sent_b, x, y, 2, sent)
    low_a, high_a = over_plane(chip_a, plane_sent(chip_a, x, y, 3), x, y, 3, sent)
    sent_a = corner_sent(low_a, high_a, x, y, 3)
    d_out_b = jnp.sum(d_middle, axis=0)
    d_out_w = matmul_tn(attended, d_middle).reshape(COLUMNS, 2, 2, 2, shard, D)

    d_proj = attend_back(
        seq_lengths, projected, d_out, head_out, log_sum, *sent_a, column_b
    )
    d_qkv_w = matmul_tn(normed_out_one, d_proj)
    grid = d_qkv_w.reshape(COLUMNS, 2, 2, 2, shard, wide)
    first = pick(grid, 1 - core, 2)
    grid = pick(grid, core, 2) + swap(first, over_core)
    sent = pick(grid, 1 - x, 1)
    grid = pick(grid, x, 1) + swap(sent, over_x)
    column_a = over_corner(low_a, high_a, sent_a, x, y, 3, first)
    down_grad = sum_column(column_b, z, first)
    up_parts = sum_column(column_a, z, sent)
    arrived = swap(pick(up_parts, 1 - core, 0), over_core)
    up_grad = by_core(
        pick(up_parts, core, 0).reshape(shard, 2 * COLUMNS, 8 * shard),
        arrived.reshape(shard, 2 * COLUMNS, 8 * shard),
        core,
        2,
    ).reshape(shard, 4 * D)

    column_qkv = grid
    grid = sum_column(column_qkv, z)
    here = pick(grid, y, 0)
    there = swap(pick(grid, 1 - y, 0), over_y)
    qkv_grad = jnp.where(y == 0, jnp.stack([here, there]), jnp.stack([there, here]))
    qkv_grad = qkv_grad.reshape(2, shard, pairs, 3, PAIR).transpose(1, 3, 0, 2, 4)

    d_norm = matmul_nt(d_proj, after(w_qkv, first))
    d_gain_one = jnp.sum(d_norm * normed_one, axis=0)
    d_shift_one = jnp.sum(d_norm, axis=0)
    d_norm_other = swap(after(rows_of(d_norm, 1 - y), sent), over_y)
    d_norm_own = rows_of(d_norm, y) + after(d_norm_other, here)
    d_norm_one, unused, unused = norm_backward(
        d_norm_own, normed_own, inv_one, gain_one
    )
    input_grad = d_middle + d_norm_one

    d_bias = jnp.sum(d_proj, axis=0).reshape(pairs, 3, PAIR)
    d_bias = jnp.stack([d_bias[:, 0], d_bias[:, 2]]).reshape(2, 1, half)
    blank = jnp.zeros_like(d_bias)
    d_qv_b = jnp.where(
        y == 0, jnp.concatenate([d_bias, blank], 1), jnp.concatenate([blank, d_bias], 1)
    )

    d_up_b = d_up_b.reshape(2 * COLUMNS, 8 * shard)
    d_up_b = by_core(d_up_b, jnp.zeros_like(d_up_b), core, 1)

    def lanes(*vectors):
        line = jnp.concatenate([v.reshape(32, -1) for v in vectors], axis=1)
        return jnp.pad(line, ((0, 0), (0, PAIR - line.shape[1])))

    lines = jnp.stack(
        [
            lanes(d_qv_b, d_out_b, d_gain_one, d_shift_one),
            lanes(d_up_b, d_down_b),
            lanes(d_gain_two, d_shift_two),
        ],
        axis=1,
    )
    small = jnp.pad(lines, ((0, 0), (0, shard - 3), (0, 0)))
    small = small.reshape(COLUMNS, 2, 2, 2, shard, PAIR)
    grid = jnp.concatenate([d_out_w, small], axis=-1)
    grid = pick(grid, core, 2) + swap(after(pick(grid, 1 - core, 2), sent), over_core)
    grid = pick(grid, y, 2) + after(swap(pick(grid, 1 - y, 2), over_y), column_qkv)
    grid = pick(grid, x, 1) + swap(pick(grid, 1 - x, 1), over_x)
    grid = sum_column(grid, z)
    out_grad, lines = grid[:, :D], grid[:, D:]
    return (
        layer_output,
        input_grad,
        qkv_grad.reshape(shard, 3 * D),
        lines[0, : 2 * shard],
        out_grad,
        lines[0, 2 * shard : 3 * shard],
        lines[0, 3 * shard : 4 * shard],
        lines[0, 4 * shard : 5 * shard],
        up_grad,
        lines[1, : 4 * shard],
        down_grad,
        lines[1, 4 * shard : 5 * shard],
        lines[2, :shard],
        lines[2, shard : 2 * shard],
    )


def solution(mesh):
    shape = (mesh.shape["dp"], mesh.shape["seq"])
    body = body_grid if shape == (COLUMNS * 4, 2) else body_general
    row = P(AXES, None)
    vec = P(AXES)
    return jax.shard_map(
        body,
        mesh=mesh,
        in_specs=(row, row, P("dp"), row, vec, row, vec, vec, vec, row, vec, row, vec, vec, vec),
        out_specs=(row, row, row, vec, row, vec, vec, vec, row, vec, row, vec, vec, vec),
        check_vma=False,
    )
```

```python
import functools

import jax
import jax.numpy as jnp
from jax import lax
from jax.experimental import pallas as pl
from jax.experimental.pallas import tpu as pltpu
from jax.sharding import PartitionSpec as P

D = 768
HEADS = 12
HEAD_DIM = 64
PAIR = 2 * HEAD_DIM
TILE = 256
AXES = ("dp", "seq")

eps_norm = 1e-05
neg_big = -1e30
top_prec = lax.Precision.HIGH
f32 = jnp.float32
bf16 = jnp.bfloat16


def matmul(left, right):
    return jnp.dot(left, right, precision=top_prec, preferred_element_type=jnp.float32)


def matmul_tn(left, right):
    return lax.dot_general(
        left,
        right,
        (((0,), (0,)), ((), ())),
        precision=top_prec,
        preferred_element_type=jnp.float32,
    )


def matmul_nt(left, right):
    return lax.dot_general(
        left,
        right,
        (((1,), (1,)), ((), ())),
        precision=top_prec,
        preferred_element_type=jnp.float32,
    )


def norm_forward(values, gain, shift):
    centred = values - jnp.mean(values, axis=1, keepdims=True)
    inv_std = lax.rsqrt(jnp.mean(centred * centred, axis=1, keepdims=True) + eps_norm)
    normed = centred * inv_std
    return (normed * gain + shift, normed, inv_std)


def norm_backward(upstream, normed, inv_std, gain):
    scaled = upstream * gain
    inner = (
        scaled
        - jnp.mean(scaled, axis=1, keepdims=True)
        - normed * jnp.mean(scaled * normed, axis=1, keepdims=True)
    )
    return (inner * inv_std, jnp.sum(upstream * normed, axis=0), jnp.sum(upstream, axis=0))


def split_heads(values):
    return values.reshape(values.shape[0], HEADS, HEAD_DIM).transpose(1, 0, 2)


def join_heads(values):
    return values.transpose(1, 0, 2).reshape(values.shape[1], HEADS * HEAD_DIM)


def gelu_forward(values):
    return 0.5 * values * (1.0 + lax.erf(values * 0.7071067811865476))


def gelu_slope(values):
    cdf_part = 0.5 * (1.0 + lax.erf(values * 0.7071067811865476))
    return cdf_part + values * jnp.exp(-0.5 * values * values) * 0.3989422804014327


def body_general(
    layer_input,
    cotangent,
    seq_lengths,
    qkv_weight,
    qv_bias,
    out_weight,
    out_bias,
    first_gain,
    first_shift,
    up_weight,
    up_bias,
    down_weight,
    down_bias,
    second_gain,
    second_shift,
):
    gathered = (
        lax.all_gather(qkv_weight, ("dp", "seq"), axis=0, tiled=True),
        lax.all_gather(qv_bias, ("dp", "seq"), axis=0, tiled=True),
        lax.all_gather(out_weight, ("dp", "seq"), axis=0, tiled=True),
        lax.all_gather(out_bias, ("dp", "seq"), axis=0, tiled=True),
        lax.all_gather(first_gain, ("dp", "seq"), axis=0, tiled=True),
        lax.all_gather(first_shift, ("dp", "seq"), axis=0, tiled=True),
        lax.all_gather(up_weight, ("dp", "seq"), axis=0, tiled=True),
        lax.all_gather(up_bias, ("dp", "seq"), axis=0, tiled=True),
        lax.all_gather(down_weight, ("dp", "seq"), axis=0, tiled=True),
        lax.all_gather(down_bias, ("dp", "seq"), axis=0, tiled=True),
        lax.all_gather(second_gain, ("dp", "seq"), axis=0, tiled=True),
        lax.all_gather(second_shift, ("dp", "seq"), axis=0, tiled=True),
    )
    (
        w_qkv,
        b_qv,
        w_out,
        b_out,
        gain_one,
        shift_one,
        w_up,
        b_up,
        w_down,
        b_down,
        gain_two,
        shift_two,
    ) = gathered
    tok_rows = layer_input.shape[0]
    group_rows = tok_rows * lax.axis_size("seq")
    score_scale = HEAD_DIM ** (-0.5)
    seq_len = seq_lengths[0]
    first_own = lax.axis_index("seq") * tok_rows
    query_pos = first_own + jnp.arange(tok_rows, dtype=jnp.int32)
    last_query = first_own + tok_rows - 1

    def segment_of(positions):
        return jnp.where(positions < seq_len, 0, positions + 1)

    query_seg = segment_of(query_pos)

    def key_mask(key_pos):
        return (segment_of(key_pos)[None, :] == query_seg[:, None]) & (
            key_pos[None, :] <= query_pos[:, None]
        )

    normed_out_one, normed_one, inv_one = norm_forward(layer_input, gain_one, shift_one)
    qkv_bias = jnp.concatenate([b_qv[:D], jnp.zeros((D,), jnp.float32), b_qv[D:]])
    projected = matmul(normed_out_one, w_qkv) + qkv_bias
    queries = projected[:, :D]
    keys_local = projected[:, D : 2 * D]
    values_local = projected[:, 2 * D :]
    query_heads = split_heads(queries)
    start_state = (
        jnp.full((HEADS, tok_rows), neg_big, jnp.float32),
        jnp.zeros((HEADS, tok_rows), jnp.float32),
        jnp.zeros((HEADS, tok_rows, HEAD_DIM), jnp.float32),
    )
    key_piece = lax.all_gather(keys_local, "seq", axis=0, tiled=True)
    value_piece = lax.all_gather(values_local, "seq", axis=0, tiled=True)

    def compute_block(state_in):
        key_pos = jnp.arange(key_piece.shape[0], dtype=jnp.int32)
        allowed = key_mask(key_pos)
        key_heads = split_heads(key_piece)
        value_heads = split_heads(value_piece)

        def one_head(ignored, head_item):
            q_head, k_head, v_head, old_max, old_sum, old_acc = head_item
            scores = jnp.where(allowed, matmul_nt(q_head, k_head) * score_scale, neg_big)
            new_max = jnp.maximum(old_max, jnp.max(scores, axis=1))
            weights_soft = jnp.where(allowed, jnp.exp(scores - new_max[:, None]), 0.0)
            decay_old = jnp.exp(old_max - new_max)
            new_sum = old_sum * decay_old + jnp.sum(weights_soft, axis=1)
            new_acc = old_acc * decay_old[:, None] + matmul(weights_soft, v_head)
            return (ignored, (new_max, new_sum, new_acc))

        unused, updated = lax.scan(
            one_head,
            jnp.zeros((), jnp.float32),
            (query_heads, key_heads, value_heads, state_in[0], state_in[1], state_in[2]),
        )
        return updated

    def keep_block(state_in):
        return (state_in[0], state_in[1], state_in[2])

    run_max, run_sum, run_acc = lax.cond(
        jnp.int32(0) > last_query, keep_block, compute_block, start_state
    )
    head_out = run_acc / run_sum[:, :, None]
    log_sum = run_max + jnp.log(run_sum)
    attended = join_heads(head_out)
    middle = layer_input + matmul(attended, w_out) + b_out
    normed_out_two, normed_two, inv_two = norm_forward(middle, gain_two, shift_two)
    pre_act = matmul(normed_out_two, w_up) + b_up
    activ = gelu_forward(pre_act)
    layer_output = middle + matmul(activ, w_down) + b_down
    d_down_b = jnp.sum(cotangent, axis=0)
    d_down_w = matmul_tn(activ, cotangent)
    d_pre = matmul_nt(cotangent, w_down) * gelu_slope(pre_act)
    d_up_b = jnp.sum(d_pre, axis=0)
    d_up_w = matmul_tn(normed_out_two, d_pre)
    d_norm_two, d_gain_two, d_shift_two = norm_backward(
        matmul_nt(d_pre, w_up), normed_two, inv_two, gain_two
    )
    d_middle = cotangent + d_norm_two
    d_out_b = jnp.sum(d_middle, axis=0)
    d_out_w = matmul_tn(attended, d_middle)
    d_att = matmul_nt(d_middle, w_out)
    dout_heads = split_heads(d_att)
    delta_heads = jnp.sum(dout_heads * head_out, axis=2)
    key_all, value_all = (
        lax.all_gather(keys_local, "seq", axis=0, tiled=True),
        lax.all_gather(values_local, "seq", axis=0, tiled=True),
    )
    allowed_all = key_mask(jnp.arange(group_rows, dtype=jnp.int32))

    def back_head(ignored, head_item):
        q_head, k_head, v_head, do_head, lse_head, delta_head = head_item
        scores = jnp.where(allowed_all, matmul_nt(q_head, k_head) * score_scale, neg_big)
        weights_soft = jnp.where(allowed_all, jnp.exp(scores - lse_head[:, None]), 0.0)
        dv_head = matmul_tn(weights_soft, do_head)
        d_soft = matmul_nt(do_head, v_head)
        d_scores = weights_soft * (d_soft - delta_head[:, None]) * score_scale
        return (ignored, (matmul(d_scores, k_head), matmul_tn(d_scores, q_head), dv_head))

    unused, head_grads = lax.scan(
        back_head,
        jnp.zeros((), jnp.float32),
        (
            query_heads,
            split_heads(key_all),
            split_heads(value_all),
            dout_heads,
            log_sum,
            delta_heads,
        ),
    )
    d_query = join_heads(head_grads[0])
    key_terms = join_heads(head_grads[1])
    value_terms = join_heads(head_grads[2])
    d_key, d_value = (
        lax.psum_scatter(key_terms, "seq", scatter_dimension=0, tiled=True),
        lax.psum_scatter(value_terms, "seq", scatter_dimension=0, tiled=True),
    )
    d_proj = jnp.concatenate([d_query, d_key, d_value], axis=1)
    d_qv_b = jnp.concatenate([jnp.sum(d_query, axis=0), jnp.sum(d_value, axis=0)])
    d_qkv_w = matmul_tn(normed_out_one, d_proj)
    d_norm_one, d_gain_one, d_shift_one = norm_backward(
        matmul_nt(d_proj, w_qkv), normed_one, inv_one, gain_one
    )
    input_grad = d_middle + d_norm_one
    summed = (
        lax.psum_scatter(d_qkv_w, ("dp", "seq"), scatter_dimension=0, tiled=True),
        lax.psum_scatter(d_qv_b, ("dp", "seq"), scatter_dimension=0, tiled=True),
        lax.psum_scatter(d_out_w, ("dp", "seq"), scatter_dimension=0, tiled=True),
        lax.psum_scatter(d_out_b, ("dp", "seq"), scatter_dimension=0, tiled=True),
        lax.psum_scatter(d_gain_one, ("dp", "seq"), scatter_dimension=0, tiled=True),
        lax.psum_scatter(d_shift_one, ("dp", "seq"), scatter_dimension=0, tiled=True),
        lax.psum_scatter(d_up_w, ("dp", "seq"), scatter_dimension=0, tiled=True),
        lax.psum_scatter(d_up_b, ("dp", "seq"), scatter_dimension=0, tiled=True),
        lax.psum_scatter(d_down_w, ("dp", "seq"), scatter_dimension=0, tiled=True),
        lax.psum_scatter(d_down_b, ("dp", "seq"), scatter_dimension=0, tiled=True),
        lax.psum_scatter(d_gain_two, ("dp", "seq"), scatter_dimension=0, tiled=True),
        lax.psum_scatter(d_shift_two, ("dp", "seq"), scatter_dimension=0, tiled=True),
    )
    return (
        layer_output,
        input_grad,
        summed[0],
        summed[1],
        summed[2],
        summed[3],
        summed[4],
        summed[5],
        summed[6],
        summed[7],
        summed[8],
        summed[9],
        summed[10],
        summed[11],
    )


def split(v):
    high=v.astype(bf16)
    return high,(v-high.astype(f32)).astype(bf16)

def dot_nn(a,b):
    return lax.dot_general(a,b,(((1,),(0,)),((),())),preferred_element_type=f32)
def dot_nt(a,b):
    return lax.dot_general(a,b,(((1,),(1,)),((),())),preferred_element_type=f32)
def dot_tn(a,b):
    return lax.dot_general(a,b,(((0,),(0,)),((),())),preferred_element_type=f32)

def fold(v):
    return v[:,:PAIR]+v[:,PAIR:]

def attend_kernel(len_ref,qkv_ref,*refs):
    out_ref,lse_ref=refs[-2:]
    rows=qkv_ref.shape[0]
    seq_len=len_ref[0]
    lane=lax.broadcasted_iota(jnp.int32,(1,PAIR),1)
    q_high,q_low=split(qkv_ref[:,:PAIR]*(HEAD_DIM**-0.5))
    q_both=jnp.concatenate([q_high,q_low],axis=1)
    v_high,v_low=split(qkv_ref[:,2*PAIR:])
    v_both=jnp.concatenate([v_high,v_low],axis=1)
    k_all=qkv_ref[:,PAIR:2*PAIR]
    k_parts=[]
    for head in range(2):
        kh,kl=split(jnp.where(lane//HEAD_DIM==head,k_all,0.0))
        k_parts.append((jnp.concatenate([kh,kh],axis=1),kl))
    for start in range(0,rows,TILE):
        stop=start+TILE
        q_pos=start+lax.broadcasted_iota(jnp.int32,(TILE,1),0)
        first=jnp.where(q_pos<seq_len,0,q_pos)
        k_pos=lax.broadcasted_iota(jnp.int32,(1,stop),1)
        allowed=(k_pos>=first)&(k_pos<=q_pos)
        outs,lses=[],[]
        for head in range(2):
            kd,kl=k_parts[head]
            scores=dot_nt(q_both[start:stop],kd[:stop])+dot_nt(q_high[start:stop],kl[:stop])
            scores=jnp.where(allowed,scores,neg_big)
            top=jnp.max(scores,axis=1,keepdims=True)
            probs=jnp.exp(scores-top)
            total=jnp.sum(probs,axis=1,keepdims=True)
            ph,pw=split(probs)
            acc=fold(dot_nn(ph,v_both[:stop]))+dot_nn(pw,v_high[:stop])
            outs.append(acc*(1.0/total))
            lses.append(jnp.broadcast_to(top+jnp.log(total),(TILE,PAIR)))
        out_ref[start:stop]=jnp.where(lane<HEAD_DIM,outs[0],outs[1])
        lse_ref[start:stop]=jnp.where(lane<HEAD_DIM,lses[0],lses[1])

def attend_back_kernel(len_ref,qkv_ref,do_ref,out_ref,lse_ref,*refs):
    grad_ref,sum_ref=refs[-2:]
    rows=qkv_ref.shape[0]
    seq_len=len_ref[0]
    lane=lax.broadcasted_iota(jnp.int32,(1,PAIR),1)
    scale=HEAD_DIM**-0.5
    q_high,q_low=split(qkv_ref[:,:PAIR]*scale)
    q_both=jnp.concatenate([q_high,q_low],axis=1)
    q_twice=jnp.concatenate([q_high,q_high],axis=1)
    do_all=do_ref[...]
    do_high,do_low=split(do_all)
    do_both=jnp.concatenate([do_high,do_low],axis=1)
    do_twice=jnp.concatenate([do_high,do_high],axis=1)
    delta_t=jnp.transpose(do_all*out_ref[...])
    lse_t=jnp.transpose(lse_ref[...])
    dq=[[jnp.zeros((TILE,PAIR),f32) for _ in range(rows//TILE)] for _ in range(2)]
    for start in range(0,rows,TILE):
        stop=start+TILE
        n=rows-start
        k_pos=start+lax.broadcasted_iota(jnp.int32,(TILE,1),0)
        q_pos=start+lax.broadcasted_iota(jnp.int32,(1,n),1)
        first=jnp.where(q_pos<seq_len,0,q_pos)
        allowed=(k_pos>=first)&(k_pos<=q_pos)
        k_all=qkv_ref[start:stop,PAIR:2*PAIR]
        v_all=qkv_ref[start:stop,2*PAIR:]
        k_grads,v_grads=[],[]
        for head in range(2):
            mine=lane//HEAD_DIM==head
            kh,kl=split(jnp.where(mine,k_all,0.0))
            vh,vl=split(jnp.where(mine,v_all,0.0))
            k_both=jnp.concatenate([kh,kl],axis=1)
            v_both=jnp.concatenate([vh,vl],axis=1)
            scores=dot_nt(k_both,q_twice[start:])+dot_nt(kh,q_low[start:])
            lse_row=lse_t[head*HEAD_DIM:head*HEAD_DIM+1,start:]
            probs=jnp.where(allowed,jnp.exp(scores-lse_row),0.0)
            ph,pw=split(probs)
            v_grads.append(fold(dot_nn(ph,do_both[start:]))+dot_nn(pw,do_high[start:]))
            d_probs=dot_nt(v_both,do_twice[start:])+dot_nt(vh,do_low[start:])
            delta_row=jnp.sum(delta_t[head*HEAD_DIM:(head+1)*HEAD_DIM,start:],axis=0,keepdims=True)
            d_scores=probs*(d_probs-delta_row)
            sh,sl=split(d_scores)
            k_grads.append(fold(dot_nn(sh,q_both[start:]))+dot_nn(sl,q_high[start:]))
            part=fold(dot_tn(sh,k_both))+dot_tn(sl,kh)
            for t in range(n//TILE):
                dq[head][start//TILE+t]+=part[t*TILE:(t+1)*TILE]
        grad_ref[start:stop,PAIR:2*PAIR]=jnp.where(lane<HEAD_DIM,k_grads[0],k_grads[1])
        grad_ref[start:stop,2*PAIR:]=jnp.where(lane<HEAD_DIM,v_grads[0],v_grads[1])
        grad_ref[start:stop,:PAIR]=(dq[0][start//TILE]+dq[1][start//TILE])*scale
    sum_ref[...]=jnp.broadcast_to(jnp.sum(grad_ref[...],axis=0,keepdims=True),sum_ref.shape)

def attend(seq_len,qkv,*earlier):
    rows,cols=qkv.shape
    pairs=cols//(3*PAIR)
    block=lambda w: pl.BlockSpec((rows,w),lambda j:(0,j))
    return pl.pallas_call(
        attend_kernel,
        grid=(pairs,),
        in_specs=[pl.BlockSpec(memory_space=pltpu.SMEM),block(3*PAIR)]
        +[pl.BlockSpec(memory_space=pl.ANY)]*len(earlier),
        out_specs=[block(PAIR),block(PAIR)],
        out_shape=[jax.ShapeDtypeStruct((rows,pairs*PAIR),f32)]*2,
        compiler_params=pltpu.CompilerParams(vmem_limit_bytes=48*2**20),
        cost_estimate=pl.CostEstimate(flops=0,bytes_accessed=0,transcendentals=0),
        name="attend",
    )(seq_len,qkv,*earlier)

def attend_back(seq_len,qkv,d_out,out,lse,*earlier):
    rows,cols=qkv.shape
    pairs=cols//(3*PAIR)
    block=lambda w: pl.BlockSpec((rows,w),lambda j:(0,j))
    return pl.pallas_call(
        attend_back_kernel,
        grid=(pairs,),
        in_specs=[pl.BlockSpec(memory_space=pltpu.SMEM),block(3*PAIR),block(PAIR),block(PAIR),block(PAIR)]
        +[pl.BlockSpec(memory_space=pl.ANY)]*len(earlier),
        out_specs=[block(3*PAIR),pl.BlockSpec((8,3*PAIR),lambda j:(0,j))],
        out_shape=[jax.ShapeDtypeStruct((rows,cols),f32),jax.ShapeDtypeStruct((8,cols),f32)],
        compiler_params=pltpu.CompilerParams(vmem_limit_bytes=48*2**20),
        cost_estimate=pl.CostEstimate(flops=0,bytes_accessed=0,transcendentals=0),
        name="attend_back",
    )(seq_len,qkv,d_out,out,lse,*earlier)


COLUMNS = 4
CUT = 3


def table(move):
    pairs = []
    for z in range(COLUMNS):
        for x in range(2):
            for core in range(2):
                for y in range(2):
                    there = move(z, x, core, y)
                    number = lambda p: ((p[0] * 2 + p[1]) * 2 + p[2]) * 2 + p[3]
                    pairs.append((number((z, x, core, y)), number(there)))
    return pairs


over_core = table(lambda z, x, core, y: (z, x, 1 - core, y))
over_x = table(lambda z, x, core, y: (z, 1 - x, core, y))
over_y = table(lambda z, x, core, y: (z, x, core, 1 - y))
over_z = [None] + [
    table(lambda z, x, core, y, k=k: (z ^ k, x, core, y)) for k in range(1, COLUMNS)
]


def swap(values, pairs):
    return lax.ppermute(values, AXES, pairs)


def place():
    dp = lax.axis_index("dp")
    return dp // 4, (dp // 2) % 2, dp % 2, lax.axis_index("seq")


def pick(values, index, axis):
    return lax.dynamic_index_in_dim(values, index, axis, keepdims=False)


def order_kernel(*refs):
    pass


def after(values, *earlier):
    anywhere = pl.BlockSpec(memory_space=pl.ANY)
    return pl.pallas_call(
        order_kernel,
        in_specs=[anywhere] * (1 + len(earlier)),
        out_specs=anywhere,
        out_shape=jax.ShapeDtypeStruct(values.shape, values.dtype),
        input_output_aliases={0: 0},
        cost_estimate=pl.CostEstimate(flops=0, bytes_accessed=0, transcendentals=0),
        name="after",
    )(values, *earlier)


def assemble_kernel(plan, place_ref, *refs):
    count, copies_of = plan
    pieces, outs, sems = refs[:count], refs[count:-1], refs[-1]
    mine = [place_ref[i] for i in range(4)]
    copies = []
    for piece, source, out, shift, axes in copies_of:
        slot = tuple(mine[axis] ^ move for axis, move in zip(axes, shift))
        copies.append(
            pltpu.make_async_copy(
                pieces[piece].at[source], outs[out].at[slot], sems.at[len(copies)]
            )
        )
    for copy in copies:
        copy.start()
    for copy in copies:
        copy.wait()


def assemble(where, pieces, shapes, copies):
    anywhere = pl.BlockSpec(memory_space=pl.ANY)
    whole = pl.BlockSpec(memory_space=pltpu.VMEM)
    size = 4 * sum(functools.reduce(lambda m, n: m * n, shape) for shape in shapes)
    return pl.pallas_call(
        functools.partial(assemble_kernel, (len(pieces), copies)),
        in_specs=[pl.BlockSpec(memory_space=pltpu.SMEM)] + [anywhere] * len(pieces),
        out_specs=[whole] * len(shapes),
        out_shape=[jax.ShapeDtypeStruct(shape, f32) for shape in shapes],
        scratch_shapes=[pltpu.SemaphoreType.DMA((len(copies),))],
        compiler_params=pltpu.CompilerParams(vmem_limit_bytes=size + 4 * 2**20),
        cost_estimate=pl.CostEstimate(flops=0, bytes_accessed=0, transcendentals=0),
        name="assemble",
    )(where, *pieces)


def plane_pieces():
    for k in range(COLUMNS):
        yield 0, k, k, 0, 0
        yield 1, k, k, 1, 0
        yield 2, k, k, 0, 1
        yield 3 + k // CUT, k % CUT, k, 1, 1


def gather_column(shard):
    return jnp.stack([shard] + [swap(shard, over_z[k]) for k in range(1, COLUMNS)])


def gather_sides(own):
    return swap(own, over_x), swap(own, over_y)


def by_core(own, other, core, axis):
    return jnp.where(
        core == 0, jnp.stack([own, other], axis), jnp.stack([other, own], axis)
    )


def local_call(kernel, name, where, arrays, earlier, shapes, scratch=()):
    whole = pl.BlockSpec(memory_space=pltpu.VMEM)
    anywhere = pl.BlockSpec(memory_space=pl.ANY)
    count = len(arrays)

    def call(place_ref, *refs):
        place = [place_ref[i] for i in range(4)]
        kernel(place, *refs[:count], *refs[count + len(earlier) :])

    return pl.pallas_call(
        call,
        in_specs=[pl.BlockSpec(memory_space=pltpu.SMEM)]
        + [whole] * count
        + [anywhere] * len(earlier),
        out_specs=[whole] * len(shapes),
        out_shape=[jax.ShapeDtypeStruct(shape, f32) for shape in shapes],
        scratch_shapes=[pltpu.VMEM(shape, f32) for shape in scratch],
        compiler_params=pltpu.CompilerParams(vmem_limit_bytes=30 * 2**20),
        cost_estimate=pl.CostEstimate(flops=0, bytes_accessed=0, transcendentals=0),
        name=name,
    )(where, *arrays, *earlier)


def lanes_of_up(part):
    return slice(D + part * 2 * D, D + (part + 1) * 2 * D)


def put_block(chip, place, target, at, z, x, y, *added):
    def total(value, lanes):
        for ref, index in added:
            value = value + (ref[index] if lanes is None else ref[index + (slice(None), lanes)])
        return value

    if len(chip) == 1:
        target[at] = total(chip[0][z, x, y], None)
        return
    up, out, arrived = chip
    rows = (slice(None),)
    target[at + rows + (slice(0, D),)] = total(
        out[z, x, place[2], y] + arrived[z, x, y], slice(0, D)
    )
    for c in range(2):
        target[at + rows + (lanes_of_up(c),)] = total(up[z, x, c, y], lanes_of_up(c))


def plane_first(where, chip, block, cut, earlier=()):
    def kernel(place, *refs):
        chip_refs, (to_x, to_y) = refs[:-2], refs[-2:]
        z, x, core, y = place
        for other in range(2):
            for row in range(cut):
                put_block(chip_refs, place, to_x, (row, other), row, 1 - x, other)
            for row in range(cut, COLUMNS):
                put_block(chip_refs, place, to_y, (row - cut, other), row, other, 1 - y)

    shapes = [(cut, 2) + block, (COLUMNS - cut, 2) + block]
    return local_call(kernel, "plane_first", where, chip, earlier, shapes)


def plane_second(where, chip, block, from_x, from_y, cut, earlier=()):
    def kernel(place, *refs):
        chip_refs = refs[:-5]
        from_x, from_y, kept, to_y, to_x = refs[-5:]
        z, x, core, y = place
        for row in range(cut):
            put_block(chip_refs, place, to_y, (row,), row, x, 1 - y, (from_x, (row, 1 - y)))
            put_block(chip_refs, place, kept, (row,), row, x, y, (from_x, (row, y)))
        for row in range(cut, COLUMNS):
            low = row - cut
            put_block(chip_refs, place, to_x, (low,), row, 1 - x, y, (from_y, (low, 1 - x)))
            put_block(chip_refs, place, kept, (row,), row, x, y, (from_y, (low, x)))

    return local_call(
        kernel,
        "plane_second",
        where,
        list(chip) + [from_x, from_y],
        earlier,
        [(COLUMNS,) + block, (cut,) + block, (COLUMNS - cut,) + block],
    )


def column_first(where, block, kept, from_y, from_x, cut, earlier=()):
    def kernel(place, kept, from_y, from_x, *refs):
        z, outs, column = place[0], refs[:-1], refs[-1]
        for row in range(cut):
            column[row] = kept[row] + from_y[row]
        for row in range(cut, COLUMNS):
            column[row] = kept[row] + from_x[row - cut]
        for k in range(COLUMNS):
            outs[k % 2][k // 2] = column[z ^ k]

    return local_call(
        kernel,
        "column_first",
        where,
        [kept, from_y, from_x],
        earlier,
        [(2,) + block] * 2,
        [(COLUMNS,) + block],
    )


def column_second(where, pair, arrived, earlier=()):
    def kernel(place, pair, arrived, own, sent):
        own[...] = pair[0] + arrived[0]
        sent[...] = pair[1] + arrived[1]

    block = pair.shape[1:]
    return local_call(
        kernel, "column_second", where, [pair, arrived], earlier, [block] * 2
    )


def sum_after(where, own, arrived, earlier):
    def kernel(place, own, arrived, out):
        out[...] = own[...] + arrived[...]

    return local_call(kernel, "sum_after", where, [own, arrived], earlier, [own.shape])[0]


def zero_after(where, *earlier):
    def kernel(place, zero):
        zero[...] = jnp.zeros_like(zero)

    zero, = local_call(kernel, "zero_after", where, [], earlier, [(8, PAIR)])
    return zero[0, 0]


def copy_after(where, values, earlier):
    def kernel(place, values, out):
        out[...] = values[...]

    return local_call(kernel, "copy_after", where, [values], earlier, [values.shape])[0]


def gather_pair(where, shard, earlier=()):
    def kernel(place, shard, beside, out):
        out[0] = shard[...]
        out[1] = beside[...]

    return local_call(
        kernel, "pair", where, [shard, swap(shard, over_z[2])], earlier, [(2,) + shard.shape]
    )[0]


def gather_pairs(where, pair, earlier):
    beside = swap(pair, over_z[1])

    def kernel(place, pair, beside, out):
        for k in range(COLUMNS):
            out[k] = (pair, beside)[k % 2][k // 2]

    shapes = [(COLUMNS,) + pair.shape[1:]]
    return local_call(kernel, "pairs", where, [pair, beside], earlier, shapes)[0]


def normalise(values):
    centred = values - jnp.mean(values, axis=1, keepdims=True)
    inv_std = lax.rsqrt(jnp.mean(centred * centred, axis=1, keepdims=True) + eps_norm)
    return centred * inv_std, inv_std


def body_grid(
    layer_input,
    cotangent,
    seq_lengths,
    qkv_weight,
    qv_bias,
    out_weight,
    out_bias,
    first_gain,
    first_shift,
    up_weight,
    up_bias,
    down_weight,
    down_bias,
    second_gain,
    second_shift,
):
    z, x, core, y = place()
    where = jnp.stack([z, x, core, y]).astype(jnp.int32)
    rows = layer_input.shape[0]
    shard = qkv_weight.shape[0]
    half = D // 2
    pairs = half // PAIR
    wide = 3 * half
    hidden = 2 * D

    def both_rows(own, other):
        return jnp.where(
            y == 0, jnp.concatenate([own, other]), jnp.concatenate([other, own])
        )

    def rows_of(values, part):
        return lax.dynamic_slice_in_dim(values, part * rows, rows, 0)

    normed_own, inv_one = normalise(layer_input)
    other_normed = swap(normed_own, over_y)
    other_cotangent = swap(cotangent, over_core)

    by_head = qkv_weight.reshape(shard, 3, 2, pairs, PAIR).transpose(2, 0, 3, 1, 4)
    by_head = by_head.reshape(2, shard, wide)
    line_one = jnp.concatenate([qv_bias, out_bias, first_gain, first_shift])
    line_two = jnp.concatenate([up_bias, down_bias])
    line_three = jnp.concatenate([second_gain, second_shift])
    lines = jnp.stack(
        [jnp.pad(line, (0, PAIR - line.shape[0])) for line in (line_one, line_two, line_three)]
    )
    small = jnp.pad(lines, ((0, shard - 3), (0, 0)))
    sent = swap(jnp.concatenate([pick(by_head, 1 - y, 0), small], axis=1), over_y)
    kept = jnp.concatenate([pick(by_head, y, 0), small], axis=1)
    block = jnp.where(y == 0, jnp.stack([kept, sent]), jnp.stack([sent, kept]))
    column = gather_column(after(block, normed_own))
    beside = swap(column, over_x)

    by_unit = up_weight.reshape(shard, 2 * COLUMNS, 2, 8 * shard).transpose(2, 0, 1, 3)
    by_unit = by_unit.reshape(2, shard, hidden)
    kept_up = pick(by_unit, core, 0)
    arrived_up = swap(pick(by_unit, 1 - core, 0), over_core)
    both_up = by_core(kept_up, arrived_up, core, 1).reshape(shard, 2 * hidden)
    shard_a = after(jnp.concatenate([out_weight, both_up], axis=1), column)
    pair_a = gather_pair(where, shard_a)
    shard_b = after(down_weight, pair_a)
    own_a = gather_pairs(where, pair_a, [beside])
    sides_a = gather_sides(own_a)

    pieces = [column, beside]
    pieces += [swap(column, over_core), swap(copy_after(where, beside, [other_normed, own_a]), over_core)]
    copies = []
    for k in range(COLUMNS):
        for piece in range(4):
            shift = (k, piece % 2, piece // 2)
            copies.append((piece, (k, slice(None), slice(None), slice(0, wide)), 0, shift, (0, 1, 2)))
            copies.append(
                (piece, (k, slice(None), slice(0, 8), slice(wide, wide + PAIR)), 1, shift, (0, 1, 2))
            )
    grid = (COLUMNS, 2, 2, 2)
    w_qkv, lines = assemble(
        where, pieces, [grid + (shard, wide), grid + (8, PAIR)], copies
    )
    pair_b = gather_pair(where, shard_b, [w_qkv])
    w_qkv = w_qkv.reshape(D, wide)
    lines = lines.reshape(32, 8, PAIR)
    b_qv = lines[:, 0, : 2 * shard].reshape(2 * D)
    b_out = lines[:, 0, 2 * shard : 3 * shard].reshape(D)
    gain_one = lines[:, 0, 3 * shard : 4 * shard].reshape(D)
    shift_one = lines[:, 0, 4 * shard : 5 * shard].reshape(D)
    b_up = lines[:, 1, : 4 * shard].reshape(2 * COLUMNS, 2, 2, 4 * shard)
    b_up = pick(b_up, core, 1).reshape(hidden)
    b_down = lines[:, 1, 4 * shard : 5 * shard].reshape(D)
    gain_two = lines[:, 2, :shard].reshape(D)
    shift_two = lines[:, 2, shard : 2 * shard].reshape(D)

    normed_one = both_rows(normed_own, other_normed)
    normed_out_one = normed_one * gain_one + shift_one
    bias = pick(b_qv.reshape(2, 2, pairs, PAIR), y, 1)
    qkv_bias = jnp.stack([bias[0], jnp.zeros_like(bias[0]), bias[1]], axis=1).reshape(wide)
    projected = matmul(normed_out_one, w_qkv) + qkv_bias
    own_b = gather_pairs(where, pair_b, [projected])
    sides_b = gather_sides(own_b)
    head_out, log_sum = attend(seq_lengths, projected, own_b)
    there = swap(rows_of(head_out, 1 - y), over_y)
    here = rows_of(head_out, y)
    attended = jnp.where(
        y == 0, jnp.concatenate([here, there], 1), jnp.concatenate([there, here], 1)
    )


    def corner_first(place, beside_y, out):
        out[...] = beside_y[:CUT]

    def corner_rest(place, x_of_a, x_of_b, y_of_b, y_corner_a, x_corner_b, y_corner_b):
        y_corner_a[...] = x_of_a[CUT:]
        x_corner_b[...] = y_of_b[:CUT]
        y_corner_b[...] = x_of_b[CUT:]

    low, high = (CUT,), (COLUMNS - CUT,)
    block_a, block_b = own_a.shape[1:], own_b.shape[1:]
    x_corner_a, = local_call(
        corner_first, "corner_first", where, [sides_a[1]], [head_out], [low + block_a]
    )
    y_corner_a, x_corner_b, y_corner_b = local_call(
        corner_rest, "corner_rest", where, [sides_a[0], *sides_b], [there],
        [high + block_a, low + block_b, high + block_b],
    )
    corners_a = swap(x_corner_a, over_x), swap(y_corner_a, over_y)
    corners_b = swap(x_corner_b, over_x), swap(y_corner_b, over_y)
    every = slice(None)
    copies = []
    for piece, at, dz, dx, dy in plane_pieces():
        copies.append((piece, (at, every, slice(0, D)), 0, (dz, dx, dy), (0, 1, 3)))
    w_out_half, = assemble(
        where, [own_a, *sides_a, *corners_a], [(COLUMNS, 2, 2, shard, D)], copies
    )
    copies = []
    for piece, at, dz, dx, dy in plane_pieces():
        for c in range(2):
            cols = slice(D + c * hidden, D + (c + 1) * hidden)
            copies.append((piece, (at, every, cols), c, (dz, dx, dy), (0, 1, 3)))
    w_up_parts = assemble(
        where, [own_a, *sides_a, *corners_a], [(COLUMNS, 2, 2, shard, hidden)] * 2, copies
    )
    copies = []
    for piece, at, dz, dx, dy in plane_pieces():
        copies.append((piece, (at,), 0, (dz, dx, dy), (0, 1, 3)))
    w_down, = assemble(
        where, [own_b, *sides_b, *corners_b], [(COLUMNS, 2, 2, 4 * shard, D)], copies
    )
    w_out = by_core(w_out_half, swap(w_out_half, over_core), core, 2).reshape(D, D)
    w_up = jnp.stack(w_up_parts, axis=2).reshape(D, hidden)
    w_down = w_down.reshape(hidden, D)

    middle = layer_input + matmul(attended, w_out) + b_out
    normed_out_two, normed_two, inv_two = norm_forward(middle, gain_two, shift_two)
    both_normed = jnp.concatenate([normed_out_two, swap(normed_out_two, over_core)])
    both_cotangent = jnp.concatenate([cotangent, other_cotangent])
    raw_act = matmul(both_normed, w_up)
    pre_act = raw_act + b_up
    activ = gelu_forward(pre_act)

    d_down_b = jnp.sum(cotangent, axis=0)
    d_down_w = matmul_tn(activ, both_cotangent)
    chip_b = d_down_w.reshape(COLUMNS, 2, 2, 4 * shard, D)
    d_pre = matmul_nt(both_cotangent, w_down) * gelu_slope(pre_act)
    d_up_b = jnp.sum(d_pre, axis=0)
    d_part = matmul_nt(d_pre, w_up)
    d_norm_two, d_gain_two, d_shift_two = norm_backward(
        d_part[:rows] + swap(d_part[rows:], over_core), normed_two, inv_two, gain_two
    )
    d_middle = cotangent + d_norm_two
    d_out_b = jnp.sum(d_middle, axis=0)
    d_att = matmul_nt(d_middle, w_out)
    d_heads = d_att.reshape(rows, 2, half)
    sent = pick(d_heads, 1 - y, 1)
    d_up_b = d_up_b.reshape(2 * COLUMNS, 8 * shard)
    d_up_b = by_core(d_up_b, jnp.zeros_like(d_up_b), core, 1)

    def lanes(*vectors):
        line = jnp.concatenate([v.reshape(32, -1) for v in vectors], axis=1)
        return jnp.pad(line, ((0, 0), (0, PAIR - line.shape[1])))

    small = jnp.stack(
        [lanes(d_out_b, d_gain_two, d_shift_two), lanes(d_up_b, d_down_b)],
        axis=1,
    )
    grid = (COLUMNS, 2, 2, 2)
    scales = jnp.stack([gain_one, shift_one], axis=1).reshape(grid + (shard, 2))
    small = jnp.pad(small, ((0, 0), (0, 6), (0, 0)))
    chip_a = matmul_tn(both_normed + zero_after(where, sent, small, scales), d_pre).reshape(COLUMNS, 2, 2, 2, shard, hidden)
    def join_rows(place, own, arrived, out):
        y = place[3]
        out[pl.ds(y * rows, rows)] = own[...]
        out[pl.ds((1 - y) * rows, rows)] = arrived[...]

    d_out, = local_call(
        join_rows, "join_rows", where, [pick(d_heads, y, 1), swap(sent, over_y)],
        [chip_a], [(2 * rows, half)],
    )
    block_b = (4 * shard, D)
    block_a = (shard, 5 * D)
    to_x, to_y = plane_first(where, [chip_b], block_b, CUT)
    side_b = swap(to_x, over_x), swap(to_y, over_y)
    d_out_w = matmul_tn(attended, d_middle).reshape(COLUMNS, 2, 2, 2, shard, D)
    chip_a = [chip_a, d_out_w, swap(pick(d_out_w, 1 - core, 2), over_core)]
    kept_b, *sent_b = plane_second(where, [chip_b], block_b, *side_b, CUT, [d_out])
    first_a = plane_first(where, chip_a, block_a, 2, sent_b)
    side_a = swap(first_a[0], over_x), swap(first_a[1], over_y)

    d_proj, d_bias_all = attend_back(
        seq_lengths, projected, d_out, head_out, log_sum, *first_a, *sent_b
    )
    corner = swap(sent_b[0], over_y), swap(sent_b[1], over_x)
    pair_b, sent_b = column_first(where, block_b, kept_b, *corner, CUT, [d_proj])
    kept_a, *sent_a = plane_second(where, chip_a, block_a, *side_a, 2, [sent_b])
    corner_a = swap(sent_a[0], over_y), swap(sent_a[1], over_x)

    moved = matmul_tn(normed_one + zero_after(where, *sent_a), d_proj)
    last_lane = wide + PAIR - 1

    def finish(place, moved, weight, scales, total, small, kept, sent):
        core = place[2]
        y = place[3]
        total = total[:1]
        for z in range(COLUMNS):
            for xy in range(4):
                for target, c in ((kept, core), (sent, 1 - core)):
                    at = (z, xy // 2, c, xy % 2)
                    to = (z, xy // 2, xy % 2)
                    rows_of_grad, rows_of_weight = moved[at], weight[at]
                    scale = scales[at]
                    target[to + (slice(None), slice(0, wide))] = (
                        rows_of_grad * scale[:, 0:1] + scale[:, 1:2] * total
                    )
                    gain_grad = jnp.sum(rows_of_grad * rows_of_weight, axis=1, keepdims=True)
                    shift_grad = jnp.sum(total * rows_of_weight, axis=1, keepdims=True)
                    lane = lax.broadcasted_iota(jnp.int32, (shard, PAIR), 1)
                    side = jnp.where(lane == PAIR - 1, gain_grad, 0.0)
                    side = jnp.where(lane == PAIR - 2, shift_grad, side)
                    lines = jnp.concatenate(
                        [small[at], jnp.zeros((shard - 8, PAIR), f32)], axis=0
                    )
                    target[to + (slice(None), slice(wide, wide + PAIR))] = side + lines

        line = slice(wide, wide + 2 * shard)
        for part, z in ((0, y), (2, 2 + y)):
            column = jnp.concatenate(
                [total[:, (3 * p + part) * PAIR : (3 * p + part + 1) * PAIR] for p in range(pairs)],
                axis=1,
            )
            for xy in range(4):
                x, side = xy // 2, xy % 2
                low = column[:, 2 * shard * (4 * x + side) :][:, : 2 * shard]
                high = column[:, 2 * shard * (4 * x + 2 + side) :][:, : 2 * shard]
                kept[z, x, side, 2:3, line] = jnp.where(core == 0, low, high)
                sent[z, x, side, 2:3, line] = jnp.where(core == 0, high, low)

    block = (shard, wide + PAIR)
    kept, first = local_call(
        finish,
        "finish",
        where,
        [
            moved.reshape(grid + (shard, wide)),
            w_qkv.reshape(grid + (shard, wide)),
            scales,
            d_bias_all,
            small.reshape(grid + (8, PAIR)),
        ],
        (),
        [(COLUMNS, 2, 2) + block] * 2,
    )

    def chip_sum(place, kept, arrived, mine, sent):
        x = place[1]
        for z in range(COLUMNS):
            mine[z] = kept[z, x] + arrived[z, x]
            sent[z] = kept[z, 1 - x] + arrived[z, 1 - x]

    kept, second = local_call(
        chip_sum,
        "chip_sum",
        where,
        [kept, swap(first, over_core)],
        (),
        [(COLUMNS, 2) + block] * 2,
    )
    own_b, sent_b = column_second(where, pair_b, swap(sent_b, over_z[1]), [second])
    pair_a, sent_a = column_first(where, block_a, kept_a, *corner_a, 2, [sent_b])
    d_norm = matmul_nt(d_proj + zero_after(where, sent_a), w_qkv)
    d_norm_sent = rows_of(d_norm, 1 - y)

    def line_sum(place, kept, arrived, pair, sent):
        z = place[0]
        for k in range(COLUMNS):
            (pair, sent)[k % 2][k // 2] = kept[z ^ k] + arrived[z ^ k]

    pair_qkv, sent_qkv = local_call(
        line_sum, "line_sum", where, [kept, swap(second, over_x)], [d_norm],
        [(2, 2) + block] * 2,
    )
    own_a, sent_a = column_second(where, pair_a, swap(sent_a, over_z[1]), [sent_qkv])
    down_part = matmul(gelu_forward(raw_act + (b_up + zero_after(where, sent_a))), w_down)
    layer_output = middle + down_part[:rows] + swap(down_part[rows:], over_core) + b_down
    own_qkv, sent_qkv = column_second(
        where, pair_qkv, swap(sent_qkv, over_z[1]), [down_part]
    )
    down_grad = sum_after(where, own_b, swap(sent_b, over_z[2]), [sent_qkv])
    grad_a = sum_after(where, own_a, swap(sent_a, over_z[2]), [sent_qkv])

    def last_sum(place, own, arrived, here, sent):
        y = place[3]
        here[...] = own[y] + arrived[y]
        sent[...] = own[1 - y] + arrived[1 - y]

    here, third = local_call(
        last_sum, "last_sum", where, [own_qkv, swap(sent_qkv, over_z[2])], (), [block] * 2
    )
    there = swap(third, over_y)
    out_grad = grad_a[:, :D]
    up_parts = jnp.stack([grad_a[:, lanes_of_up(0)], grad_a[:, lanes_of_up(1)]])
    arrived = swap(pick(up_parts, 1 - core, 0), over_core)
    up_grad = by_core(
        pick(up_parts, core, 0).reshape(shard, 2 * COLUMNS, 8 * shard),
        arrived.reshape(shard, 2 * COLUMNS, 8 * shard),
        core,
        2,
    ).reshape(shard, 4 * D)


    def place_qkv(place, here, there, grad, side):
        y = place[3]
        side[...] = here[:, wide:] + there[:, wide:]
        for part in range(3):
            for p in range(pairs):
                source = slice((3 * p + part) * PAIR, (3 * p + part + 1) * PAIR)
                mine, other = here[:, source], there[:, source]
                target = part * D + p * PAIR
                grad[:, target : target + PAIR] = jnp.where(y == 0, mine, other)
                target = target + half
                grad[:, target : target + PAIR] = jnp.where(y == 0, other, mine)

    qkv_grad, side = local_call(
        place_qkv, "place_qkv", where, [here, there], [up_grad, down_grad, layer_output], [(shard, 3 * D), (shard, PAIR)]
    )
    d_norm_own = rows_of(d_norm, y) + swap(d_norm_sent, over_y)
    d_norm_one, unused, unused = norm_backward(
        d_norm_own, normed_own, inv_one, gain_one
    )
    input_grad = d_middle + d_norm_one
    return (
        layer_output,
        input_grad,
        qkv_grad,
        side[2, : 2 * shard],
        out_grad,
        side[0, :shard],
        side[:, PAIR - 1],
        side[:, PAIR - 2],
        up_grad,
        side[1, : 4 * shard],
        down_grad,
        side[1, 4 * shard : 5 * shard],
        side[0, shard : 2 * shard],
        side[0, 2 * shard : 3 * shard],
    )


def solution(mesh):
    shape = (mesh.shape["dp"], mesh.shape["seq"])
    body = body_grid if shape == (COLUMNS * 4, 2) else body_general
    row = P(AXES, None)
    vec = P(AXES)
    return jax.shard_map(
        body,
        mesh=mesh,
        in_specs=(row, row, P("dp"), row, vec, row, vec, vec, vec, row, vec, row, vec, vec, vec),
        out_specs=(row, row, row, vec, row, vec, vec, vec, row, vec, row, vec, vec, vec),
        check_vma=False,
    )
```

```python
import functools

import jax
import jax.numpy as jnp
from jax import lax
from jax.experimental import pallas as pl
from jax.experimental.pallas import tpu as pltpu
from jax.sharding import PartitionSpec as P

D = 768
HEADS = 12
HEAD_DIM = 64
PAIR = 2 * HEAD_DIM
TILE = 256
AXES = ("dp", "seq")

eps_norm = 1e-05
neg_big = -1e30
top_prec = lax.Precision.HIGH
f32 = jnp.float32
bf16 = jnp.bfloat16


def matmul(left, right):
    return jnp.dot(left, right, precision=top_prec, preferred_element_type=jnp.float32)


def matmul_tn(left, right):
    return lax.dot_general(
        left,
        right,
        (((0,), (0,)), ((), ())),
        precision=top_prec,
        preferred_element_type=jnp.float32,
    )


def matmul_nt(left, right):
    return lax.dot_general(
        left,
        right,
        (((1,), (1,)), ((), ())),
        precision=top_prec,
        preferred_element_type=jnp.float32,
    )


def norm_forward(values, gain, shift):
    centred = values - jnp.mean(values, axis=1, keepdims=True)
    inv_std = lax.rsqrt(jnp.mean(centred * centred, axis=1, keepdims=True) + eps_norm)
    normed = centred * inv_std
    return (normed * gain + shift, normed, inv_std)


def norm_backward(upstream, normed, inv_std, gain):
    scaled = upstream * gain
    inner = (
        scaled
        - jnp.mean(scaled, axis=1, keepdims=True)
        - normed * jnp.mean(scaled * normed, axis=1, keepdims=True)
    )
    return (inner * inv_std, jnp.sum(upstream * normed, axis=0), jnp.sum(upstream, axis=0))


def split_heads(values):
    return values.reshape(values.shape[0], HEADS, HEAD_DIM).transpose(1, 0, 2)


def join_heads(values):
    return values.transpose(1, 0, 2).reshape(values.shape[1], HEADS * HEAD_DIM)


def gelu_forward(values):
    return 0.5 * values * (1.0 + lax.erf(values * 0.7071067811865476))


def gelu_slope(values):
    cdf_part = 0.5 * (1.0 + lax.erf(values * 0.7071067811865476))
    return cdf_part + values * jnp.exp(-0.5 * values * values) * 0.3989422804014327


def body_general(
    layer_input,
    cotangent,
    seq_lengths,
    qkv_weight,
    qv_bias,
    out_weight,
    out_bias,
    first_gain,
    first_shift,
    up_weight,
    up_bias,
    down_weight,
    down_bias,
    second_gain,
    second_shift,
):
    gathered = (
        lax.all_gather(qkv_weight, ("dp", "seq"), axis=0, tiled=True),
        lax.all_gather(qv_bias, ("dp", "seq"), axis=0, tiled=True),
        lax.all_gather(out_weight, ("dp", "seq"), axis=0, tiled=True),
        lax.all_gather(out_bias, ("dp", "seq"), axis=0, tiled=True),
        lax.all_gather(first_gain, ("dp", "seq"), axis=0, tiled=True),
        lax.all_gather(first_shift, ("dp", "seq"), axis=0, tiled=True),
        lax.all_gather(up_weight, ("dp", "seq"), axis=0, tiled=True),
        lax.all_gather(up_bias, ("dp", "seq"), axis=0, tiled=True),
        lax.all_gather(down_weight, ("dp", "seq"), axis=0, tiled=True),
        lax.all_gather(down_bias, ("dp", "seq"), axis=0, tiled=True),
        lax.all_gather(second_gain, ("dp", "seq"), axis=0, tiled=True),
        lax.all_gather(second_shift, ("dp", "seq"), axis=0, tiled=True),
    )
    (
        w_qkv,
        b_qv,
        w_out,
        b_out,
        gain_one,
        shift_one,
        w_up,
        b_up,
        w_down,
        b_down,
        gain_two,
        shift_two,
    ) = gathered
    tok_rows = layer_input.shape[0]
    group_rows = tok_rows * lax.axis_size("seq")
    score_scale = HEAD_DIM ** (-0.5)
    seq_len = seq_lengths[0]
    first_own = lax.axis_index("seq") * tok_rows
    query_pos = first_own + jnp.arange(tok_rows, dtype=jnp.int32)
    last_query = first_own + tok_rows - 1

    def segment_of(positions):
        return jnp.where(positions < seq_len, 0, positions + 1)

    query_seg = segment_of(query_pos)

    def key_mask(key_pos):
        return (segment_of(key_pos)[None, :] == query_seg[:, None]) & (
            key_pos[None, :] <= query_pos[:, None]
        )

    normed_out_one, normed_one, inv_one = norm_forward(layer_input, gain_one, shift_one)
    qkv_bias = jnp.concatenate([b_qv[:D], jnp.zeros((D,), jnp.float32), b_qv[D:]])
    projected = matmul(normed_out_one, w_qkv) + qkv_bias
    queries = projected[:, :D]
    keys_local = projected[:, D : 2 * D]
    values_local = projected[:, 2 * D :]
    query_heads = split_heads(queries)
    start_state = (
        jnp.full((HEADS, tok_rows), neg_big, jnp.float32),
        jnp.zeros((HEADS, tok_rows), jnp.float32),
        jnp.zeros((HEADS, tok_rows, HEAD_DIM), jnp.float32),
    )
    key_piece = lax.all_gather(keys_local, "seq", axis=0, tiled=True)
    value_piece = lax.all_gather(values_local, "seq", axis=0, tiled=True)

    def compute_block(state_in):
        key_pos = jnp.arange(key_piece.shape[0], dtype=jnp.int32)
        allowed = key_mask(key_pos)
        key_heads = split_heads(key_piece)
        value_heads = split_heads(value_piece)

        def one_head(ignored, head_item):
            q_head, k_head, v_head, old_max, old_sum, old_acc = head_item
            scores = jnp.where(allowed, matmul_nt(q_head, k_head) * score_scale, neg_big)
            new_max = jnp.maximum(old_max, jnp.max(scores, axis=1))
            weights_soft = jnp.where(allowed, jnp.exp(scores - new_max[:, None]), 0.0)
            decay_old = jnp.exp(old_max - new_max)
            new_sum = old_sum * decay_old + jnp.sum(weights_soft, axis=1)
            new_acc = old_acc * decay_old[:, None] + matmul(weights_soft, v_head)
            return (ignored, (new_max, new_sum, new_acc))

        unused, updated = lax.scan(
            one_head,
            jnp.zeros((), jnp.float32),
            (query_heads, key_heads, value_heads, state_in[0], state_in[1], state_in[2]),
        )
        return updated

    def keep_block(state_in):
        return (state_in[0], state_in[1], state_in[2])

    run_max, run_sum, run_acc = lax.cond(
        jnp.int32(0) > last_query, keep_block, compute_block, start_state
    )
    head_out = run_acc / run_sum[:, :, None]
    log_sum = run_max + jnp.log(run_sum)
    attended = join_heads(head_out)
    middle = layer_input + matmul(attended, w_out) + b_out
    normed_out_two, normed_two, inv_two = norm_forward(middle, gain_two, shift_two)
    pre_act = matmul(normed_out_two, w_up) + b_up
    activ = gelu_forward(pre_act)
    layer_output = middle + matmul(activ, w_down) + b_down
    d_down_b = jnp.sum(cotangent, axis=0)
    d_down_w = matmul_tn(activ, cotangent)
    d_pre = matmul_nt(cotangent, w_down) * gelu_slope(pre_act)
    d_up_b = jnp.sum(d_pre, axis=0)
    d_up_w = matmul_tn(normed_out_two, d_pre)
    d_norm_two, d_gain_two, d_shift_two = norm_backward(
        matmul_nt(d_pre, w_up), normed_two, inv_two, gain_two
    )
    d_middle = cotangent + d_norm_two
    d_out_b = jnp.sum(d_middle, axis=0)
    d_out_w = matmul_tn(attended, d_middle)
    d_att = matmul_nt(d_middle, w_out)
    dout_heads = split_heads(d_att)
    delta_heads = jnp.sum(dout_heads * head_out, axis=2)
    key_all, value_all = (
        lax.all_gather(keys_local, "seq", axis=0, tiled=True),
        lax.all_gather(values_local, "seq", axis=0, tiled=True),
    )
    allowed_all = key_mask(jnp.arange(group_rows, dtype=jnp.int32))

    def back_head(ignored, head_item):
        q_head, k_head, v_head, do_head, lse_head, delta_head = head_item
        scores = jnp.where(allowed_all, matmul_nt(q_head, k_head) * score_scale, neg_big)
        weights_soft = jnp.where(allowed_all, jnp.exp(scores - lse_head[:, None]), 0.0)
        dv_head = matmul_tn(weights_soft, do_head)
        d_soft = matmul_nt(do_head, v_head)
        d_scores = weights_soft * (d_soft - delta_head[:, None]) * score_scale
        return (ignored, (matmul(d_scores, k_head), matmul_tn(d_scores, q_head), dv_head))

    unused, head_grads = lax.scan(
        back_head,
        jnp.zeros((), jnp.float32),
        (
            query_heads,
            split_heads(key_all),
            split_heads(value_all),
            dout_heads,
            log_sum,
            delta_heads,
        ),
    )
    d_query = join_heads(head_grads[0])
    key_terms = join_heads(head_grads[1])
    value_terms = join_heads(head_grads[2])
    d_key, d_value = (
        lax.psum_scatter(key_terms, "seq", scatter_dimension=0, tiled=True),
        lax.psum_scatter(value_terms, "seq", scatter_dimension=0, tiled=True),
    )
    d_proj = jnp.concatenate([d_query, d_key, d_value], axis=1)
    d_qv_b = jnp.concatenate([jnp.sum(d_query, axis=0), jnp.sum(d_value, axis=0)])
    d_qkv_w = matmul_tn(normed_out_one, d_proj)
    d_norm_one, d_gain_one, d_shift_one = norm_backward(
        matmul_nt(d_proj, w_qkv), normed_one, inv_one, gain_one
    )
    input_grad = d_middle + d_norm_one
    summed = (
        lax.psum_scatter(d_qkv_w, ("dp", "seq"), scatter_dimension=0, tiled=True),
        lax.psum_scatter(d_qv_b, ("dp", "seq"), scatter_dimension=0, tiled=True),
        lax.psum_scatter(d_out_w, ("dp", "seq"), scatter_dimension=0, tiled=True),
        lax.psum_scatter(d_out_b, ("dp", "seq"), scatter_dimension=0, tiled=True),
        lax.psum_scatter(d_gain_one, ("dp", "seq"), scatter_dimension=0, tiled=True),
        lax.psum_scatter(d_shift_one, ("dp", "seq"), scatter_dimension=0, tiled=True),
        lax.psum_scatter(d_up_w, ("dp", "seq"), scatter_dimension=0, tiled=True),
        lax.psum_scatter(d_up_b, ("dp", "seq"), scatter_dimension=0, tiled=True),
        lax.psum_scatter(d_down_w, ("dp", "seq"), scatter_dimension=0, tiled=True),
        lax.psum_scatter(d_down_b, ("dp", "seq"), scatter_dimension=0, tiled=True),
        lax.psum_scatter(d_gain_two, ("dp", "seq"), scatter_dimension=0, tiled=True),
        lax.psum_scatter(d_shift_two, ("dp", "seq"), scatter_dimension=0, tiled=True),
    )
    return (
        layer_output,
        input_grad,
        summed[0],
        summed[1],
        summed[2],
        summed[3],
        summed[4],
        summed[5],
        summed[6],
        summed[7],
        summed[8],
        summed[9],
        summed[10],
        summed[11],
    )


def split(v):
    high=v.astype(bf16)
    return high,(v-high.astype(f32)).astype(bf16)

def dot_nn(a,b):
    return lax.dot_general(a,b,(((1,),(0,)),((),())),preferred_element_type=f32)
def dot_nt(a,b):
    return lax.dot_general(a,b,(((1,),(1,)),((),())),preferred_element_type=f32)
def dot_tn(a,b):
    return lax.dot_general(a,b,(((0,),(0,)),((),())),preferred_element_type=f32)

def fold(v):
    return v[:,:PAIR]+v[:,PAIR:]

def attend_kernel(len_ref,qkv_ref,*refs):
    out_ref,lse_ref=refs[-2:]
    rows=qkv_ref.shape[0]
    seq_len=len_ref[0]
    lane=lax.broadcasted_iota(jnp.int32,(1,PAIR),1)
    q_high,q_low=split(qkv_ref[:,:PAIR]*(HEAD_DIM**-0.5))
    q_both=jnp.concatenate([q_high,q_low],axis=1)
    v_high,v_low=split(qkv_ref[:,2*PAIR:])
    v_both=jnp.concatenate([v_high,v_low],axis=1)
    k_all=qkv_ref[:,PAIR:2*PAIR]
    k_parts=[]
    for head in range(2):
        kh,kl=split(jnp.where(lane//HEAD_DIM==head,k_all,0.0))
        k_parts.append((jnp.concatenate([kh,kh],axis=1),kl))
    for start in range(0,rows,TILE):
        stop=start+TILE
        q_pos=start+lax.broadcasted_iota(jnp.int32,(TILE,1),0)
        first=jnp.where(q_pos<seq_len,0,q_pos)
        k_pos=lax.broadcasted_iota(jnp.int32,(1,stop),1)
        allowed=(k_pos>=first)&(k_pos<=q_pos)
        outs,lses=[],[]
        for head in range(2):
            kd,kl=k_parts[head]
            scores=dot_nt(q_both[start:stop],kd[:stop])+dot_nt(q_high[start:stop],kl[:stop])
            scores=jnp.where(allowed,scores,neg_big)
            top=jnp.max(scores,axis=1,keepdims=True)
            probs=jnp.exp(scores-top)
            total=jnp.sum(probs,axis=1,keepdims=True)
            ph,pw=split(probs)
            acc=fold(dot_nn(ph,v_both[:stop]))+dot_nn(pw,v_high[:stop])
            outs.append(acc*(1.0/total))
            lses.append(jnp.broadcast_to(top+jnp.log(total),(TILE,PAIR)))
        out_ref[start:stop]=jnp.where(lane<HEAD_DIM,outs[0],outs[1])
        lse_ref[start:stop]=jnp.where(lane<HEAD_DIM,lses[0],lses[1])

def attend_back_kernel(len_ref,qkv_ref,do_ref,out_ref,lse_ref,*refs):
    grad_ref,sum_ref=refs[-2:]
    rows=qkv_ref.shape[0]
    seq_len=len_ref[0]
    lane=lax.broadcasted_iota(jnp.int32,(1,PAIR),1)
    scale=HEAD_DIM**-0.5
    q_high,q_low=split(qkv_ref[:,:PAIR]*scale)
    q_both=jnp.concatenate([q_high,q_low],axis=1)
    q_twice=jnp.concatenate([q_high,q_high],axis=1)
    do_all=do_ref[...]
    do_high,do_low=split(do_all)
    do_both=jnp.concatenate([do_high,do_low],axis=1)
    do_twice=jnp.concatenate([do_high,do_high],axis=1)
    delta_t=jnp.transpose(do_all*out_ref[...])
    lse_t=jnp.transpose(lse_ref[...])
    dq=[[jnp.zeros((TILE,PAIR),f32) for _ in range(rows//TILE)] for _ in range(2)]
    for start in range(0,rows,TILE):
        stop=start+TILE
        n=rows-start
        k_pos=start+lax.broadcasted_iota(jnp.int32,(TILE,1),0)
        q_pos=start+lax.broadcasted_iota(jnp.int32,(1,n),1)
        first=jnp.where(q_pos<seq_len,0,q_pos)
        allowed=(k_pos>=first)&(k_pos<=q_pos)
        k_all=qkv_ref[start:stop,PAIR:2*PAIR]
        v_all=qkv_ref[start:stop,2*PAIR:]
        k_grads,v_grads=[],[]
        for head in range(2):
            mine=lane//HEAD_DIM==head
            kh,kl=split(jnp.where(mine,k_all,0.0))
            vh,vl=split(jnp.where(mine,v_all,0.0))
            k_both=jnp.concatenate([kh,kl],axis=1)
            v_both=jnp.concatenate([vh,vl],axis=1)
            scores=dot_nt(k_both,q_twice[start:])+dot_nt(kh,q_low[start:])
            lse_row=lse_t[head*HEAD_DIM:head*HEAD_DIM+1,start:]
            probs=jnp.where(allowed,jnp.exp(scores-lse_row),0.0)
            ph,pw=split(probs)
            v_grads.append(fold(dot_nn(ph,do_both[start:]))+dot_nn(pw,do_high[start:]))
            d_probs=dot_nt(v_both,do_twice[start:])+dot_nt(vh,do_low[start:])
            delta_row=jnp.sum(delta_t[head*HEAD_DIM:(head+1)*HEAD_DIM,start:],axis=0,keepdims=True)
            d_scores=probs*(d_probs-delta_row)
            sh,sl=split(d_scores)
            k_grads.append(fold(dot_nn(sh,q_both[start:]))+dot_nn(sl,q_high[start:]))
            part=fold(dot_tn(sh,k_both))+dot_tn(sl,kh)
            for t in range(n//TILE):
                dq[head][start//TILE+t]+=part[t*TILE:(t+1)*TILE]
        grad_ref[start:stop,PAIR:2*PAIR]=jnp.where(lane<HEAD_DIM,k_grads[0],k_grads[1])
        grad_ref[start:stop,2*PAIR:]=jnp.where(lane<HEAD_DIM,v_grads[0],v_grads[1])
        grad_ref[start:stop,:PAIR]=(dq[0][start//TILE]+dq[1][start//TILE])*scale
    sum_ref[...]=jnp.broadcast_to(jnp.sum(grad_ref[...],axis=0,keepdims=True),sum_ref.shape)

def attend(seq_len,qkv,*earlier):
    rows,cols=qkv.shape
    pairs=cols//(3*PAIR)
    block=lambda w: pl.BlockSpec((rows,w),lambda j:(0,j))
    return pl.pallas_call(
        attend_kernel,
        grid=(pairs,),
        in_specs=[pl.BlockSpec(memory_space=pltpu.SMEM),block(3*PAIR)]
        +[pl.BlockSpec(memory_space=pl.ANY)]*len(earlier),
        out_specs=[block(PAIR),block(PAIR)],
        out_shape=[jax.ShapeDtypeStruct((rows,pairs*PAIR),f32)]*2,
        compiler_params=pltpu.CompilerParams(vmem_limit_bytes=48*2**20),
        cost_estimate=pl.CostEstimate(flops=0,bytes_accessed=0,transcendentals=0),
        name="attend",
    )(seq_len,qkv,*earlier)

def attend_back(seq_len,qkv,d_out,out,lse,*earlier):
    rows,cols=qkv.shape
    pairs=cols//(3*PAIR)
    block=lambda w: pl.BlockSpec((rows,w),lambda j:(0,j))
    return pl.pallas_call(
        attend_back_kernel,
        grid=(pairs,),
        in_specs=[pl.BlockSpec(memory_space=pltpu.SMEM),block(3*PAIR),block(PAIR),block(PAIR),block(PAIR)]
        +[pl.BlockSpec(memory_space=pl.ANY)]*len(earlier),
        out_specs=[block(3*PAIR),pl.BlockSpec((8,3*PAIR),lambda j:(0,j))],
        out_shape=[jax.ShapeDtypeStruct((rows,cols),f32),jax.ShapeDtypeStruct((8,cols),f32)],
        compiler_params=pltpu.CompilerParams(vmem_limit_bytes=48*2**20),
        cost_estimate=pl.CostEstimate(flops=0,bytes_accessed=0,transcendentals=0),
        name="attend_back",
    )(seq_len,qkv,d_out,out,lse,*earlier)


COLUMNS = 4
CUT = 3


def table(move):
    pairs = []
    for z in range(COLUMNS):
        for x in range(2):
            for core in range(2):
                for y in range(2):
                    there = move(z, x, core, y)
                    number = lambda p: ((p[0] * 2 + p[1]) * 2 + p[2]) * 2 + p[3]
                    pairs.append((number((z, x, core, y)), number(there)))
    return pairs


over_core = table(lambda z, x, core, y: (z, x, 1 - core, y))
over_x = table(lambda z, x, core, y: (z, 1 - x, core, y))
over_y = table(lambda z, x, core, y: (z, x, core, 1 - y))
over_z = [None] + [
    table(lambda z, x, core, y, k=k: (z ^ k, x, core, y)) for k in range(1, COLUMNS)
]


def swap(values, pairs):
    return lax.ppermute(values, AXES, pairs)


def place():
    dp = lax.axis_index("dp")
    return dp // 4, (dp // 2) % 2, dp % 2, lax.axis_index("seq")


def pick(values, index, axis):
    return lax.dynamic_index_in_dim(values, index, axis, keepdims=False)


def order_kernel(*refs):
    pass


def after(values, *earlier):
    anywhere = pl.BlockSpec(memory_space=pl.ANY)
    return pl.pallas_call(
        order_kernel,
        in_specs=[anywhere] * (1 + len(earlier)),
        out_specs=anywhere,
        out_shape=jax.ShapeDtypeStruct(values.shape, values.dtype),
        input_output_aliases={0: 0},
        cost_estimate=pl.CostEstimate(flops=0, bytes_accessed=0, transcendentals=0),
        name="after",
    )(values, *earlier)


def assemble_kernel(plan, place_ref, *refs):
    count, copies_of = plan
    pieces, outs, sems = refs[:count], refs[count:-1], refs[-1]
    mine = [place_ref[i] for i in range(4)]
    copies = []
    for piece, source, out, shift, axes in copies_of:
        slot = tuple(mine[axis] ^ move for axis, move in zip(axes, shift))
        copies.append(
            pltpu.make_async_copy(
                pieces[piece].at[source], outs[out].at[slot], sems.at[len(copies)]
            )
        )
    for copy in copies:
        copy.start()
    for copy in copies:
        copy.wait()


def assemble(where, pieces, shapes, copies):
    anywhere = pl.BlockSpec(memory_space=pl.ANY)
    whole = pl.BlockSpec(memory_space=pltpu.VMEM)
    size = 4 * sum(functools.reduce(lambda m, n: m * n, shape) for shape in shapes)
    return pl.pallas_call(
        functools.partial(assemble_kernel, (len(pieces), copies)),
        in_specs=[pl.BlockSpec(memory_space=pltpu.SMEM)] + [anywhere] * len(pieces),
        out_specs=[whole] * len(shapes),
        out_shape=[jax.ShapeDtypeStruct(shape, f32) for shape in shapes],
        scratch_shapes=[pltpu.SemaphoreType.DMA((len(copies),))],
        compiler_params=pltpu.CompilerParams(vmem_limit_bytes=size + 4 * 2**20),
        cost_estimate=pl.CostEstimate(flops=0, bytes_accessed=0, transcendentals=0),
        name="assemble",
    )(where, *pieces)


def plane_pieces():
    for k in range(COLUMNS):
        yield 0, k, k, 0, 0
        yield 1, k, k, 1, 0
        yield 2, k, k, 0, 1
        yield 3 + k // CUT, k % CUT, k, 1, 1


def gather_column(shard):
    return jnp.stack([shard] + [swap(shard, over_z[k]) for k in range(1, COLUMNS)])


def gather_sides(own):
    return swap(own, over_x), swap(own, over_y)


def by_core(own, other, core, axis):
    return jnp.where(
        core == 0, jnp.stack([own, other], axis), jnp.stack([other, own], axis)
    )


def local_call(kernel, name, where, arrays, earlier, shapes, scratch=()):
    whole = pl.BlockSpec(memory_space=pltpu.VMEM)
    anywhere = pl.BlockSpec(memory_space=pl.ANY)
    count = len(arrays)

    def call(place_ref, *refs):
        place = [place_ref[i] for i in range(4)]
        kernel(place, *refs[:count], *refs[count + len(earlier) :])

    return pl.pallas_call(
        call,
        in_specs=[pl.BlockSpec(memory_space=pltpu.SMEM)]
        + [whole] * count
        + [anywhere] * len(earlier),
        out_specs=[whole] * len(shapes),
        out_shape=[jax.ShapeDtypeStruct(shape, f32) for shape in shapes],
        scratch_shapes=[pltpu.VMEM(shape, f32) for shape in scratch],
        compiler_params=pltpu.CompilerParams(vmem_limit_bytes=30 * 2**20),
        cost_estimate=pl.CostEstimate(flops=0, bytes_accessed=0, transcendentals=0),
        name=name,
    )(where, *arrays, *earlier)


def lanes_of_up(part):
    return slice(D + part * 2 * D, D + (part + 1) * 2 * D)


def put_block(chip, place, target, at, z, x, y, *added):
    def total(value, lanes):
        for ref, index in added:
            value = value + (ref[index] if lanes is None else ref[index + (slice(None), lanes)])
        return value

    if len(chip) == 1:
        target[at] = total(chip[0][z, x, y], None)
        return
    up, out, arrived = chip
    rows = (slice(None),)
    target[at + rows + (slice(0, D),)] = total(
        out[z, x, place[2], y] + arrived[z, x, y], slice(0, D)
    )
    for c in range(2):
        target[at + rows + (lanes_of_up(c),)] = total(up[z, x, c, y], lanes_of_up(c))


def plane_first(where, chip, block, cut, earlier=()):
    def kernel(place, *refs):
        chip_refs, (to_x, to_y) = refs[:-2], refs[-2:]
        z, x, core, y = place
        for other in range(2):
            for row in range(cut):
                put_block(chip_refs, place, to_x, (row, other), row, 1 - x, other)
            for row in range(cut, COLUMNS):
                put_block(chip_refs, place, to_y, (row - cut, other), row, other, 1 - y)

    shapes = [(cut, 2) + block, (COLUMNS - cut, 2) + block]
    return local_call(kernel, "plane_first", where, chip, earlier, shapes)


def plane_second(where, chip, block, from_x, from_y, cut, earlier=()):
    def kernel(place, *refs):
        chip_refs = refs[:-5]
        from_x, from_y, kept, to_y, to_x = refs[-5:]
        z, x, core, y = place
        for row in range(cut):
            put_block(chip_refs, place, to_y, (row,), row, x, 1 - y, (from_x, (row, 1 - y)))
            put_block(chip_refs, place, kept, (row,), row, x, y, (from_x, (row, y)))
        for row in range(cut, COLUMNS):
            low = row - cut
            put_block(chip_refs, place, to_x, (low,), row, 1 - x, y, (from_y, (low, 1 - x)))
            put_block(chip_refs, place, kept, (row,), row, x, y, (from_y, (low, x)))

    return local_call(
        kernel,
        "plane_second",
        where,
        list(chip) + [from_x, from_y],
        earlier,
        [(COLUMNS,) + block, (cut,) + block, (COLUMNS - cut,) + block],
    )


def column_first(where, block, kept, from_y, from_x, cut, earlier=()):
    def kernel(place, kept, from_y, from_x, *refs):
        z, outs, column = place[0], refs[:-1], refs[-1]
        for row in range(cut):
            column[row] = kept[row] + from_y[row]
        for row in range(cut, COLUMNS):
            column[row] = kept[row] + from_x[row - cut]
        for k in range(COLUMNS):
            outs[k % 2][k // 2] = column[z ^ k]

    return local_call(
        kernel,
        "column_first",
        where,
        [kept, from_y, from_x],
        earlier,
        [(2,) + block] * 2,
        [(COLUMNS,) + block],
    )


def column_second(where, pair, arrived, earlier=()):
    def kernel(place, pair, arrived, own, sent):
        own[...] = pair[0] + arrived[0]
        sent[...] = pair[1] + arrived[1]

    block = pair.shape[1:]
    return local_call(
        kernel, "column_second", where, [pair, arrived], earlier, [block] * 2
    )


def sum_after(where, own, arrived, earlier):
    def kernel(place, own, arrived, out):
        out[...] = own[...] + arrived[...]

    return local_call(kernel, "sum_after", where, [own, arrived], earlier, [own.shape])[0]


def zero_after(where, *earlier):
    def kernel(place, zero):
        zero[...] = jnp.zeros_like(zero)

    zero, = local_call(kernel, "zero_after", where, [], earlier, [(8, PAIR)])
    return zero[0, 0]


def copy_after(where, values, earlier):
    def kernel(place, values, out):
        out[...] = values[...]

    return local_call(kernel, "copy_after", where, [values], earlier, [values.shape])[0]


def gather_pair(where, shard, earlier=()):
    def kernel(place, shard, beside, out):
        out[0] = shard[...]
        out[1] = beside[...]

    return local_call(
        kernel, "pair", where, [shard, swap(shard, over_z[2])], earlier, [(2,) + shard.shape]
    )[0]


def gather_pairs(where, pair, earlier):
    beside = swap(pair, over_z[1])

    def kernel(place, pair, beside, out):
        for k in range(COLUMNS):
            out[k] = (pair, beside)[k % 2][k // 2]

    shapes = [(COLUMNS,) + pair.shape[1:]]
    return local_call(kernel, "pairs", where, [pair, beside], earlier, shapes)[0]


def normalise(values):
    centred = values - jnp.mean(values, axis=1, keepdims=True)
    inv_std = lax.rsqrt(jnp.mean(centred * centred, axis=1, keepdims=True) + eps_norm)
    return centred * inv_std, inv_std


def body_grid(
    layer_input,
    cotangent,
    seq_lengths,
    qkv_weight,
    qv_bias,
    out_weight,
    out_bias,
    first_gain,
    first_shift,
    up_weight,
    up_bias,
    down_weight,
    down_bias,
    second_gain,
    second_shift,
):
    z, x, core, y = place()
    where = jnp.stack([z, x, core, y]).astype(jnp.int32)
    rows = layer_input.shape[0]
    shard = qkv_weight.shape[0]
    half = D // 2
    pairs = half // PAIR
    wide = 3 * half
    hidden = 2 * D

    def both_rows(own, other):
        return jnp.where(
            y == 0, jnp.concatenate([own, other]), jnp.concatenate([other, own])
        )

    def rows_of(values, part):
        return lax.dynamic_slice_in_dim(values, part * rows, rows, 0)

    normed_own, inv_one = normalise(layer_input)
    other_normed = swap(normed_own, over_y)
    other_cotangent = swap(cotangent, over_core)

    by_head = qkv_weight.reshape(shard, 3, 2, pairs, PAIR).transpose(2, 0, 3, 1, 4)
    by_head = by_head.reshape(2, shard, wide)
    line_one = jnp.concatenate([qv_bias, out_bias, first_gain, first_shift])
    line_two = jnp.concatenate([up_bias, down_bias])
    line_three = jnp.concatenate([second_gain, second_shift])
    lines = jnp.stack(
        [jnp.pad(line, (0, PAIR - line.shape[0])) for line in (line_one, line_two, line_three)]
    )
    small = jnp.pad(lines, ((0, shard - 3), (0, 0)))
    sent = swap(jnp.concatenate([pick(by_head, 1 - y, 0), small], axis=1), over_y)
    kept = jnp.concatenate([pick(by_head, y, 0), small], axis=1)
    block = jnp.where(y == 0, jnp.stack([kept, sent]), jnp.stack([sent, kept]))
    column = gather_column(after(block, normed_own))
    beside = swap(column, over_x)

    by_unit = up_weight.reshape(shard, 2 * COLUMNS, 2, 8 * shard).transpose(2, 0, 1, 3)
    by_unit = by_unit.reshape(2, shard, hidden)
    kept_up = pick(by_unit, core, 0)
    arrived_up = swap(pick(by_unit, 1 - core, 0), over_core)
    both_up = by_core(kept_up, arrived_up, core, 1).reshape(shard, 2 * hidden)
    shard_a = after(jnp.concatenate([out_weight, both_up], axis=1), column)
    pair_a = gather_pair(where, shard_a)
    shard_b = after(down_weight, pair_a)
    own_a = gather_pairs(where, pair_a, [beside])
    sides_a = gather_sides(own_a)

    pieces = [column, beside]
    pieces += [swap(column, over_core), swap(copy_after(where, beside, [other_normed, own_a]), over_core)]
    copies = []
    for k in range(COLUMNS):
        for piece in range(4):
            shift = (k, piece % 2, piece // 2)
            copies.append((piece, (k, slice(None), slice(None), slice(0, wide)), 0, shift, (0, 1, 2)))
            copies.append(
                (piece, (k, slice(None), slice(0, 8), slice(wide, wide + PAIR)), 1, shift, (0, 1, 2))
            )
    grid = (COLUMNS, 2, 2, 2)
    w_qkv, lines = assemble(
        where, pieces, [grid + (shard, wide), grid + (8, PAIR)], copies
    )
    pair_b = gather_pair(where, shard_b, [w_qkv])
    w_qkv = w_qkv.reshape(D, wide)
    lines = lines.reshape(32, 8, PAIR)
    b_qv = lines[:, 0, : 2 * shard].reshape(2 * D)
    b_out = lines[:, 0, 2 * shard : 3 * shard].reshape(D)
    gain_one = lines[:, 0, 3 * shard : 4 * shard].reshape(D)
    shift_one = lines[:, 0, 4 * shard : 5 * shard].reshape(D)
    b_up = lines[:, 1, : 4 * shard].reshape(2 * COLUMNS, 2, 2, 4 * shard)
    b_up = pick(b_up, core, 1).reshape(hidden)
    b_down = lines[:, 1, 4 * shard : 5 * shard].reshape(D)
    gain_two = lines[:, 2, :shard].reshape(D)
    shift_two = lines[:, 2, shard : 2 * shard].reshape(D)

    normed_one = both_rows(normed_own, other_normed)
    normed_out_one = normed_one * gain_one + shift_one
    bias = pick(b_qv.reshape(2, 2, pairs, PAIR), y, 1)
    qkv_bias = jnp.stack([bias[0], jnp.zeros_like(bias[0]), bias[1]], axis=1).reshape(wide)
    projected = matmul(normed_out_one, w_qkv) + qkv_bias
    own_b = gather_pairs(where, pair_b, [projected])
    sides_b = gather_sides(own_b)
    head_out, log_sum = attend(seq_lengths, projected, own_b)
    there = swap(rows_of(head_out, 1 - y), over_y)
    here = rows_of(head_out, y)
    attended = jnp.where(
        y == 0, jnp.concatenate([here, there], 1), jnp.concatenate([there, here], 1)
    )


    def corner_first(place, beside_y, out):
        out[...] = beside_y[:CUT]

    def corner_rest(place, x_of_a, x_of_b, y_of_b, y_corner_a, x_corner_b, y_corner_b):
        y_corner_a[...] = x_of_a[CUT:]
        x_corner_b[...] = y_of_b[:CUT]
        y_corner_b[...] = x_of_b[CUT:]

    grid = (COLUMNS, 2, 2, 2)
    scales = jnp.stack([gain_one, shift_one], axis=1).reshape(grid + (shard, 2))
    low, high = (CUT,), (COLUMNS - CUT,)
    block_a, block_b = own_a.shape[1:], own_b.shape[1:]
    x_corner_a, = local_call(
        corner_first, "corner_first", where, [sides_a[1]], [head_out], [low + block_a]
    )
    y_corner_a, x_corner_b, y_corner_b = local_call(
        corner_rest, "corner_rest", where, [sides_a[0], *sides_b], [there, scales],
        [high + block_a, low + block_b, high + block_b],
    )
    corners_a = swap(x_corner_a, over_x), swap(y_corner_a, over_y)
    corners_b = swap(x_corner_b, over_x), swap(y_corner_b, over_y)
    every = slice(None)
    copies = []
    for piece, at, dz, dx, dy in plane_pieces():
        copies.append((piece, (at, every, slice(0, D)), 0, (dz, dx, dy), (0, 1, 3)))
    w_out_half, = assemble(
        where, [own_a, *sides_a, *corners_a], [(COLUMNS, 2, 2, shard, D)], copies
    )
    copies = []
    for piece, at, dz, dx, dy in plane_pieces():
        for c in range(2):
            cols = slice(D + c * hidden, D + (c + 1) * hidden)
            copies.append((piece, (at, every, cols), c, (dz, dx, dy), (0, 1, 3)))
    w_up_parts = assemble(
        where, [own_a, *sides_a, *corners_a], [(COLUMNS, 2, 2, shard, hidden)] * 2, copies
    )
    copies = []
    for piece, at, dz, dx, dy in plane_pieces():
        copies.append((piece, (at,), 0, (dz, dx, dy), (0, 1, 3)))
    w_down, = assemble(
        where, [own_b, *sides_b, *corners_b], [(COLUMNS, 2, 2, 4 * shard, D)], copies
    )
    w_out = by_core(w_out_half, swap(w_out_half, over_core), core, 2).reshape(D, D)
    w_up = jnp.stack(w_up_parts, axis=2).reshape(D, hidden)
    w_down = w_down.reshape(hidden, D)

    middle = layer_input + matmul(attended, w_out) + b_out
    normed_out_two, normed_two, inv_two = norm_forward(middle, gain_two, shift_two)
    both_normed = jnp.concatenate([normed_out_two, swap(normed_out_two, over_core)])
    both_cotangent = jnp.concatenate([cotangent, other_cotangent])
    raw_act = matmul(both_normed, w_up)
    pre_act = raw_act + b_up
    activ = gelu_forward(pre_act)

    d_down_b = jnp.sum(cotangent, axis=0)
    d_down_w = matmul_tn(activ, both_cotangent)
    chip_b = d_down_w.reshape(COLUMNS, 2, 2, 4 * shard, D)
    d_pre = matmul_nt(both_cotangent, w_down) * gelu_slope(pre_act)
    d_up_b = jnp.sum(d_pre, axis=0)
    d_part = matmul_nt(d_pre, w_up)
    d_norm_two, d_gain_two, d_shift_two = norm_backward(
        d_part[:rows] + swap(d_part[rows:], over_core), normed_two, inv_two, gain_two
    )
    d_middle = cotangent + d_norm_two
    d_out_b = jnp.sum(d_middle, axis=0)
    d_att = matmul_nt(d_middle, w_out)
    d_heads = d_att.reshape(rows, 2, half)
    sent = pick(d_heads, 1 - y, 1)
    d_up_b = d_up_b.reshape(2 * COLUMNS, 8 * shard)
    d_up_b = by_core(d_up_b, jnp.zeros_like(d_up_b), core, 1)

    def lanes(*vectors):
        line = jnp.concatenate([v.reshape(32, -1) for v in vectors], axis=1)
        return jnp.pad(line, ((0, 0), (0, PAIR - line.shape[1])))

    small = jnp.stack(
        [lanes(d_out_b, d_gain_two, d_shift_two), lanes(d_up_b, d_down_b)],
        axis=1,
    )
    small = jnp.pad(small, ((0, 0), (0, 6), (0, 0)))
    chip_a = matmul_tn(both_normed + zero_after(where, sent, small), d_pre).reshape(COLUMNS, 2, 2, 2, shard, hidden)
    def join_rows(place, own, arrived, out):
        y = place[3]
        out[pl.ds(y * rows, rows)] = own[...]
        out[pl.ds((1 - y) * rows, rows)] = arrived[...]

    d_out, = local_call(
        join_rows, "join_rows", where, [pick(d_heads, y, 1), swap(sent, over_y)],
        [chip_a], [(2 * rows, half)],
    )
    block_b = (4 * shard, D)
    block_a = (shard, 5 * D)
    to_x, to_y = plane_first(where, [chip_b], block_b, 2)
    side_b = swap(to_x, over_x), swap(to_y, over_y)
    d_out_w = matmul_tn(attended, d_middle).reshape(COLUMNS, 2, 2, 2, shard, D)
    chip_a = [chip_a, d_out_w, swap(pick(d_out_w, 1 - core, 2), over_core)]
    kept_b, *sent_b = plane_second(where, [chip_b], block_b, *side_b, 2, [d_out])
    first_a = plane_first(where, chip_a, block_a, 2, sent_b)
    side_a = swap(first_a[0], over_x), swap(first_a[1], over_y)

    d_proj, d_bias_all = attend_back(
        seq_lengths, projected, d_out, head_out, log_sum, *first_a, *sent_b
    )
    corner = swap(sent_b[0], over_y), swap(sent_b[1], over_x)
    pair_b, sent_b = column_first(where, block_b, kept_b, *corner, 2, [d_proj])
    kept_a, *sent_a = plane_second(where, chip_a, block_a, *side_a, 2, [sent_b])
    corner_a = swap(sent_a[0], over_y), swap(sent_a[1], over_x)

    moved = matmul_tn(normed_one + zero_after(where, *sent_a), d_proj)
    own_b, sent_b = column_second(where, pair_b, swap(sent_b, over_z[1]), [moved])
    pair_a, sent_a = column_first(where, block_a, kept_a, *corner_a, 2, [sent_b])
    last_lane = wide + PAIR - 1

    def finish(place, moved, weight, scales, total, small, kept, sent):
        core = place[2]
        y = place[3]
        total = total[:1]
        for z in range(COLUMNS):
            for xy in range(4):
                for target, c in ((kept, core), (sent, 1 - core)):
                    at = (z, xy // 2, c, xy % 2)
                    to = (z, xy // 2, xy % 2)
                    rows_of_grad, rows_of_weight = moved[at], weight[at]
                    scale = scales[at]
                    target[to + (slice(None), slice(0, wide))] = (
                        rows_of_grad * scale[:, 0:1] + scale[:, 1:2] * total
                    )
                    gain_grad = jnp.sum(rows_of_grad * rows_of_weight, axis=1, keepdims=True)
                    shift_grad = jnp.sum(total * rows_of_weight, axis=1, keepdims=True)
                    lane = lax.broadcasted_iota(jnp.int32, (shard, PAIR), 1)
                    side = jnp.where(lane == PAIR - 1, gain_grad, 0.0)
                    side = jnp.where(lane == PAIR - 2, shift_grad, side)
                    lines = jnp.concatenate(
                        [small[at], jnp.zeros((shard - 8, PAIR), f32)], axis=0
                    )
                    target[to + (slice(None), slice(wide, wide + PAIR))] = side + lines

        line = slice(wide, wide + 2 * shard)
        for part, z in ((0, y), (2, 2 + y)):
            column = jnp.concatenate(
                [total[:, (3 * p + part) * PAIR : (3 * p + part + 1) * PAIR] for p in range(pairs)],
                axis=1,
            )
            for xy in range(4):
                x, side = xy // 2, xy % 2
                low = column[:, 2 * shard * (4 * x + side) :][:, : 2 * shard]
                high = column[:, 2 * shard * (4 * x + 2 + side) :][:, : 2 * shard]
                kept[z, x, side, 2:3, line] = jnp.where(core == 0, low, high)
                sent[z, x, side, 2:3, line] = jnp.where(core == 0, high, low)

    block = (shard, wide + PAIR)
    kept, first = local_call(
        finish,
        "finish",
        where,
        [
            moved.reshape(grid + (shard, wide)),
            w_qkv.reshape(grid + (shard, wide)),
            scales,
            d_bias_all,
            small.reshape(grid + (8, PAIR)),
        ],
        [sent_a],
        [(COLUMNS, 2, 2) + block] * 2,
    )

    def chip_sum(place, kept, arrived, mine, sent):
        x = place[1]
        for z in range(COLUMNS):
            mine[z] = kept[z, x] + arrived[z, x]
            sent[z] = kept[z, 1 - x] + arrived[z, 1 - x]

    kept, second = local_call(
        chip_sum,
        "chip_sum",
        where,
        [kept, swap(first, over_core)],
        (),
        [(COLUMNS, 2) + block] * 2,
    )
    d_norm = matmul_nt(d_proj + zero_after(where, second), w_qkv)
    d_norm_sent = rows_of(d_norm, 1 - y)

    def line_sum(place, kept, arrived, pair, sent):
        z = place[0]
        for k in range(COLUMNS):
            (pair, sent)[k % 2][k // 2] = kept[z ^ k] + arrived[z ^ k]

    pair_qkv, sent_qkv = local_call(
        line_sum, "line_sum", where, [kept, swap(second, over_x)], [d_norm],
        [(2, 2) + block] * 2,
    )
    own_a, sent_a = column_second(where, pair_a, swap(sent_a, over_z[1]), [sent_qkv])
    down_part = matmul(gelu_forward(raw_act + (b_up + zero_after(where, sent_a))), w_down)
    layer_output = middle + down_part[:rows] + swap(down_part[rows:], over_core) + b_down
    own_qkv, sent_qkv = column_second(
        where, pair_qkv, swap(sent_qkv, over_z[1]), [down_part]
    )
    down_grad = sum_after(where, own_b, swap(sent_b, over_z[2]), [sent_qkv])
    grad_a = sum_after(where, own_a, swap(sent_a, over_z[2]), [sent_qkv])

    def last_sum(place, own, arrived, here, sent):
        y = place[3]
        here[...] = own[y] + arrived[y]
        sent[...] = own[1 - y] + arrived[1 - y]

    here, third = local_call(
        last_sum, "last_sum", where, [own_qkv, swap(sent_qkv, over_z[2])], (), [block] * 2
    )
    there = swap(third, over_y)
    out_grad = grad_a[:, :D]
    up_parts = jnp.stack([grad_a[:, lanes_of_up(0)], grad_a[:, lanes_of_up(1)]])
    arrived = swap(pick(up_parts, 1 - core, 0), over_core)
    up_grad = by_core(
        pick(up_parts, core, 0).reshape(shard, 2 * COLUMNS, 8 * shard),
        arrived.reshape(shard, 2 * COLUMNS, 8 * shard),
        core,
        2,
    ).reshape(shard, 4 * D)


    def place_qkv(place, here, there, grad, side):
        y = place[3]
        side[...] = here[:, wide:] + there[:, wide:]
        for part in range(3):
            for p in range(pairs):
                source = slice((3 * p + part) * PAIR, (3 * p + part + 1) * PAIR)
                mine, other = here[:, source], there[:, source]
                target = part * D + p * PAIR
                grad[:, target : target + PAIR] = jnp.where(y == 0, mine, other)
                target = target + half
                grad[:, target : target + PAIR] = jnp.where(y == 0, other, mine)

    qkv_grad, side = local_call(
        place_qkv, "place_qkv", where, [here, there], [up_grad, down_grad, layer_output], [(shard, 3 * D), (shard, PAIR)]
    )
    d_norm_own = rows_of(d_norm, y) + swap(d_norm_sent, over_y)
    d_norm_one, unused, unused = norm_backward(
        d_norm_own, normed_own, inv_one, gain_one
    )
    input_grad = d_middle + d_norm_one
    return (
        layer_output,
        input_grad,
        qkv_grad,
        side[2, : 2 * shard],
        out_grad,
        side[0, :shard],
        side[:, PAIR - 1],
        side[:, PAIR - 2],
        up_grad,
        side[1, : 4 * shard],
        down_grad,
        side[1, 4 * shard : 5 * shard],
        side[0, shard : 2 * shard],
        side[0, 2 * shard : 3 * shard],
    )


def solution(mesh):
    shape = (mesh.shape["dp"], mesh.shape["seq"])
    body = body_grid if shape == (COLUMNS * 4, 2) else body_general
    row = P(AXES, None)
    vec = P(AXES)
    return jax.shard_map(
        body,
        mesh=mesh,
        in_specs=(row, row, P("dp"), row, vec, row, vec, vec, vec, row, vec, row, vec, vec, vec),
        out_specs=(row, row, row, vec, row, vec, vec, vec, row, vec, row, vec, vec, vec),
        check_vma=False,
    )
```

```python
import functools

import jax
import jax.numpy as jnp
from jax import lax
from jax.experimental import pallas as pl
from jax.experimental.pallas import tpu as pltpu
from jax.sharding import PartitionSpec as P

D = 768
HEADS = 12
HEAD_DIM = 64
PAIR = 2 * HEAD_DIM
TILE = 256
AXES = ("dp", "seq")

eps_norm = 1e-05
neg_big = -1e30
top_prec = lax.Precision.HIGH
f32 = jnp.float32
bf16 = jnp.bfloat16


def matmul(left, right):
    return jnp.dot(left, right, precision=top_prec, preferred_element_type=jnp.float32)


def matmul_tn(left, right):
    return lax.dot_general(
        left,
        right,
        (((0,), (0,)), ((), ())),
        precision=top_prec,
        preferred_element_type=jnp.float32,
    )


def matmul_nt(left, right):
    return lax.dot_general(
        left,
        right,
        (((1,), (1,)), ((), ())),
        precision=top_prec,
        preferred_element_type=jnp.float32,
    )


def norm_forward(values, gain, shift):
    centred = values - jnp.mean(values, axis=1, keepdims=True)
    inv_std = lax.rsqrt(jnp.mean(centred * centred, axis=1, keepdims=True) + eps_norm)
    normed = centred * inv_std
    return (normed * gain + shift, normed, inv_std)


def norm_backward(upstream, normed, inv_std, gain):
    scaled = upstream * gain
    inner = (
        scaled
        - jnp.mean(scaled, axis=1, keepdims=True)
        - normed * jnp.mean(scaled * normed, axis=1, keepdims=True)
    )
    return (inner * inv_std, jnp.sum(upstream * normed, axis=0), jnp.sum(upstream, axis=0))


def split_heads(values):
    return values.reshape(values.shape[0], HEADS, HEAD_DIM).transpose(1, 0, 2)


def join_heads(values):
    return values.transpose(1, 0, 2).reshape(values.shape[1], HEADS * HEAD_DIM)


def gelu_forward(values):
    return 0.5 * values * (1.0 + lax.erf(values * 0.7071067811865476))


def gelu_slope(values):
    cdf_part = 0.5 * (1.0 + lax.erf(values * 0.7071067811865476))
    return cdf_part + values * jnp.exp(-0.5 * values * values) * 0.3989422804014327


def body_general(
    layer_input,
    cotangent,
    seq_lengths,
    qkv_weight,
    qv_bias,
    out_weight,
    out_bias,
    first_gain,
    first_shift,
    up_weight,
    up_bias,
    down_weight,
    down_bias,
    second_gain,
    second_shift,
):
    gathered = (
        lax.all_gather(qkv_weight, ("dp", "seq"), axis=0, tiled=True),
        lax.all_gather(qv_bias, ("dp", "seq"), axis=0, tiled=True),
        lax.all_gather(out_weight, ("dp", "seq"), axis=0, tiled=True),
        lax.all_gather(out_bias, ("dp", "seq"), axis=0, tiled=True),
        lax.all_gather(first_gain, ("dp", "seq"), axis=0, tiled=True),
        lax.all_gather(first_shift, ("dp", "seq"), axis=0, tiled=True),
        lax.all_gather(up_weight, ("dp", "seq"), axis=0, tiled=True),
        lax.all_gather(up_bias, ("dp", "seq"), axis=0, tiled=True),
        lax.all_gather(down_weight, ("dp", "seq"), axis=0, tiled=True),
        lax.all_gather(down_bias, ("dp", "seq"), axis=0, tiled=True),
        lax.all_gather(second_gain, ("dp", "seq"), axis=0, tiled=True),
        lax.all_gather(second_shift, ("dp", "seq"), axis=0, tiled=True),
    )
    (
        w_qkv,
        b_qv,
        w_out,
        b_out,
        gain_one,
        shift_one,
        w_up,
        b_up,
        w_down,
        b_down,
        gain_two,
        shift_two,
    ) = gathered
    tok_rows = layer_input.shape[0]
    group_rows = tok_rows * lax.axis_size("seq")
    score_scale = HEAD_DIM ** (-0.5)
    seq_len = seq_lengths[0]
    first_own = lax.axis_index("seq") * tok_rows
    query_pos = first_own + jnp.arange(tok_rows, dtype=jnp.int32)
    last_query = first_own + tok_rows - 1

    def segment_of(positions):
        return jnp.where(positions < seq_len, 0, positions + 1)

    query_seg = segment_of(query_pos)

    def key_mask(key_pos):
        return (segment_of(key_pos)[None, :] == query_seg[:, None]) & (
            key_pos[None, :] <= query_pos[:, None]
        )

    normed_out_one, normed_one, inv_one = norm_forward(layer_input, gain_one, shift_one)
    qkv_bias = jnp.concatenate([b_qv[:D], jnp.zeros((D,), jnp.float32), b_qv[D:]])
    projected = matmul(normed_out_one, w_qkv) + qkv_bias
    queries = projected[:, :D]
    keys_local = projected[:, D : 2 * D]
    values_local = projected[:, 2 * D :]
    query_heads = split_heads(queries)
    start_state = (
        jnp.full((HEADS, tok_rows), neg_big, jnp.float32),
        jnp.zeros((HEADS, tok_rows), jnp.float32),
        jnp.zeros((HEADS, tok_rows, HEAD_DIM), jnp.float32),
    )
    key_piece = lax.all_gather(keys_local, "seq", axis=0, tiled=True)
    value_piece = lax.all_gather(values_local, "seq", axis=0, tiled=True)

    def compute_block(state_in):
        key_pos = jnp.arange(key_piece.shape[0], dtype=jnp.int32)
        allowed = key_mask(key_pos)
        key_heads = split_heads(key_piece)
        value_heads = split_heads(value_piece)

        def one_head(ignored, head_item):
            q_head, k_head, v_head, old_max, old_sum, old_acc = head_item
            scores = jnp.where(allowed, matmul_nt(q_head, k_head) * score_scale, neg_big)
            new_max = jnp.maximum(old_max, jnp.max(scores, axis=1))
            weights_soft = jnp.where(allowed, jnp.exp(scores - new_max[:, None]), 0.0)
            decay_old = jnp.exp(old_max - new_max)
            new_sum = old_sum * decay_old + jnp.sum(weights_soft, axis=1)
            new_acc = old_acc * decay_old[:, None] + matmul(weights_soft, v_head)
            return (ignored, (new_max, new_sum, new_acc))

        unused, updated = lax.scan(
            one_head,
            jnp.zeros((), jnp.float32),
            (query_heads, key_heads, value_heads, state_in[0], state_in[1], state_in[2]),
        )
        return updated

    def keep_block(state_in):
        return (state_in[0], state_in[1], state_in[2])

    run_max, run_sum, run_acc = lax.cond(
        jnp.int32(0) > last_query, keep_block, compute_block, start_state
    )
    head_out = run_acc / run_sum[:, :, None]
    log_sum = run_max + jnp.log(run_sum)
    attended = join_heads(head_out)
    middle = layer_input + matmul(attended, w_out) + b_out
    normed_out_two, normed_two, inv_two = norm_forward(middle, gain_two, shift_two)
    pre_act = matmul(normed_out_two, w_up) + b_up
    activ = gelu_forward(pre_act)
    layer_output = middle + matmul(activ, w_down) + b_down
    d_down_b = jnp.sum(cotangent, axis=0)
    d_down_w = matmul_tn(activ, cotangent)
    d_pre = matmul_nt(cotangent, w_down) * gelu_slope(pre_act)
    d_up_b = jnp.sum(d_pre, axis=0)
    d_up_w = matmul_tn(normed_out_two, d_pre)
    d_norm_two, d_gain_two, d_shift_two = norm_backward(
        matmul_nt(d_pre, w_up), normed_two, inv_two, gain_two
    )
    d_middle = cotangent + d_norm_two
    d_out_b = jnp.sum(d_middle, axis=0)
    d_out_w = matmul_tn(attended, d_middle)
    d_att = matmul_nt(d_middle, w_out)
    dout_heads = split_heads(d_att)
    delta_heads = jnp.sum(dout_heads * head_out, axis=2)
    key_all, value_all = (
        lax.all_gather(keys_local, "seq", axis=0, tiled=True),
        lax.all_gather(values_local, "seq", axis=0, tiled=True),
    )
    allowed_all = key_mask(jnp.arange(group_rows, dtype=jnp.int32))

    def back_head(ignored, head_item):
        q_head, k_head, v_head, do_head, lse_head, delta_head = head_item
        scores = jnp.where(allowed_all, matmul_nt(q_head, k_head) * score_scale, neg_big)
        weights_soft = jnp.where(allowed_all, jnp.exp(scores - lse_head[:, None]), 0.0)
        dv_head = matmul_tn(weights_soft, do_head)
        d_soft = matmul_nt(do_head, v_head)
        d_scores = weights_soft * (d_soft - delta_head[:, None]) * score_scale
        return (ignored, (matmul(d_scores, k_head), matmul_tn(d_scores, q_head), dv_head))

    unused, head_grads = lax.scan(
        back_head,
        jnp.zeros((), jnp.float32),
        (
            query_heads,
            split_heads(key_all),
            split_heads(value_all),
            dout_heads,
            log_sum,
            delta_heads,
        ),
    )
    d_query = join_heads(head_grads[0])
    key_terms = join_heads(head_grads[1])
    value_terms = join_heads(head_grads[2])
    d_key, d_value = (
        lax.psum_scatter(key_terms, "seq", scatter_dimension=0, tiled=True),
        lax.psum_scatter(value_terms, "seq", scatter_dimension=0, tiled=True),
    )
    d_proj = jnp.concatenate([d_query, d_key, d_value], axis=1)
    d_qv_b = jnp.concatenate([jnp.sum(d_query, axis=0), jnp.sum(d_value, axis=0)])
    d_qkv_w = matmul_tn(normed_out_one, d_proj)
    d_norm_one, d_gain_one, d_shift_one = norm_backward(
        matmul_nt(d_proj, w_qkv), normed_one, inv_one, gain_one
    )
    input_grad = d_middle + d_norm_one
    summed = (
        lax.psum_scatter(d_qkv_w, ("dp", "seq"), scatter_dimension=0, tiled=True),
        lax.psum_scatter(d_qv_b, ("dp", "seq"), scatter_dimension=0, tiled=True),
        lax.psum_scatter(d_out_w, ("dp", "seq"), scatter_dimension=0, tiled=True),
        lax.psum_scatter(d_out_b, ("dp", "seq"), scatter_dimension=0, tiled=True),
        lax.psum_scatter(d_gain_one, ("dp", "seq"), scatter_dimension=0, tiled=True),
        lax.psum_scatter(d_shift_one, ("dp", "seq"), scatter_dimension=0, tiled=True),
        lax.psum_scatter(d_up_w, ("dp", "seq"), scatter_dimension=0, tiled=True),
        lax.psum_scatter(d_up_b, ("dp", "seq"), scatter_dimension=0, tiled=True),
        lax.psum_scatter(d_down_w, ("dp", "seq"), scatter_dimension=0, tiled=True),
        lax.psum_scatter(d_down_b, ("dp", "seq"), scatter_dimension=0, tiled=True),
        lax.psum_scatter(d_gain_two, ("dp", "seq"), scatter_dimension=0, tiled=True),
        lax.psum_scatter(d_shift_two, ("dp", "seq"), scatter_dimension=0, tiled=True),
    )
    return (
        layer_output,
        input_grad,
        summed[0],
        summed[1],
        summed[2],
        summed[3],
        summed[4],
        summed[5],
        summed[6],
        summed[7],
        summed[8],
        summed[9],
        summed[10],
        summed[11],
    )


def split(v):
    high=v.astype(bf16)
    return high,(v-high.astype(f32)).astype(bf16)

def dot_nn(a,b):
    return lax.dot_general(a,b,(((1,),(0,)),((),())),preferred_element_type=f32)
def dot_nt(a,b):
    return lax.dot_general(a,b,(((1,),(1,)),((),())),preferred_element_type=f32)
def dot_tn(a,b):
    return lax.dot_general(a,b,(((0,),(0,)),((),())),preferred_element_type=f32)

def fold(v):
    return v[:,:PAIR]+v[:,PAIR:]

def attend_kernel(len_ref,qkv_ref,*refs):
    out_ref,lse_ref=refs[-2:]
    rows=qkv_ref.shape[0]
    seq_len=len_ref[0]
    lane=lax.broadcasted_iota(jnp.int32,(1,PAIR),1)
    q_high,q_low=split(qkv_ref[:,:PAIR]*(HEAD_DIM**-0.5))
    q_both=jnp.concatenate([q_high,q_low],axis=1)
    v_high,v_low=split(qkv_ref[:,2*PAIR:])
    v_both=jnp.concatenate([v_high,v_low],axis=1)
    k_all=qkv_ref[:,PAIR:2*PAIR]
    k_parts=[]
    for head in range(2):
        kh,kl=split(jnp.where(lane//HEAD_DIM==head,k_all,0.0))
        k_parts.append((jnp.concatenate([kh,kh],axis=1),kl))
    for start in range(0,rows,TILE):
        stop=start+TILE
        q_pos=start+lax.broadcasted_iota(jnp.int32,(TILE,1),0)
        first=jnp.where(q_pos<seq_len,0,q_pos)
        k_pos=lax.broadcasted_iota(jnp.int32,(1,stop),1)
        allowed=(k_pos>=first)&(k_pos<=q_pos)
        outs,lses=[],[]
        for head in range(2):
            kd,kl=k_parts[head]
            scores=dot_nt(q_both[start:stop],kd[:stop])+dot_nt(q_high[start:stop],kl[:stop])
            scores=jnp.where(allowed,scores,neg_big)
            top=jnp.max(scores,axis=1,keepdims=True)
            probs=jnp.exp(scores-top)
            total=jnp.sum(probs,axis=1,keepdims=True)
            ph,pw=split(probs)
            acc=fold(dot_nn(ph,v_both[:stop]))+dot_nn(pw,v_high[:stop])
            outs.append(acc*(1.0/total))
            lses.append(jnp.broadcast_to(top+jnp.log(total),(TILE,PAIR)))
        out_ref[start:stop]=jnp.where(lane<HEAD_DIM,outs[0],outs[1])
        lse_ref[start:stop]=jnp.where(lane<HEAD_DIM,lses[0],lses[1])

def attend_back_kernel(len_ref,qkv_ref,do_ref,out_ref,lse_ref,*refs):
    grad_ref,sum_ref=refs[-2:]
    rows=qkv_ref.shape[0]
    seq_len=len_ref[0]
    lane=lax.broadcasted_iota(jnp.int32,(1,PAIR),1)
    scale=HEAD_DIM**-0.5
    q_high,q_low=split(qkv_ref[:,:PAIR]*scale)
    q_both=jnp.concatenate([q_high,q_low],axis=1)
    q_twice=jnp.concatenate([q_high,q_high],axis=1)
    do_all=do_ref[...]
    do_high,do_low=split(do_all)
    do_both=jnp.concatenate([do_high,do_low],axis=1)
    do_twice=jnp.concatenate([do_high,do_high],axis=1)
    delta_t=jnp.transpose(do_all*out_ref[...])
    lse_t=jnp.transpose(lse_ref[...])
    dq=[[jnp.zeros((TILE,PAIR),f32) for _ in range(rows//TILE)] for _ in range(2)]
    for start in range(0,rows,TILE):
        stop=start+TILE
        n=rows-start
        k_pos=start+lax.broadcasted_iota(jnp.int32,(TILE,1),0)
        q_pos=start+lax.broadcasted_iota(jnp.int32,(1,n),1)
        first=jnp.where(q_pos<seq_len,0,q_pos)
        allowed=(k_pos>=first)&(k_pos<=q_pos)
        k_all=qkv_ref[start:stop,PAIR:2*PAIR]
        v_all=qkv_ref[start:stop,2*PAIR:]
        k_grads,v_grads=[],[]
        for head in range(2):
            mine=lane//HEAD_DIM==head
            kh,kl=split(jnp.where(mine,k_all,0.0))
            vh,vl=split(jnp.where(mine,v_all,0.0))
            k_both=jnp.concatenate([kh,kl],axis=1)
            v_both=jnp.concatenate([vh,vl],axis=1)
            scores=dot_nt(k_both,q_twice[start:])+dot_nt(kh,q_low[start:])
            lse_row=lse_t[head*HEAD_DIM:head*HEAD_DIM+1,start:]
            probs=jnp.where(allowed,jnp.exp(scores-lse_row),0.0)
            ph,pw=split(probs)
            v_grads.append(fold(dot_nn(ph,do_both[start:]))+dot_nn(pw,do_high[start:]))
            d_probs=dot_nt(v_both,do_twice[start:])+dot_nt(vh,do_low[start:])
            delta_row=jnp.sum(delta_t[head*HEAD_DIM:(head+1)*HEAD_DIM,start:],axis=0,keepdims=True)
            d_scores=probs*(d_probs-delta_row)
            sh,sl=split(d_scores)
            k_grads.append(fold(dot_nn(sh,q_both[start:]))+dot_nn(sl,q_high[start:]))
            part=fold(dot_tn(sh,k_both))+dot_tn(sl,kh)
            for t in range(n//TILE):
                dq[head][start//TILE+t]+=part[t*TILE:(t+1)*TILE]
        grad_ref[start:stop,PAIR:2*PAIR]=jnp.where(lane<HEAD_DIM,k_grads[0],k_grads[1])
        grad_ref[start:stop,2*PAIR:]=jnp.where(lane<HEAD_DIM,v_grads[0],v_grads[1])
        grad_ref[start:stop,:PAIR]=(dq[0][start//TILE]+dq[1][start//TILE])*scale
    sum_ref[...]=jnp.broadcast_to(jnp.sum(grad_ref[...],axis=0,keepdims=True),sum_ref.shape)

def attend(seq_len,qkv,*earlier):
    rows,cols=qkv.shape
    pairs=cols//(3*PAIR)
    block=lambda w: pl.BlockSpec((rows,w),lambda j:(0,j))
    return pl.pallas_call(
        attend_kernel,
        grid=(pairs,),
        in_specs=[pl.BlockSpec(memory_space=pltpu.SMEM),block(3*PAIR)]
        +[pl.BlockSpec(memory_space=pl.ANY)]*len(earlier),
        out_specs=[block(PAIR),block(PAIR)],
        out_shape=[jax.ShapeDtypeStruct((rows,pairs*PAIR),f32)]*2,
        compiler_params=pltpu.CompilerParams(vmem_limit_bytes=30*2**20),
        cost_estimate=pl.CostEstimate(flops=0,bytes_accessed=0,transcendentals=0),
        name="attend",
    )(seq_len,qkv,*earlier)

def attend_back(seq_len,qkv,d_out,out,lse,*earlier):
    rows,cols=qkv.shape
    pairs=cols//(3*PAIR)
    block=lambda w: pl.BlockSpec((rows,w),lambda j:(0,j))
    return pl.pallas_call(
        attend_back_kernel,
        grid=(pairs,),
        in_specs=[pl.BlockSpec(memory_space=pltpu.SMEM),block(3*PAIR),block(PAIR),block(PAIR),block(PAIR)]
        +[pl.BlockSpec(memory_space=pl.ANY)]*len(earlier),
        out_specs=[block(3*PAIR),pl.BlockSpec((8,3*PAIR),lambda j:(0,j))],
        out_shape=[jax.ShapeDtypeStruct((rows,cols),f32),jax.ShapeDtypeStruct((8,cols),f32)],
        compiler_params=pltpu.CompilerParams(vmem_limit_bytes=30*2**20),
        cost_estimate=pl.CostEstimate(flops=0,bytes_accessed=0,transcendentals=0),
        name="attend_back",
    )(seq_len,qkv,d_out,out,lse,*earlier)


COLUMNS = 4
CUT = 3


def table(move):
    pairs = []
    for z in range(COLUMNS):
        for x in range(2):
            for core in range(2):
                for y in range(2):
                    there = move(z, x, core, y)
                    number = lambda p: ((p[0] * 2 + p[1]) * 2 + p[2]) * 2 + p[3]
                    pairs.append((number((z, x, core, y)), number(there)))
    return pairs


over_core = table(lambda z, x, core, y: (z, x, 1 - core, y))
over_x = table(lambda z, x, core, y: (z, 1 - x, core, y))
over_y = table(lambda z, x, core, y: (z, x, core, 1 - y))
over_z = [None] + [
    table(lambda z, x, core, y, k=k: (z ^ k, x, core, y)) for k in range(1, COLUMNS)
]


def swap(values, pairs):
    return lax.ppermute(values, AXES, pairs)


def place():
    dp = lax.axis_index("dp")
    return dp // 4, (dp // 2) % 2, dp % 2, lax.axis_index("seq")


def pick(values, index, axis):
    return lax.dynamic_index_in_dim(values, index, axis, keepdims=False)


def order_kernel(*refs):
    pass


def after(values, *earlier):
    anywhere = pl.BlockSpec(memory_space=pl.ANY)
    return pl.pallas_call(
        order_kernel,
        in_specs=[anywhere] * (1 + len(earlier)),
        out_specs=anywhere,
        out_shape=jax.ShapeDtypeStruct(values.shape, values.dtype),
        input_output_aliases={0: 0},
        cost_estimate=pl.CostEstimate(flops=0, bytes_accessed=0, transcendentals=0),
        name="after",
    )(values, *earlier)


def assemble_kernel(plan, place_ref, *refs):
    count, copies_of = plan
    pieces, outs, sems = refs[:count], refs[count:-1], refs[-1]
    mine = [place_ref[i] for i in range(4)]
    copies = []
    for piece, source, out, shift, axes in copies_of:
        slot = tuple(mine[axis] ^ move for axis, move in zip(axes, shift))
        copies.append(
            pltpu.make_async_copy(
                pieces[piece].at[source], outs[out].at[slot], sems.at[len(copies)]
            )
        )
    for copy in copies:
        copy.start()
    for copy in copies:
        copy.wait()


def assemble(where, pieces, shapes, copies):
    anywhere = pl.BlockSpec(memory_space=pl.ANY)
    whole = pl.BlockSpec(memory_space=pltpu.VMEM)
    size = 4 * sum(functools.reduce(lambda m, n: m * n, shape) for shape in shapes)
    return pl.pallas_call(
        functools.partial(assemble_kernel, (len(pieces), copies)),
        in_specs=[pl.BlockSpec(memory_space=pltpu.SMEM)] + [anywhere] * len(pieces),
        out_specs=[whole] * len(shapes),
        out_shape=[jax.ShapeDtypeStruct(shape, f32) for shape in shapes],
        scratch_shapes=[pltpu.SemaphoreType.DMA((len(copies),))],
        compiler_params=pltpu.CompilerParams(vmem_limit_bytes=size + 4 * 2**20),
        cost_estimate=pl.CostEstimate(flops=0, bytes_accessed=0, transcendentals=0),
        name="assemble",
    )(where, *pieces)


def plane_pieces():
    for k in range(COLUMNS):
        yield 0, k, k, 0, 0
        yield 1, k, k, 1, 0
        yield 2, k, k, 0, 1
        yield 3 + k // CUT, k % CUT, k, 1, 1


def gather_column(shard):
    return jnp.stack([shard] + [swap(shard, over_z[k]) for k in range(1, COLUMNS)])


def gather_sides(own):
    return swap(own, over_x), swap(own, over_y)


def by_core(own, other, core, axis):
    return jnp.where(
        core == 0, jnp.stack([own, other], axis), jnp.stack([other, own], axis)
    )


def local_call(kernel, name, where, arrays, earlier, shapes, scratch=()):
    whole = pl.BlockSpec(memory_space=pltpu.VMEM)
    anywhere = pl.BlockSpec(memory_space=pl.ANY)
    count = len(arrays)

    def call(place_ref, *refs):
        place = [place_ref[i] for i in range(4)]
        kernel(place, *refs[:count], *refs[count + len(earlier) :])

    return pl.pallas_call(
        call,
        in_specs=[pl.BlockSpec(memory_space=pltpu.SMEM)]
        + [whole] * count
        + [anywhere] * len(earlier),
        out_specs=[whole] * len(shapes),
        out_shape=[jax.ShapeDtypeStruct(shape, f32) for shape in shapes],
        scratch_shapes=[pltpu.VMEM(shape, f32) for shape in scratch],
        compiler_params=pltpu.CompilerParams(vmem_limit_bytes=30 * 2**20),
        cost_estimate=pl.CostEstimate(flops=0, bytes_accessed=0, transcendentals=0),
        name=name,
    )(where, *arrays, *earlier)


def lanes_of_up(part):
    return slice(D + part * 2 * D, D + (part + 1) * 2 * D)


def put_block(chip, place, target, at, z, x, y, *added):
    def total(value, lanes):
        for ref, index in added:
            value = value + (ref[index] if lanes is None else ref[index + (slice(None), lanes)])
        return value

    if len(chip) == 1:
        target[at] = total(chip[0][z, x, y], None)
        return
    up, out, arrived = chip
    rows = (slice(None),)
    target[at + rows + (slice(0, D),)] = total(
        out[z, x, place[2], y] + arrived[z, x, y], slice(0, D)
    )
    for c in range(2):
        target[at + rows + (lanes_of_up(c),)] = total(up[z, x, c, y], lanes_of_up(c))


def plane_first(where, chip, block, cut, earlier=()):
    def kernel(place, *refs):
        chip_refs, (to_x, to_y) = refs[:-2], refs[-2:]
        z, x, core, y = place
        for other in range(2):
            for row in range(cut):
                put_block(chip_refs, place, to_x, (row, other), row, 1 - x, other)
            for row in range(cut, COLUMNS):
                put_block(chip_refs, place, to_y, (row - cut, other), row, other, 1 - y)

    shapes = [(cut, 2) + block, (COLUMNS - cut, 2) + block]
    return local_call(kernel, "plane_first", where, chip, earlier, shapes)


def plane_second(where, chip, block, from_x, from_y, cut, earlier=()):
    def kernel(place, *refs):
        chip_refs = refs[:-5]
        from_x, from_y, kept, to_y, to_x = refs[-5:]
        z, x, core, y = place
        for row in range(cut):
            put_block(chip_refs, place, to_y, (row,), row, x, 1 - y, (from_x, (row, 1 - y)))
            put_block(chip_refs, place, kept, (row,), row, x, y, (from_x, (row, y)))
        for row in range(cut, COLUMNS):
            low = row - cut
            put_block(chip_refs, place, to_x, (low,), row, 1 - x, y, (from_y, (low, 1 - x)))
            put_block(chip_refs, place, kept, (row,), row, x, y, (from_y, (low, x)))

    return local_call(
        kernel,
        "plane_second",
        where,
        list(chip) + [from_x, from_y],
        earlier,
        [(COLUMNS,) + block, (cut,) + block, (COLUMNS - cut,) + block],
    )


def column_first(where, block, kept, from_y, from_x, cut, earlier=()):
    def kernel(place, kept, from_y, from_x, *refs):
        z, outs, column = place[0], refs[:-1], refs[-1]
        for row in range(cut):
            column[row] = kept[row] + from_y[row]
        for row in range(cut, COLUMNS):
            column[row] = kept[row] + from_x[row - cut]
        for k in range(COLUMNS):
            outs[k % 2][k // 2] = column[z ^ k]

    return local_call(
        kernel,
        "column_first",
        where,
        [kept, from_y, from_x],
        earlier,
        [(2,) + block] * 2,
        [(COLUMNS,) + block],
    )


def column_second(where, pair, arrived, earlier=()):
    def kernel(place, pair, arrived, own, sent):
        own[...] = pair[0] + arrived[0]
        sent[...] = pair[1] + arrived[1]

    block = pair.shape[1:]
    return local_call(
        kernel, "column_second", where, [pair, arrived], earlier, [block] * 2
    )


def sum_after(where, own, arrived, earlier):
    def kernel(place, own, arrived, out):
        out[...] = own[...] + arrived[...]

    return local_call(kernel, "sum_after", where, [own, arrived], earlier, [own.shape])[0]


def zeros_after(where, cols, *earlier):
    def kernel(place, zero):
        zero[...] = jnp.zeros_like(zero)

    return local_call(kernel, "zeros_after", where, [], earlier, [(1, cols)])[0]


def copy_after(where, values, earlier):
    def kernel(place, values, out):
        out[...] = values[...]

    return local_call(kernel, "copy_after", where, [values], earlier, [values.shape])[0]


def gather_pair(where, shard, earlier=()):
    def kernel(place, shard, beside, out):
        out[0] = shard[...]
        out[1] = beside[...]

    return local_call(
        kernel, "pair", where, [shard, swap(shard, over_z[2])], earlier, [(2,) + shard.shape]
    )[0]


def gather_pairs(where, pair, earlier):
    beside = swap(pair, over_z[1])

    def kernel(place, pair, beside, out):
        for k in range(COLUMNS):
            out[k] = (pair, beside)[k % 2][k // 2]

    shapes = [(COLUMNS,) + pair.shape[1:]]
    return local_call(kernel, "pairs", where, [pair, beside], earlier, shapes)[0]


def normalise(values):
    centred = values - jnp.mean(values, axis=1, keepdims=True)
    inv_std = lax.rsqrt(jnp.mean(centred * centred, axis=1, keepdims=True) + eps_norm)
    return centred * inv_std, inv_std


def body_grid(
    layer_input,
    cotangent,
    seq_lengths,
    qkv_weight,
    qv_bias,
    out_weight,
    out_bias,
    first_gain,
    first_shift,
    up_weight,
    up_bias,
    down_weight,
    down_bias,
    second_gain,
    second_shift,
):
    z, x, core, y = place()
    where = jnp.stack([z, x, core, y]).astype(jnp.int32)
    rows = layer_input.shape[0]
    shard = qkv_weight.shape[0]
    half = D // 2
    pairs = half // PAIR
    wide = 3 * half
    hidden = 2 * D

    def both_rows(own, other):
        return jnp.where(
            y == 0, jnp.concatenate([own, other]), jnp.concatenate([other, own])
        )

    def rows_of(values, part):
        return lax.dynamic_slice_in_dim(values, part * rows, rows, 0)

    normed_own, inv_one = normalise(layer_input)
    other_normed = swap(normed_own, over_y)
    other_cotangent = swap(cotangent, over_core)

    by_head = qkv_weight.reshape(shard, 3, 2, pairs, PAIR).transpose(2, 0, 3, 1, 4)
    by_head = by_head.reshape(2, shard, wide)
    line_one = jnp.concatenate([qv_bias, out_bias, first_gain, first_shift])
    line_two = jnp.concatenate([up_bias, down_bias])
    line_three = jnp.concatenate([second_gain, second_shift])
    lines = jnp.stack(
        [jnp.pad(line, (0, PAIR - line.shape[0])) for line in (line_one, line_two, line_three)]
    )
    small = jnp.pad(lines, ((0, shard - 3), (0, 0)))
    sent = swap(jnp.concatenate([pick(by_head, 1 - y, 0), small], axis=1), over_y)
    kept = jnp.concatenate([pick(by_head, y, 0), small], axis=1)
    block = jnp.where(y == 0, jnp.stack([kept, sent]), jnp.stack([sent, kept]))
    column = gather_column(after(block, normed_own))
    beside = swap(column, over_x)

    by_unit = up_weight.reshape(shard, 2 * COLUMNS, 2, 8 * shard).transpose(2, 0, 1, 3)
    by_unit = by_unit.reshape(2, shard, hidden)
    kept_up = pick(by_unit, core, 0)
    arrived_up = swap(pick(by_unit, 1 - core, 0), over_core)
    both_up = by_core(kept_up, arrived_up, core, 1).reshape(shard, 2 * hidden)
    shard_a = after(jnp.concatenate([out_weight, both_up], axis=1), column)
    pair_a = gather_pair(where, shard_a)
    shard_b = after(down_weight, pair_a)
    own_a = gather_pairs(where, pair_a, [beside])
    sides_a = gather_sides(own_a)

    pieces = [column, beside]
    pieces += [swap(column, over_core), swap(copy_after(where, beside, [other_normed, own_a]), over_core)]
    copies = []
    for k in range(COLUMNS):
        for piece in range(4):
            shift = (k, piece % 2, piece // 2)
            copies.append((piece, (k, slice(None), slice(None), slice(0, wide)), 0, shift, (0, 1, 2)))
            copies.append(
                (piece, (k, slice(None), slice(0, 8), slice(wide, wide + PAIR)), 1, shift, (0, 1, 2))
            )
    grid = (COLUMNS, 2, 2, 2)
    w_qkv, lines = assemble(
        where, pieces, [grid + (shard, wide), grid + (8, PAIR)], copies
    )
    pair_b = gather_pair(where, shard_b, [w_qkv])
    w_qkv = w_qkv.reshape(D, wide)
    lines = lines.reshape(32, 8, PAIR)
    b_qv = lines[:, 0, : 2 * shard].reshape(2 * D)
    b_out = lines[:, 0, 2 * shard : 3 * shard].reshape(D)
    gain_one = lines[:, 0, 3 * shard : 4 * shard].reshape(D)
    shift_one = lines[:, 0, 4 * shard : 5 * shard].reshape(D)
    b_up = lines[:, 1, : 4 * shard].reshape(2 * COLUMNS, 2, 2, 4 * shard)
    b_up = pick(b_up, core, 1).reshape(hidden)
    b_down = lines[:, 1, 4 * shard : 5 * shard].reshape(D)
    gain_two = lines[:, 2, :shard].reshape(D)
    shift_two = lines[:, 2, shard : 2 * shard].reshape(D)

    normed_one = both_rows(normed_own, other_normed)
    normed_out_one = normed_one * gain_one + shift_one
    bias = pick(b_qv.reshape(2, 2, pairs, PAIR), y, 1)
    qkv_bias = jnp.stack([bias[0], jnp.zeros_like(bias[0]), bias[1]], axis=1).reshape(wide)
    projected = matmul(normed_out_one, w_qkv) + qkv_bias
    own_b = gather_pairs(where, pair_b, [projected])
    sides_b = gather_sides(own_b)
    head_out, log_sum = attend(seq_lengths, projected, own_b)
    there = swap(rows_of(head_out, 1 - y), over_y)
    here = rows_of(head_out, y)
    attended = jnp.where(
        y == 0, jnp.concatenate([here, there], 1), jnp.concatenate([there, here], 1)
    )


    def corner_first(place, beside_y, out):
        out[...] = beside_y[:CUT]

    def corner_rest(place, x_of_a, x_of_b, y_of_b, y_corner_a, x_corner_b, y_corner_b):
        y_corner_a[...] = x_of_a[CUT:]
        x_corner_b[...] = y_of_b[:CUT]
        y_corner_b[...] = x_of_b[CUT:]

    grid = (COLUMNS, 2, 2, 2)
    scales = jnp.stack([gain_one, shift_one], axis=1).reshape(grid + (shard, 2))
    low, high = (CUT,), (COLUMNS - CUT,)
    block_a, block_b = own_a.shape[1:], own_b.shape[1:]
    x_corner_a, = local_call(
        corner_first, "corner_first", where, [sides_a[1]], [head_out], [low + block_a]
    )
    y_corner_a, x_corner_b, y_corner_b = local_call(
        corner_rest, "corner_rest", where, [sides_a[0], *sides_b], [there, scales],
        [high + block_a, low + block_b, high + block_b],
    )
    corners_a = swap(x_corner_a, over_x), swap(y_corner_a, over_y)
    corners_b = swap(x_corner_b, over_x), swap(y_corner_b, over_y)
    every = slice(None)
    copies = []
    for piece, at, dz, dx, dy in plane_pieces():
        copies.append((piece, (at, every, slice(0, D)), 0, (dz, dx, dy), (0, 1, 3)))
    w_out_half, = assemble(
        where, [own_a, *sides_a, *corners_a], [(COLUMNS, 2, 2, shard, D)], copies
    )
    copies = []
    for piece, at, dz, dx, dy in plane_pieces():
        for c in range(2):
            cols = slice(D + c * hidden, D + (c + 1) * hidden)
            copies.append((piece, (at, every, cols), c, (dz, dx, dy), (0, 1, 3)))
    w_up_parts = assemble(
        where, [own_a, *sides_a, *corners_a], [(COLUMNS, 2, 2, shard, hidden)] * 2, copies
    )
    copies = []
    for piece, at, dz, dx, dy in plane_pieces():
        copies.append((piece, (at,), 0, (dz, dx, dy), (0, 1, 3)))
    w_down, = assemble(
        where, [own_b, *sides_b, *corners_b], [(COLUMNS, 2, 2, 4 * shard, D)], copies
    )
    w_out = by_core(w_out_half, swap(w_out_half, over_core), core, 2).reshape(D, D)
    w_up = jnp.stack(w_up_parts, axis=2).reshape(D, hidden)
    w_down = w_down.reshape(hidden, D)

    middle = layer_input + matmul(attended, w_out) + b_out
    normed_out_two, normed_two, inv_two = norm_forward(middle, gain_two, shift_two)
    both_normed = jnp.concatenate([normed_out_two, swap(normed_out_two, over_core)])
    both_cotangent = jnp.concatenate([cotangent, other_cotangent])
    raw_act = matmul(both_normed, w_up)
    pre_act = raw_act + b_up
    activ = gelu_forward(pre_act)

    d_down_b = jnp.sum(cotangent, axis=0)
    d_down_w = matmul_tn(activ, both_cotangent)
    chip_b = d_down_w.reshape(COLUMNS, 2, 2, 4 * shard, D)
    d_pre = matmul_nt(both_cotangent, w_down) * gelu_slope(pre_act)
    d_up_b = jnp.sum(d_pre, axis=0)
    d_part = matmul_nt(d_pre, w_up)
    d_norm_two, d_gain_two, d_shift_two = norm_backward(
        d_part[:rows] + swap(d_part[rows:], over_core), normed_two, inv_two, gain_two
    )
    d_middle = cotangent + d_norm_two
    d_out_b = jnp.sum(d_middle, axis=0)
    d_att = matmul_nt(d_middle, w_out)
    d_heads = d_att.reshape(rows, 2, half)
    sent = pick(d_heads, 1 - y, 1)
    d_up_b = d_up_b.reshape(2 * COLUMNS, 8 * shard)
    d_up_b = by_core(d_up_b, jnp.zeros_like(d_up_b), core, 1)

    def lanes(*vectors):
        line = jnp.concatenate([v.reshape(32, -1) for v in vectors], axis=1)
        return jnp.pad(line, ((0, 0), (0, PAIR - line.shape[1])))

    small = jnp.stack(
        [lanes(d_out_b, d_gain_two, d_shift_two), lanes(d_up_b, d_down_b)],
        axis=1,
    )
    small = jnp.pad(small, ((0, 0), (0, 6), (0, 0)))
    chip_a = matmul_tn(both_normed + zeros_after(where, D, sent, small), d_pre).reshape(COLUMNS, 2, 2, 2, shard, hidden)
    def join_rows(place, own, arrived, out):
        y = place[3]
        out[pl.ds(y * rows, rows)] = own[...]
        out[pl.ds((1 - y) * rows, rows)] = arrived[...]

    d_out, = local_call(
        join_rows, "join_rows", where, [pick(d_heads, y, 1), swap(sent, over_y)],
        [chip_a], [(2 * rows, half)],
    )
    block_b = (4 * shard, D)
    block_a = (shard, 5 * D)
    to_x, to_y = plane_first(where, [chip_b], block_b, 2)
    side_b = swap(to_x, over_x), swap(to_y, over_y)
    d_out_w = matmul_tn(attended, d_middle).reshape(COLUMNS, 2, 2, 2, shard, D)
    chip_a = [chip_a, d_out_w, swap(pick(d_out_w, 1 - core, 2), over_core)]
    kept_b, *sent_b = plane_second(where, [chip_b], block_b, *side_b, 2, [d_out])
    first_a = plane_first(where, chip_a, block_a, 2, sent_b)
    side_a = swap(first_a[0], over_x), swap(first_a[1], over_y)

    d_proj, d_bias_all = attend_back(
        seq_lengths, projected, d_out, head_out, log_sum, *first_a, *sent_b
    )
    corner = swap(sent_b[0], over_y), swap(sent_b[1], over_x)
    pair_b, sent_b = column_first(where, block_b, kept_b, *corner, 2, [d_proj])
    kept_a, *sent_a = plane_second(where, chip_a, block_a, *side_a, 2, [sent_b])
    corner_a = swap(sent_a[0], over_y), swap(sent_a[1], over_x)

    moved = matmul_tn(normed_one + zeros_after(where, D, *sent_a), d_proj)
    own_b, sent_b = column_second(where, pair_b, swap(sent_b, over_z[1]), [moved])
    pair_a, sent_a = column_first(where, block_a, kept_a, *corner_a, 2, [sent_b])
    last_lane = wide + PAIR - 1

    def finish(place, moved, weight, scales, total, small, kept, sent):
        core = place[2]
        y = place[3]
        total = total[:1]
        for z in range(COLUMNS):
            for xy in range(4):
                for target, c in ((kept, core), (sent, 1 - core)):
                    at = (z, xy // 2, c, xy % 2)
                    to = (z, xy // 2, xy % 2)
                    rows_of_grad, rows_of_weight = moved[at], weight[at]
                    scale = scales[at]
                    target[to + (slice(None), slice(0, wide))] = (
                        rows_of_grad * scale[:, 0:1] + scale[:, 1:2] * total
                    )
                    gain_grad = jnp.sum(rows_of_grad * rows_of_weight, axis=1, keepdims=True)
                    shift_grad = jnp.sum(total * rows_of_weight, axis=1, keepdims=True)
                    lane = lax.broadcasted_iota(jnp.int32, (shard, PAIR), 1)
                    side = jnp.where(lane == PAIR - 1, gain_grad, 0.0)
                    side = jnp.where(lane == PAIR - 2, shift_grad, side)
                    lines = jnp.concatenate(
                        [small[at], jnp.zeros((shard - 8, PAIR), f32)], axis=0
                    )
                    target[to + (slice(None), slice(wide, wide + PAIR))] = side + lines

        line = slice(wide, wide + 2 * shard)
        for part, z in ((0, y), (2, 2 + y)):
            column = jnp.concatenate(
                [total[:, (3 * p + part) * PAIR : (3 * p + part + 1) * PAIR] for p in range(pairs)],
                axis=1,
            )
            for xy in range(4):
                x, side = xy // 2, xy % 2
                low = column[:, 2 * shard * (4 * x + side) :][:, : 2 * shard]
                high = column[:, 2 * shard * (4 * x + 2 + side) :][:, : 2 * shard]
                kept[z, x, side, 2:3, line] = jnp.where(core == 0, low, high)
                sent[z, x, side, 2:3, line] = jnp.where(core == 0, high, low)

    block = (shard, wide + PAIR)
    kept, first = local_call(
        finish,
        "finish",
        where,
        [
            moved.reshape(grid + (shard, wide)),
            w_qkv.reshape(grid + (shard, wide)),
            scales,
            d_bias_all,
            small.reshape(grid + (8, PAIR)),
        ],
        [sent_a],
        [(COLUMNS, 2, 2) + block] * 2,
    )

    def chip_sum(place, kept, arrived, mine, sent):
        x = place[1]
        for z in range(COLUMNS):
            mine[z] = kept[z, x] + arrived[z, x]
            sent[z] = kept[z, 1 - x] + arrived[z, 1 - x]

    kept, second = local_call(
        chip_sum,
        "chip_sum",
        where,
        [kept, swap(first, over_core)],
        (),
        [(COLUMNS, 2) + block] * 2,
    )
    d_norm = matmul_nt(d_proj + zeros_after(where, wide, second), w_qkv)
    d_norm_sent = rows_of(d_norm, 1 - y)

    def line_sum(place, kept, arrived, pair, sent):
        z = place[0]
        for k in range(COLUMNS):
            (pair, sent)[k % 2][k // 2] = kept[z ^ k] + arrived[z ^ k]

    pair_qkv, sent_qkv = local_call(
        line_sum, "line_sum", where, [kept, swap(second, over_x)], [d_norm],
        [(2, 2) + block] * 2,
    )
    own_a, sent_a = column_second(where, pair_a, swap(sent_a, over_z[1]), [sent_qkv])
    down_part = matmul(
        gelu_forward(raw_act + (b_up + zeros_after(where, hidden, sent_a))), w_down
    )
    layer_output = middle + down_part[:rows] + swap(down_part[rows:], over_core) + b_down
    own_qkv, sent_qkv = column_second(
        where, pair_qkv, swap(sent_qkv, over_z[1]), [down_part]
    )
    down_grad = sum_after(where, own_b, swap(sent_b, over_z[2]), [sent_qkv])
    grad_a = sum_after(where, own_a, swap(sent_a, over_z[2]), [sent_qkv])

    def last_sum(place, own, arrived, here, sent):
        y = place[3]
        here[...] = own[y] + arrived[y]
        sent[...] = own[1 - y] + arrived[1 - y]

    here, third = local_call(
        last_sum, "last_sum", where, [own_qkv, swap(sent_qkv, over_z[2])], (), [block] * 2
    )
    there = swap(third, over_y)
    out_grad = grad_a[:, :D]
    up_parts = jnp.stack([grad_a[:, lanes_of_up(0)], grad_a[:, lanes_of_up(1)]])
    arrived = swap(pick(up_parts, 1 - core, 0), over_core)
    up_grad = by_core(
        pick(up_parts, core, 0).reshape(shard, 2 * COLUMNS, 8 * shard),
        arrived.reshape(shard, 2 * COLUMNS, 8 * shard),
        core,
        2,
    ).reshape(shard, 4 * D)


    def place_qkv(place, here, there, grad, side):
        y = place[3]
        side[...] = here[:, wide:] + there[:, wide:]
        for part in range(3):
            for p in range(pairs):
                source = slice((3 * p + part) * PAIR, (3 * p + part + 1) * PAIR)
                mine, other = here[:, source], there[:, source]
                target = part * D + p * PAIR
                grad[:, target : target + PAIR] = jnp.where(y == 0, mine, other)
                target = target + half
                grad[:, target : target + PAIR] = jnp.where(y == 0, other, mine)

    qkv_grad, side = local_call(
        place_qkv, "place_qkv", where, [here, there], [up_grad, down_grad, layer_output], [(shard, 3 * D), (shard, PAIR)]
    )
    d_norm_own = rows_of(d_norm, y) + swap(d_norm_sent, over_y)
    d_norm_one, unused, unused = norm_backward(
        d_norm_own, normed_own, inv_one, gain_one
    )
    input_grad = d_middle + d_norm_one
    return (
        layer_output,
        input_grad,
        qkv_grad,
        side[2, : 2 * shard],
        out_grad,
        side[0, :shard],
        side[:, PAIR - 1],
        side[:, PAIR - 2],
        up_grad,
        side[1, : 4 * shard],
        down_grad,
        side[1, 4 * shard : 5 * shard],
        side[0, shard : 2 * shard],
        side[0, 2 * shard : 3 * shard],
    )


def solution(mesh):
    shape = (mesh.shape["dp"], mesh.shape["seq"])
    body = body_grid if shape == (COLUMNS * 4, 2) else body_general
    row = P(AXES, None)
    vec = P(AXES)
    return jax.shard_map(
        body,
        mesh=mesh,
        in_specs=(row, row, P("dp"), row, vec, row, vec, vec, vec, row, vec, row, vec, vec, vec),
        out_specs=(row, row, row, vec, row, vec, vec, vec, row, vec, row, vec, vec, vec),
        check_vma=False,
    )
```
